32 devices in a mesh: seq: 8 (over y, x, core), head: 4 (over z).
Axes of the slice: x: 2, y: 2, z: 4, core: 2. Of those that a mesh axis runs over, the one named last changes fastest.
Arguments:
- prompt_k: bfloat16 [1280, 1024], P(('seq', 'head')), may hold values from -6 to 6
- prompt_v: bfloat16 [1280, 1024], P(('seq', 'head')), may hold values from -6 to 6
- resp_q: bfloat16 [2048, 8192], P('seq', 'head'), may hold values from -7 to 7
- resp_k: bfloat16 [2048, 1024], P('seq', 'head'), may hold values from -6 to 6
- resp_v: bfloat16 [2048, 1024], P('seq', 'head'), may hold values from -6 to 6
- grad_out: bfloat16 [2048, 8192], P('seq', 'head'), may hold values from -6 to 6
- resp_lengths: int32 [8], replicated, may hold values from 1 to 1024, 2048 in all
Outputs:
- resp_out: bfloat16 [2048, 8192], P('seq', 'head')
- grad_q: bfloat16 [2048, 8192], P('seq', 'head')
- grad_k_resp: bfloat16 [2048, 1024], P('seq', 'head')
- grad_v_resp: bfloat16 [2048, 1024], P('seq', 'head')
- grad_k_prompt: bfloat16 [1280, 1024], P(('seq', 'head'))
- grad_v_prompt: bfloat16 [1280, 1024], P(('seq', 'head'))
The draws below stay inside these ranges and needn't reach their ends.
Inputs may be any that keep to these rules, and one draw needn't show every extreme that they name: `resp_lengths`: the 8 lengths add up to 2048, and the largest is exactly 1024.
All inputs are finite; a program needn't handle non-finite values.
Results may differ from the reference program's by a relative error of at most 0.02.
Values may be sent and summed in bfloat16 or wider, within the bound.
No kernel may reach another device: no remote copies, remote signals or barrier semaphores. Data moves between devices by JAX's collectives and lax.ppermute only.
A program may use at most 128 MiB of HBM per device.

```python
import math
import jax
import jax.numpy as jnp
import numpy as np
from jax import lax

H = 64
KVH = 8
HD = 128
NRESP = 8
P_SIZE = 1280
R = 2048
LMAX = 1024


def draw_resp_q(key, part):
    key = jax.random.fold_in(key, 1)
    values = jax.random.truncated_normal(key, -6.0, 6.0, (R, H, HD), jnp.float32)
    return values.reshape(R, H * HD).astype(jnp.bfloat16)


def draw_prompt_k(key, part):
    key = jax.random.fold_in(key, 2)
    values = jax.random.truncated_normal(key, -6.0, 6.0, (P_SIZE, KVH, HD), jnp.float32)
    return values.reshape(P_SIZE, KVH * HD).astype(jnp.bfloat16)


def block_scale(stream_key, extent, split, smallest, high):
    level = 1.0
    for axis_at, blocks in split:
        heights = jax.random.uniform(jax.random.fold_in(jax.random.fold_in(stream_key, 6), axis_at), (blocks,), jnp.float32, smallest / len(split), high / len(split))
        level = level * jnp.repeat(jnp.exp(heights), extent[axis_at] // blocks).reshape((-1,) + (1,) * (len(extent) - 1 - axis_at))
    return level


def length_profile(amount, total, reach, lean):
    weights = [(1 << 20) // math.isqrt(grade ** lean) + 1 for grade in range(2, amount + 1)]
    rest, given = total - reach - (amount - 1), [1] * (amount - 1)
    while rest > 0:
        movable = [i for i in range(amount - 1) if given[i] < reach]
        pool, left = sum([weights[i] for i in movable]), rest
        for i in movable:
            extra = min(reach - given[i], max(1, left * weights[i] // pool), rest)
            given[i] = given[i] + extra
            rest = rest - extra
    return np.array([reach] + given)


def uneven(rng, count, total, limit, lean):
    if count == 2:
        one = jax.random.randint(rng, (), max(1, total - limit), min(limit, total - 1) + 1)
        return jnp.stack([one, total - one])
    lengths = jnp.asarray(length_profile(count, total, limit, lean), jnp.int32)
    couples = (count - 1) // 2
    giver, sink = lengths[1:1 + 2 * couples:2], lengths[2:2 + 2 * couples:2]
    room = jnp.minimum(giver - 1, limit - sink)
    shifted = jax.random.randint(jax.random.fold_in(rng, 1), (couples,), 0, 1 << 20) % (room + 1)
    lengths = lengths.at[1:1 + 2 * couples:2].set(giver - shifted).at[2:2 + 2 * couples:2].set(sink + shifted)
    return lengths[jax.random.permutation(jax.random.fold_in(rng, 2), count)]


def normal_values(stream_key, dims, spread, limit, shards=(), kind=jnp.bfloat16):
    drawn = jax.random.normal(stream_key, dims, jnp.float32) * spread
    if len(shards) > 0:
        drawn = block_scale(stream_key, dims, shards, -0.22, 0.18) * drawn
    return jnp.clip(drawn, min=-limit, max=limit).astype(kind)


def setup_inputs(seed: int = 0) -> dict:
    seeds = jax.random.split(jax.random.key(seed), 8)
    prompt_k = draw_prompt_k(jax.random.fold_in(seeds[7], 71), 0)
    prompt_v = normal_values(seeds[1], (P_SIZE, KVH * HD), 1.0, 6.0, ((0, 32),))
    resp_q = draw_resp_q(jax.random.fold_in(seeds[7], 71), 0)
    resp_k = normal_values(seeds[3], (R, KVH * HD), 1.0, 6.0, ((0, 8), (1, 4)))
    resp_v = normal_values(seeds[4], (R, KVH * HD), 1.0, 6.0, ((0, 8), (1, 4)))
    grad_out = normal_values(seeds[5], (R, H * HD), 1.0, 6.0, ((0, 8), (1, 4)))
    resp_lengths = uneven(seeds[6], NRESP, R, LMAX, 2).astype(jnp.int32)
    return dict(prompt_k=prompt_k, prompt_v=prompt_v, resp_q=resp_q, resp_k=resp_k, resp_v=resp_v, grad_out=grad_out, resp_lengths=resp_lengths)


def segment_of(positions, seg_ends):
    return lax.optimization_barrier(jnp.sum((positions[:, None] >= seg_ends[None, :]).astype(jnp.int32), axis=1))

def head_group(prompt_keys, prompt_values, queries, key_rows, value_rows, cotangent, seg_ends):
    score_scale = 1.0 / math.sqrt(HD)
    q_block = min(512, R)
    window = LMAX + q_block
    padding = jnp.zeros((LMAX, HD), key_rows.dtype)
    padded_keys = jnp.concatenate([padding, key_rows], 0)
    padded_values = jnp.concatenate([padding, value_rows], 0)

    def advance(running, block_index):
        grad_kp, grad_vp, grad_kr, grad_vr = running
        row_start = (block_index * q_block).astype(jnp.int32)
        query_part = lax.dynamic_slice_in_dim(queries, row_start, q_block, 0).astype(jnp.float32)
        cot_part = lax.dynamic_slice_in_dim(cotangent, row_start, q_block, 0).astype(jnp.float32)
        near_keys = lax.dynamic_slice_in_dim(padded_keys, row_start, window, 0)
        near_values = lax.dynamic_slice_in_dim(padded_values, row_start, window, 0)
        row_pos = row_start + jnp.arange(q_block, dtype=jnp.int32)
        key_pos = row_start - LMAX + jnp.arange(window, dtype=jnp.int32)
        allowed = (key_pos[None, :] >= 0) & (key_pos[None, :] <= row_pos[:, None]) & (segment_of(key_pos, seg_ends)[None, :] == segment_of(row_pos, seg_ends)[:, None])
        allowed = jnp.concatenate([jnp.ones((q_block, P_SIZE), dtype=bool), allowed], 1)
        all_keys = jnp.concatenate([prompt_keys, near_keys], 0).astype(jnp.float32)
        all_values = jnp.concatenate([prompt_values, near_values], 0).astype(jnp.float32)
        scores = jnp.einsum('qgd,kd->qgk', query_part, all_keys) * score_scale
        scores = jnp.where(allowed[:, None, :], scores, -jnp.inf)
        row_max = lax.optimization_barrier(jnp.max(scores, axis=-1, keepdims=True))
        log_total = row_max + jnp.log(lax.optimization_barrier(jnp.sum(jnp.exp(scores - row_max), axis=-1, keepdims=True)))
        weights = jnp.exp(scores - log_total)
        rounded = lax.optimization_barrier(weights.astype(jnp.bfloat16)).astype(jnp.float32)
        output = jnp.einsum('qgk,kd->qgd', rounded, all_values).astype(jnp.bfloat16)
        out_wide = lax.optimization_barrier(output).astype(jnp.float32)
        row_delta = lax.optimization_barrier(jnp.sum(cot_part * out_wide, axis=-1, keepdims=True))
        grad_prob = jnp.einsum('qgd,kd->qgk', cot_part, all_values)
        dscore = lax.optimization_barrier((weights * (grad_prob - row_delta) * score_scale).astype(jnp.bfloat16)).astype(jnp.float32)
        grad_query = jnp.einsum('qgk,kd->qgd', dscore, all_keys).astype(jnp.bfloat16)
        grad_key = jnp.einsum('qgk,qgd->kd', dscore, query_part)
        grad_value = jnp.einsum('qgk,qgd->kd', rounded, cot_part)
        grad_kp = grad_kp + grad_key[:P_SIZE]
        grad_vp = grad_vp + grad_value[:P_SIZE]
        grad_kr = lax.dynamic_update_slice_in_dim(grad_kr, lax.dynamic_slice_in_dim(grad_kr, row_start, window, 0) + grad_key[P_SIZE:], row_start, 0)
        grad_vr = lax.dynamic_update_slice_in_dim(grad_vr, lax.dynamic_slice_in_dim(grad_vr, row_start, window, 0) + grad_value[P_SIZE:], row_start, 0)
        return ((grad_kp, grad_vp, grad_kr, grad_vr), (output, grad_query))
    initial = (jnp.zeros((P_SIZE, HD), jnp.float32), jnp.zeros((P_SIZE, HD), jnp.float32), jnp.zeros((R + LMAX, HD), jnp.float32), jnp.zeros((R + LMAX, HD), jnp.float32))
    finals, stacked = lax.scan(advance, initial, jnp.arange(R // q_block, dtype=jnp.int32))
    grad_kp, grad_vp, grad_kr, grad_vr = finals
    group_size = queries.shape[1]
    output = stacked[0].reshape(R, group_size, HD)
    grad_query = stacked[1].reshape(R, group_size, HD)
    return (output, grad_query, grad_kr[LMAX:].astype(jnp.bfloat16), grad_vr[LMAX:].astype(jnp.bfloat16), grad_kp.astype(jnp.bfloat16), grad_vp.astype(jnp.bfloat16))

def reference(prompt_k, prompt_v, resp_q, resp_k, resp_v, grad_out, resp_lengths):
    group_size = H // KVH
    seg_ends = jnp.cumsum(resp_lengths).astype(jnp.int32)
    prompt_keys = prompt_k.reshape(P_SIZE, KVH, HD).transpose(1, 0, 2)
    prompt_values = prompt_v.reshape(P_SIZE, KVH, HD).transpose(1, 0, 2)
    queries = resp_q.reshape(R, KVH, group_size, HD).transpose(1, 0, 2, 3)
    cotangent = grad_out.reshape(R, KVH, group_size, HD).transpose(1, 0, 2, 3)
    key_rows = resp_k.reshape(R, KVH, HD).transpose(1, 0, 2)
    value_rows = resp_v.reshape(R, KVH, HD).transpose(1, 0, 2)

    def per_head(head_items):
        return head_group(head_items[0], head_items[1], head_items[2], head_items[3], head_items[4], head_items[5], seg_ends)
    output, grad_query, grad_kr, grad_vr, grad_kp, grad_vp = lax.map(per_head, (prompt_keys, prompt_values, queries, key_rows, value_rows, cotangent))
    resp_out = output.transpose(1, 0, 2, 3).reshape(R, H * HD)
    grad_q = grad_query.transpose(1, 0, 2, 3).reshape(R, H * HD)
    grad_k_resp = grad_kr.transpose(1, 0, 2).reshape(R, KVH * HD)
    grad_v_resp = grad_vr.transpose(1, 0, 2).reshape(R, KVH * HD)
    grad_k_prompt = grad_kp.transpose(1, 0, 2).reshape(P_SIZE, KVH * HD)
    grad_v_prompt = grad_vp.transpose(1, 0, 2).reshape(P_SIZE, KVH * HD)
    return (resp_out, grad_q, grad_k_resp, grad_v_resp, grad_k_prompt, grad_v_prompt)
```

```python
import functools
import math

import jax
import jax.numpy as jnp
from jax import lax
from jax.experimental import pallas as pl
from jax.experimental.pallas import tpu as pltpu
from jax.sharding import PartitionSpec as P

HD = 128
SPAN = 4
NEG = -1e30
NT = (((1,), (1,)), ((), ()))


def dot(a, b):
    return jnp.dot(a, b, preferred_element_type=jnp.float32)


def dot_nt(a, b):
    return lax.dot_general(a, b, NT, preferred_element_type=jnp.float32)


def attention_kernel(
    prompt_chunks, chunk, meta, q_ref, do_ref, prompt_ref, *refs
):
    resp_refs = refs[: SPAN + 1]
    o_ref, dq_ref, dprompt_ref = refs[SPAN + 1 : SPAN + 4]
    dresp_refs = refs[SPAN + 4 : 2 * SPAN + 5]
    bias, s_buf, p_buf, dk_t, dv_t = refs[2 * SPAN + 5 :]
    rows = q_ref.shape[0]
    step = pl.program_id(1)
    last = pl.num_programs(1) - 1
    score_scale = 1.0 / math.sqrt(HD)
    exp_scale = score_scale * math.log2(math.e)
    count = prompt_chunks + SPAN + 1

    def keys_of(c):
        if c < prompt_chunks:
            return prompt_ref[c * chunk : (c + 1) * chunk, :HD]
        return resp_refs[c - prompt_chunks][:, :HD]

    def values_of(c):
        if c < prompt_chunks:
            return prompt_ref[c * chunk : (c + 1) * chunk, HD:]
        return resp_refs[c - prompt_chunks][:, HD:]

    @pl.when((step == 0) & (pl.program_id(0) == 0))
    def _():
        first_row = meta[0]
        row_pos = first_row + lax.broadcasted_iota(jnp.int32, (rows, rows), 0)
        seg_start = jnp.zeros((rows, rows), jnp.int32)
        end = jnp.int32(0)
        for i in range(1, meta.shape[0]):
            end = end + meta[i]
            seg_start = jnp.where(row_pos >= end, end, seg_start)
        for distance in range(SPAN + 1):
            key_pos = (first_row - distance * rows) + lax.broadcasted_iota(
                jnp.int32, (rows, rows), 1
            )
            allowed = (key_pos >= seg_start) & (key_pos <= row_pos)
            bias[distance] = jnp.where(allowed, 0.0, NEG)

    @pl.when(step == 0)
    def _():
        dk_t[...] = jnp.zeros_like(dk_t)
        dv_t[...] = jnp.zeros_like(dv_t)

    q = q_ref[...]
    top = None
    for c in range(count):
        s = dot_nt(q, keys_of(c))
        if c >= prompt_chunks:
            s = s + bias[c - prompt_chunks]
        s_buf[c, :, : s.shape[1]] = s
        for at in range(0, s.shape[1], HD):
            part = s[:, at : at + HD]
            top = part if top is None else jnp.maximum(top, part)
    top = jnp.max(top, axis=1, keepdims=True) * exp_scale

    def width_of(c):
        return chunk if c < prompt_chunks else rows

    total = jnp.zeros((rows, HD), jnp.float32)
    out = jnp.zeros((rows, HD), jnp.float32)
    for c in range(count):
        w = width_of(c)
        p = jnp.exp2(s_buf[c, :, :w] * exp_scale - top)
        for at in range(0, w, HD):
            total = total + p[:, at : at + HD]
        p = p.astype(jnp.bfloat16)
        p_buf[c, :, :w] = p
        out = out + dot(p, values_of(c))
    inverse = 1.0 / jnp.sum(total, axis=1, keepdims=True)
    out = (out * inverse).astype(jnp.bfloat16)
    o_ref[...] = out
    cot = (do_ref[...].astype(jnp.float32) * inverse).astype(jnp.bfloat16)
    delta = jnp.sum(
        cot.astype(jnp.float32) * out.astype(jnp.float32), axis=1, keepdims=True
    )
    cot_t = cot.T
    q_t = q.T
    dq = jnp.zeros((rows, HD), jnp.float32)
    for c in range(count):
        w = width_of(c)
        p = p_buf[c, :, :w]
        dp = dot_nt(cot, values_of(c))
        ds = (p.astype(jnp.float32) * (dp - delta)).astype(jnp.bfloat16)
        dq = dq + dot(ds, keys_of(c))
        dv_t[c, :, :w] += dot(cot_t, p)
        dk_t[c, :, :w] += dot(q_t, ds)
    dq_ref[...] = (dq * score_scale).astype(jnp.bfloat16)

    @pl.when(step == last)
    def _():
        for c in range(count):
            w = width_of(c)
            grad_k = (dk_t[c, :, :w] * score_scale).T
            grad_v = dv_t[c, :, :w].T
            if c < prompt_chunks:
                target = dprompt_ref.at[c * chunk : (c + 1) * chunk]
            else:
                target = dresp_refs[c - prompt_chunks]
            target[:, :HD] = grad_k.astype(target.dtype)
            target[:, HD:] = grad_v.astype(target.dtype)


def attention(meta, resp_q, grad_out, prompt_kv, resp_kvs):
    rows = resp_q.shape[0]
    prompt_len = prompt_kv.shape[0]
    kv_heads = prompt_kv.shape[1] // (2 * HD)
    group = resp_q.shape[1] // HD // kv_heads
    chunk = 256
    prompt_chunks = prompt_len // chunk
    count = prompt_chunks + SPAN + 1
    wide = max(chunk, rows)
    head_spec = pl.BlockSpec((rows, HD), lambda n, g: (0, n * group + g))
    prompt_spec = pl.BlockSpec((prompt_len, 2 * HD), lambda n, g: (0, n))
    resp_spec = pl.BlockSpec((rows, 2 * HD), lambda n, g: (0, n))
    resp_shape = (rows, kv_heads * 2 * HD)
    pairs = rows * kv_heads * group * (prompt_len + (SPAN + 1) * rows)
    return pl.pallas_call(
        functools.partial(attention_kernel, prompt_chunks, chunk),
        grid=(kv_heads, group),
        in_specs=[pl.BlockSpec(memory_space=pltpu.SMEM), head_spec, head_spec, prompt_spec]
        + [resp_spec] * (SPAN + 1),
        out_specs=[head_spec, head_spec, prompt_spec] + [resp_spec] * (SPAN + 1),
        out_shape=[
            jax.ShapeDtypeStruct(resp_q.shape, jnp.bfloat16),
            jax.ShapeDtypeStruct(resp_q.shape, jnp.bfloat16),
            jax.ShapeDtypeStruct(prompt_kv.shape, jnp.bfloat16),
            jax.ShapeDtypeStruct(resp_shape, jnp.float32),
        ]
        + [jax.ShapeDtypeStruct(resp_shape, jnp.bfloat16)] * SPAN,
        scratch_shapes=[
            pltpu.VMEM((SPAN + 1, rows, rows), jnp.float32),
            pltpu.VMEM((count, rows, wide), jnp.float32),
            pltpu.VMEM((count, rows, wide), jnp.bfloat16),
            pltpu.VMEM((count, HD, wide), jnp.float32),
            pltpu.VMEM((count, HD, wide), jnp.float32),
        ],
        compiler_params=pltpu.CompilerParams(vmem_limit_bytes=56 * 1024 * 1024),
        cost_estimate=pl.CostEstimate(
            flops=12 * HD * pairs, bytes_accessed=4 * resp_q.size * 2, transcendentals=pairs
        ),
        name="attention",
    )(meta, resp_q, grad_out, prompt_kv, *resp_kvs)


def passed_along(array, axis, by):
    devices = lax.axis_size(axis)
    pairs = [(i, i + by) for i in range(devices) if 0 <= i + by < devices]
    return lax.ppermute(array, axis, pairs)


def paired(keys, values, blocks):
    rows = keys.shape[0]
    stacked = jnp.stack(
        [keys.reshape(rows, blocks, HD), values.reshape(rows, blocks, HD)], axis=2
    )
    return stacked.reshape(rows, blocks * 2 * HD)


def unpaired(both):
    rows = both.shape[0]
    split = both.reshape(rows, -1, 2, HD)
    return split[:, :, 0].reshape(rows, -1), split[:, :, 1].reshape(rows, -1)


def shards(prompt_k, prompt_v, resp_q, resp_k, resp_v, grad_out, resp_lengths):
    kv_heads = resp_k.shape[1] // HD
    row_count = resp_q.shape[0]
    all_heads = prompt_k.shape[1] // HD
    first_row = (lax.axis_index("seq") * row_count).astype(jnp.int32)
    meta = jnp.concatenate([first_row[None], resp_lengths])

    prompt_kv = paired(prompt_k, prompt_v, all_heads)
    prompt_kv = lax.all_to_all(prompt_kv, "head", split_axis=1, concat_axis=0, tiled=True)
    prompt_kv = lax.all_gather(prompt_kv, "seq", axis=0, tiled=True)

    resp_kv = paired(resp_k, resp_v, kv_heads)
    resp_kvs = [resp_kv] + [
        passed_along(resp_kv, "seq", distance) for distance in range(1, SPAN + 1)
    ]

    resp_out, grad_q, grad_prompt, own, *others = attention(
        meta, resp_q, grad_out, prompt_kv, resp_kvs
    )

    grad_prompt = lax.psum_scatter(grad_prompt, "seq", scatter_dimension=0, tiled=True)
    grad_prompt = lax.all_to_all(grad_prompt, "head", split_axis=0, concat_axis=1, tiled=True)
    for distance, part in enumerate(others, start=1):
        own = own + passed_along(part, "seq", -distance).astype(jnp.float32)
    grad_k_resp, grad_v_resp = unpaired(own.astype(jnp.bfloat16))
    grad_k_prompt, grad_v_prompt = unpaired(grad_prompt)
    return (resp_out, grad_q, grad_k_resp, grad_v_resp, grad_k_prompt, grad_v_prompt)


def solution(mesh):
    placed = (
        P(("seq", "head"), None),
        P(("seq", "head"), None),
        P("seq", "head"),
        P("seq", "head"),
        P("seq", "head"),
        P("seq", "head"),
        P(),
    )
    return jax.shard_map(
        shards,
        mesh=mesh,
        in_specs=placed,
        out_specs=(
            P("seq", "head"),
            P("seq", "head"),
            P("seq", "head"),
            P("seq", "head"),
            P(("seq", "head"), None),
            P(("seq", "head"), None),
        ),
        check_vma=False,
    )
```

```python
import functools
import math

import jax
import jax.numpy as jnp
from jax import lax
from jax.experimental import pallas as pl
from jax.experimental.pallas import tpu as pltpu
from jax.sharding import PartitionSpec as P

HD = 128
CORES = 2
FAR = 4
HEADS_PER_STEP = 2
CHUNK = 256
NEG = -1e30
NT = (((1,), (1,)), ((), ()))
BF16 = jnp.bfloat16
F32 = jnp.float32


def dot(a, b):
    return jnp.dot(a, b, preferred_element_type=F32)


def dot_nt(a, b):
    return lax.dot_general(a, b, NT, preferred_element_type=F32)


def whole(count):
    return [pl.BlockSpec(memory_space=pltpu.VMEM)] * count


def local_call(kernel, name, inputs, outputs, scratch=()):
    return pl.pallas_call(
        kernel,
        in_specs=whole(len(inputs)),
        out_specs=whole(len(outputs)),
        out_shape=[jax.ShapeDtypeStruct(shape, kind) for shape, kind in outputs],
        scratch_shapes=list(scratch),
        compiler_params=pltpu.CompilerParams(vmem_limit_bytes=40 * 1024 * 1024),
        name=name,
    )(*inputs)


def pack_kernel(pk_ref, pv_ref, rk_ref, rv_ref, *outs):
    pieces, resp = outs[:-1], outs[-1]
    head = lax.axis_index("head")
    width = pieces[0].shape[1]
    for k, piece in enumerate(pieces):
        start = pl.multiple_of((head ^ k) * (width // 2), HD)
        for n in range(width // (2 * HD)):
            at = pl.multiple_of(start + n * HD, HD)
            piece[:, 2 * n * HD : (2 * n + 1) * HD] = pk_ref[:, pl.ds(at, HD)]
            piece[:, (2 * n + 1) * HD : (2 * n + 2) * HD] = pv_ref[:, pl.ds(at, HD)]
    for n in range(width // (2 * HD)):
        resp[:, 2 * n * HD : (2 * n + 1) * HD] = rk_ref[:, n * HD : (n + 1) * HD]
        resp[:, (2 * n + 1) * HD : (2 * n + 2) * HD] = rv_ref[:, n * HD : (n + 1) * HD]


def merge_kernel(parts, rows, kept_ref, got_ref, *outs):
    pieces, back1, back2, own = outs[:parts], outs[parts], outs[parts + 1], outs[parts + 2]
    core = lax.rem(lax.axis_index("seq"), CORES)
    to_own = jnp.where(core == 0, 1.0, 0.0)
    half = kept_ref.shape[0] - 3 * rows
    share = half // parts
    for k, piece in enumerate(pieces):
        at = slice(k * share, (k + 1) * share)
        piece[...] = (kept_ref[at] + got_ref[at].astype(F32)).astype(BF16)
    one, two, three = half + rows, half + 2 * rows, half + 3 * rows
    back1[...] = (kept_ref[half:one] + got_ref[half:one].astype(F32)).astype(BF16)
    chosen = got_ref[one:two].astype(F32)
    back2[...] = (kept_ref[one:two] + chosen * (1.0 - to_own)).astype(BF16)
    own[...] = kept_ref[two:three] + chosen * to_own


def sum_kernel(parts, *refs):
    ins, outs, total = refs[:parts], refs[parts:-1], refs[-1]
    acc = ins[0][...].astype(F32)
    for ref in ins[1:]:
        acc = acc + ref[...].astype(F32)
    total[...] = acc
    share = total.shape[0] // len(outs)
    for k, out in enumerate(outs):
        out[...] = total[k * share : (k + 1) * share].astype(BF16)


def finish_prompt_kernel(*refs):
    pieces, (gk_ref, gv_ref) = refs[:-2], refs[-2:]
    head = lax.axis_index("head")
    width = pieces[0].shape[1]
    for k, piece in enumerate(pieces):
        start = pl.multiple_of((head ^ k) * (width // 2), HD)
        for n in range(width // (2 * HD)):
            at = pl.multiple_of(start + n * HD, HD)
            gk_ref[:, pl.ds(at, HD)] = piece[:, 2 * n * HD : (2 * n + 1) * HD]
            gv_ref[:, pl.ds(at, HD)] = piece[:, (2 * n + 1) * HD : (2 * n + 2) * HD]


def finish_resp_kernel(own_ref, one_ref, two_ref, gk_ref, gv_ref):
    total = (own_ref[...] + one_ref[...].astype(F32) + two_ref[...].astype(F32)).astype(BF16)
    for n in range(own_ref.shape[1] // (2 * HD)):
        gk_ref[:, n * HD : (n + 1) * HD] = total[:, 2 * n * HD : (2 * n + 1) * HD]
        gv_ref[:, n * HD : (n + 1) * HD] = total[:, (2 * n + 1) * HD : (2 * n + 2) * HD]


def attention_kernel(
    tokens, lengths, q_ref, do_ref, sent_ref, got_ref, own_ref, far_ref,
    o_ref, dq_ref, kept_ref, back_ref,
    bias, keys, values, q_all, do_all, s_buf, p_buf, o_all, dq_all, dk_t, dv_t,
):
    heads = q_ref.shape[1] // HD
    rows = heads * tokens
    total_keys = keys.shape[0]
    prompt_len = total_keys - 5 * tokens
    half = prompt_len // 2
    step = pl.program_id(1)
    last = pl.num_programs(1) - 1
    score_scale = 1.0 / math.sqrt(HD)
    exp_scale = score_scale * math.log2(math.e)
    resp_at = [prompt_len + i * tokens for i in range(6)]
    pieces = [
        (sent_ref, 0, half, 0),
        (got_ref, 0, half, half),
        (own_ref, 0, tokens, resp_at[0]),
        (sent_ref, half, tokens, resp_at[1]),
        (far_ref, 0, tokens, resp_at[2]),
        (got_ref, half, tokens, resp_at[3]),
        (got_ref, half + tokens, tokens, resp_at[4]),
    ]

    @pl.when((step == 0) & (pl.program_id(0) == 0))
    def _():
        place = lax.axis_index("seq")
        core = lax.rem(place, CORES)
        first_row = place * tokens
        row_pos = first_row + lax.broadcasted_iota(jnp.int32, (tokens, tokens), 0)
        seg_start = jnp.zeros((tokens, tokens), jnp.int32)
        end = jnp.int32(0)
        for i in range(lengths.shape[0]):
            end = end + lengths[i]
            seg_start = jnp.where(row_pos >= end, end, seg_start)
        near = 1 + 2 * core
        for i, distance in enumerate((0, 2, FAR, near, 4 - near)):
            key_pos = (first_row - distance * tokens) + lax.broadcasted_iota(
                jnp.int32, (tokens, tokens), 1
            )
            allowed = (key_pos >= seg_start) & (key_pos <= row_pos)
            bias[i] = jnp.where(allowed, 0.0, NEG)

    @pl.when(step == 0)
    def _():
        dk_t[...] = jnp.zeros_like(dk_t)
        dv_t[...] = jnp.zeros_like(dv_t)
        for ref, start, size, at in pieces:
            keys[at : at + size] = ref[start : start + size, :HD]
            values[at : at + size] = ref[start : start + size, HD:]

    for g in range(heads):
        q_all[g * tokens : (g + 1) * tokens] = q_ref[:, g * HD : (g + 1) * HD]
        do_all[g * tokens : (g + 1) * tokens] = do_ref[:, g * HD : (g + 1) * HD]

    q = q_all[...]
    top = None
    chunks = [slice(at, at + CHUNK) for at in range(0, total_keys, CHUNK)]
    for at in chunks:
        s = dot_nt(q, keys[at])
        if at.start >= prompt_len:
            which = (at.start - prompt_len) // tokens
            s = jnp.concatenate(
                [s[g * tokens : (g + 1) * tokens] + bias[which] for g in range(heads)], axis=0
            )
        s_buf[:, at] = s
        for col in range(0, CHUNK, HD):
            part = s[:, col : col + HD]
            top = part if top is None else jnp.maximum(top, part)
    top = jnp.max(top, axis=1, keepdims=True) * exp_scale

    total = jnp.zeros((rows, HD), F32)
    out = jnp.zeros((rows, HD), F32)
    for at in chunks:
        p = jnp.exp2(s_buf[:, at] * exp_scale - top)
        for col in range(0, CHUNK, HD):
            total = total + p[:, col : col + HD]
        p = p.astype(BF16)
        p_buf[:, at] = p
        out = out + dot(p, values[at])
    inverse = 1.0 / jnp.sum(total, axis=1, keepdims=True)
    out = (out * inverse).astype(BF16)
    o_all[...] = out
    cot = (do_all[...].astype(F32) * inverse).astype(BF16)
    delta = jnp.sum(cot.astype(F32) * out.astype(F32), axis=1, keepdims=True)
    cot_t = cot.T
    q_t = q.T
    dq = jnp.zeros((rows, HD), F32)
    for at in chunks:
        p = p_buf[:, at]
        dp = dot_nt(cot, values[at])
        ds = (p.astype(F32) * (dp - delta)).astype(BF16)
        dq = dq + dot(ds, keys[at])
        dv_t[:, at] += dot(cot_t, p)
        dk_t[:, at] += dot(q_t, ds)
    dq_all[...] = (dq * score_scale).astype(BF16)
    for g in range(heads):
        o_ref[:, g * HD : (g + 1) * HD] = o_all[g * tokens : (g + 1) * tokens]
        dq_ref[:, g * HD : (g + 1) * HD] = dq_all[g * tokens : (g + 1) * tokens]

    targets = [
        (kept_ref, 0, half, 0),
        (back_ref, 0, half, half),
        (kept_ref, half + 2 * tokens, tokens, resp_at[0]),
        (kept_ref, half, tokens, resp_at[1]),
        (kept_ref, half + tokens, tokens, resp_at[2]),
        (back_ref, half, tokens, resp_at[3]),
        (back_ref, half + tokens, tokens, resp_at[4]),
    ]

    @pl.when(step == last)
    def _():
        for ref, start, size, at in targets:
            grad_k = (dk_t[:, at : at + size] * score_scale).T
            grad_v = dv_t[:, at : at + size].T
            ref[start : start + size, :HD] = grad_k.astype(ref.dtype)
            ref[start : start + size, HD:] = grad_v.astype(ref.dtype)


def attention(lengths, resp_q, grad_out, sent, got, own, far):
    tokens = resp_q.shape[0]
    half = sent.shape[0] - 2 * tokens
    total_keys = 2 * half + 5 * tokens
    kv_heads = sent.shape[1] // (2 * HD)
    heads = HEADS_PER_STEP
    steps = resp_q.shape[1] // HD // kv_heads // heads
    rows = heads * tokens
    head_spec = pl.BlockSpec((tokens, heads * HD), lambda n, g: (0, n * steps + g))

    def kv_spec(size):
        return pl.BlockSpec((size, 2 * HD), lambda n, g: (0, n))

    pairs = rows * kv_heads * steps * total_keys
    return pl.pallas_call(
        functools.partial(attention_kernel, tokens),
        grid=(kv_heads, steps),
        in_specs=[
            pl.BlockSpec(memory_space=pltpu.SMEM),
            head_spec,
            head_spec,
            kv_spec(sent.shape[0]),
            kv_spec(got.shape[0]),
            kv_spec(tokens),
            kv_spec(tokens),
        ],
        out_specs=[head_spec, head_spec, kv_spec(half + 3 * tokens), kv_spec(half + 2 * tokens)],
        out_shape=[
            jax.ShapeDtypeStruct(resp_q.shape, BF16),
            jax.ShapeDtypeStruct(resp_q.shape, BF16),
            jax.ShapeDtypeStruct((half + 3 * tokens, sent.shape[1]), F32),
            jax.ShapeDtypeStruct((half + 2 * tokens, sent.shape[1]), BF16),
        ],
        scratch_shapes=[
            pltpu.VMEM((5, tokens, tokens), F32),
            pltpu.VMEM((total_keys, HD), BF16),
            pltpu.VMEM((total_keys, HD), BF16),
            pltpu.VMEM((rows, HD), BF16),
            pltpu.VMEM((rows, HD), BF16),
            pltpu.VMEM((rows, total_keys), F32),
            pltpu.VMEM((rows, total_keys), BF16),
            pltpu.VMEM((rows, HD), BF16),
            pltpu.VMEM((rows, HD), BF16),
            pltpu.VMEM((HD, total_keys), F32),
            pltpu.VMEM((HD, total_keys), F32),
        ],
        compiler_params=pltpu.CompilerParams(vmem_limit_bytes=56 * 1024 * 1024),
        cost_estimate=pl.CostEstimate(
            flops=12 * HD * pairs, bytes_accessed=8 * resp_q.size, transcendentals=pairs
        ),
        name="attention",
    )(lengths, resp_q, grad_out, sent, got, own, far)


def swap_heads(array, by):
    devices = lax.axis_size("head")
    return lax.ppermute(array, "head", [(i, i ^ by) for i in range(devices)])


def swap_chips(array, by):
    devices = lax.axis_size("seq")
    return lax.ppermute(array, "seq", [(i, i ^ (by * CORES)) for i in range(devices)])


def swap_cores(array):
    devices = lax.axis_size("seq")
    return lax.ppermute(array, "seq", [(i, i ^ 1) for i in range(devices)])


def shift_chips(array, by):
    devices = lax.axis_size("seq")
    by = by * CORES
    return lax.ppermute(array, "seq", [(i, i + by) for i in range(devices) if 0 <= i + by < devices])


def shards(prompt_k, prompt_v, resp_q, resp_k, resp_v, grad_out, resp_lengths):
    tokens, kv_cols = resp_k.shape
    wide = 2 * kv_cols
    groups = lax.axis_size("head")
    chips = lax.axis_size("seq") // CORES
    block = prompt_k.shape[0]
    core = lax.rem(lax.axis_index("seq"), CORES)

    *pieces, own = local_call(
        pack_kernel,
        "pack",
        [prompt_k, prompt_v, resp_k, resp_v],
        [((block, wide), BF16)] * groups + [((tokens, wide), BF16)],
    )
    pieces = [pieces[0]] + [swap_heads(pieces[k], k) for k in range(1, groups)]
    near = shift_chips(own, 1)
    far = shift_chips(own, 2)
    mine = jnp.concatenate(pieces, axis=0)
    parts = [mine] + [swap_chips(mine, k) for k in range(1, chips)]
    chosen = jnp.where(core == 1, far, own)
    sent = jnp.concatenate(parts + [near, chosen], axis=0)
    got = swap_cores(sent)

    resp_out, grad_q, kept, back = attention(
        resp_lengths, resp_q, grad_out, sent, got, own, far
    )

    back = swap_cores(back)
    share = groups * block
    *parts, near, far, own = local_call(
        functools.partial(merge_kernel, chips, tokens),
        "merge",
        [kept, back],
        [((share, wide), BF16)] * chips
        + [((tokens, wide), BF16)] * 2
        + [((tokens, wide), F32)],
    )
    parts = [parts[0]] + [swap_chips(parts[k], k) for k in range(1, chips)]
    near = shift_chips(near, -1)
    far = shift_chips(far, -2)
    pieces = local_call(
        functools.partial(sum_kernel, chips),
        "sum_chips",
        parts,
        [((block, wide), BF16)] * groups,
        [pltpu.VMEM((share, wide), F32)],
    )
    pieces = [pieces[0]] + [swap_heads(pieces[k], k) for k in range(1, groups)]
    grad_k_resp, grad_v_resp = local_call(
        finish_resp_kernel, "finish_resp", [own, near, far], [((tokens, kv_cols), BF16)] * 2
    )
    grad_k_prompt, grad_v_prompt = local_call(
        finish_prompt_kernel, "finish_prompt", pieces, [(prompt_k.shape, BF16)] * 2
    )
    return (resp_out, grad_q, grad_k_resp, grad_v_resp, grad_k_prompt, grad_v_prompt)


def solution(mesh):
    placed = (
        P(("seq", "head"), None),
        P(("seq", "head"), None),
        P("seq", "head"),
        P("seq", "head"),
        P("seq", "head"),
        P("seq", "head"),
        P(),
    )
    return jax.shard_map(
        shards,
        mesh=mesh,
        in_specs=placed,
        out_specs=(
            P("seq", "head"),
            P("seq", "head"),
            P("seq", "head"),
            P("seq", "head"),
            P(("seq", "head"), None),
            P(("seq", "head"), None),
        ),
        check_vma=False,
    )
```

```python
import functools
import math

import jax
import jax.numpy as jnp
from jax import lax
from jax.experimental import pallas as pl
from jax.experimental.pallas import tpu as pltpu
from jax.sharding import PartitionSpec as P

HD = 128
CORES = 2
FAR = 4
CHUNK = 256
NEG = -1e30
BF16 = jnp.bfloat16
F32 = jnp.float32


def dot(a, b):
    return jnp.dot(a, b, preferred_element_type=F32)


def whole(count):
    return [pl.BlockSpec(memory_space=pltpu.VMEM)] * count


def local_call(kernel, name, inputs, outputs, scratch=()):
    return pl.pallas_call(
        kernel,
        in_specs=whole(len(inputs)),
        out_specs=whole(len(outputs)),
        out_shape=[jax.ShapeDtypeStruct(shape, kind) for shape, kind in outputs],
        scratch_shapes=list(scratch),
        compiler_params=pltpu.CompilerParams(vmem_limit_bytes=40 * 1024 * 1024),
        name=name,
    )(*inputs)


def pack_kernel(pk_ref, pv_ref, rk_ref, rv_ref, *outs):
    pieces, resp = outs[:-1], outs[-1]
    head = lax.axis_index("head")
    width = pieces[0].shape[1]
    for k, piece in enumerate(pieces):
        start = pl.multiple_of((head ^ k) * (width // 2), HD)
        for n in range(width // (2 * HD)):
            at = pl.multiple_of(start + n * HD, HD)
            piece[:, 2 * n * HD : (2 * n + 1) * HD] = pk_ref[:, pl.ds(at, HD)]
            piece[:, (2 * n + 1) * HD : (2 * n + 2) * HD] = pv_ref[:, pl.ds(at, HD)]
    for n in range(width // (2 * HD)):
        resp[:, 2 * n * HD : (2 * n + 1) * HD] = rk_ref[:, n * HD : (n + 1) * HD]
        resp[:, (2 * n + 1) * HD : (2 * n + 2) * HD] = rv_ref[:, n * HD : (n + 1) * HD]


def pack(inputs, groups):
    def one(array):
        return pl.BlockSpec(array.shape, lambda i: (0, 0))

    block, tokens = inputs[0].shape[0], inputs[2].shape[0]
    wide = 2 * inputs[2].shape[1]
    shapes = [(block, wide)] * groups + [(tokens, wide)]
    return pl.pallas_call(
        pack_kernel,
        grid=(1,),
        in_specs=[one(array) for array in inputs],
        out_specs=whole(groups + 1),
        out_shape=[jax.ShapeDtypeStruct(shape, BF16) for shape in shapes],
        compiler_params=pltpu.CompilerParams(vmem_limit_bytes=56 * 1024 * 1024),
        name="pack",
    )(*inputs)


def merge_kernel(parts, rows, kept_ref, got_ref, *outs):
    pieces, back1, back2, own = outs[:parts], outs[parts], outs[parts + 1], outs[parts + 2]
    core = lax.rem(lax.axis_index("seq"), CORES)
    to_own = jnp.where(core == 0, 1.0, 0.0)
    half = kept_ref.shape[0] - 3 * rows
    share = half // parts
    for k, piece in enumerate(pieces):
        at = slice(k * share, (k + 1) * share)
        piece[...] = (kept_ref[at] + got_ref[at].astype(F32)).astype(BF16)
    one, two, three = half + rows, half + 2 * rows, half + 3 * rows
    back1[...] = (kept_ref[half:one] + got_ref[half:one].astype(F32)).astype(BF16)
    chosen = got_ref[one:two].astype(F32)
    back2[...] = (kept_ref[one:two] + chosen * (1.0 - to_own)).astype(BF16)
    own[...] = kept_ref[two:three] + chosen * to_own


def sum_kernel(parts, *refs):
    ins, outs, total = refs[:parts], refs[parts:-1], refs[-1]
    acc = ins[0][...].astype(F32)
    for ref in ins[1:]:
        acc = acc + ref[...].astype(F32)
    total[...] = acc
    share = total.shape[0] // len(outs)
    for k, out in enumerate(outs):
        out[...] = total[k * share : (k + 1) * share].astype(BF16)


def finish_kernel(own_ref, one_ref, two_ref, *refs):
    pieces, (gk_ref, gv_ref, rk_ref, rv_ref) = refs[:-4], refs[-4:]
    head = lax.axis_index("head")
    width = pieces[0].shape[1]
    for k, piece in enumerate(pieces):
        start = pl.multiple_of((head ^ k) * (width // 2), HD)
        for n in range(width // (2 * HD)):
            at = pl.multiple_of(start + n * HD, HD)
            gk_ref[:, pl.ds(at, HD)] = piece[:, 2 * n * HD : (2 * n + 1) * HD]
            gv_ref[:, pl.ds(at, HD)] = piece[:, (2 * n + 1) * HD : (2 * n + 2) * HD]
    total = (own_ref[...] + one_ref[...].astype(F32) + two_ref[...].astype(F32)).astype(BF16)
    for n in range(width // (2 * HD)):
        rk_ref[:, n * HD : (n + 1) * HD] = total[:, 2 * n * HD : (2 * n + 1) * HD]
        rv_ref[:, n * HD : (n + 1) * HD] = total[:, (2 * n + 1) * HD : (2 * n + 2) * HD]


def attention_kernel(
    tokens, lengths, q_ref, do_ref, sent_ref, got_ref, own_ref, far_ref,
    o_ref, dq_ref, kept_ref, back_ref,
    bias, keys, values, keys_t, values_t, s_buf, p_buf, dk, dv,
):
    total_keys = keys.shape[0]
    prompt_len = total_keys - 5 * tokens
    half = prompt_len // 2
    head = pl.program_id(0)
    step = pl.program_id(1)
    last = pl.num_programs(1) - 1
    score_scale = 1.0 / math.sqrt(HD)
    exp_scale = score_scale * math.log2(math.e)
    k_cols = pl.ds(pl.multiple_of(head * 2 * HD, HD), HD)
    v_cols = pl.ds(pl.multiple_of(head * 2 * HD + HD, HD), HD)
    resp_at = [prompt_len + i * tokens for i in range(6)]
    pieces = [
        (sent_ref, 0, half, 0),
        (got_ref, 0, half, half),
        (own_ref, 0, tokens, resp_at[0]),
        (sent_ref, half, tokens, resp_at[1]),
        (far_ref, 0, tokens, resp_at[2]),
        (got_ref, half, tokens, resp_at[3]),
        (got_ref, half + tokens, tokens, resp_at[4]),
    ]

    @pl.when((step == 0) & (head == 0))
    def _():
        place = lax.axis_index("seq")
        core = lax.rem(place, CORES)
        first_row = place * tokens
        row_pos = first_row + lax.broadcasted_iota(jnp.int32, (tokens, tokens), 1)
        seg_start = jnp.zeros((tokens, tokens), jnp.int32)
        end = jnp.int32(0)
        for i in range(lengths.shape[0]):
            end = end + lengths[i]
            seg_start = jnp.where(row_pos >= end, end, seg_start)
        near = 1 + 2 * core
        for i, distance in enumerate((0, 2, FAR, near, 4 - near)):
            key_pos = (first_row - distance * tokens) + lax.broadcasted_iota(
                jnp.int32, (tokens, tokens), 0
            )
            allowed = (key_pos >= seg_start) & (key_pos <= row_pos)
            bias[i] = jnp.where(allowed, 0.0, NEG)

    @pl.when(step == 0)
    def _():
        dk[...] = jnp.zeros_like(dk)
        dv[...] = jnp.zeros_like(dv)
        for ref, start, size, at in pieces:
            k_rows = ref[start : start + size, k_cols]
            v_rows = ref[start : start + size, v_cols]
            keys[at : at + size] = k_rows
            values[at : at + size] = v_rows
            keys_t[:, at : at + size] = k_rows.T
            values_t[:, at : at + size] = v_rows.T

    q = q_ref[...]
    q_t = q.T
    chunks = [slice(at, at + CHUNK) for at in range(0, total_keys, CHUNK)]
    top = None
    for at in chunks:
        s = dot(keys[at], q_t)
        if at.start >= prompt_len:
            s = s + bias[(at.start - prompt_len) // tokens]
        s_buf[at] = s
        part = jnp.max(s.reshape(CHUNK // 8, 8, tokens), axis=0)
        top = part if top is None else jnp.maximum(top, part)
    top = jnp.max(top, axis=0, keepdims=True) * exp_scale

    total = jnp.zeros((8, tokens), F32)
    out = jnp.zeros((HD, tokens), F32)
    for at in chunks:
        p = jnp.exp2(s_buf[at] * exp_scale - top)
        total = total + jnp.sum(p.reshape(CHUNK // 8, 8, tokens), axis=0)
        p = p.astype(BF16)
        p_buf[at] = p
        out = out + dot(values_t[:, at], p)
    inverse = 1.0 / jnp.sum(total, axis=0, keepdims=True)
    out = (out * inverse).astype(BF16)
    o_ref[...] = out.T
    cot_t = (do_ref[...].T.astype(F32) * inverse).astype(BF16)
    delta = jnp.sum(cot_t.astype(F32) * out.astype(F32), axis=0, keepdims=True)
    cot = cot_t.T
    dq = jnp.zeros((HD, tokens), F32)
    for at in chunks:
        p = p_buf[at]
        dp = dot(values[at], cot_t)
        ds = (p.astype(F32) * (dp - delta)).astype(BF16)
        dq = dq + dot(keys_t[:, at], ds)
        dv[at] += dot(p, cot)
        dk[at] += dot(ds, q)
    dq_ref[...] = (dq * score_scale).T.astype(BF16)

    targets = [
        (kept_ref, 0, half, 0),
        (back_ref, 0, half, half),
        (kept_ref, half + 2 * tokens, tokens, resp_at[0]),
        (kept_ref, half, tokens, resp_at[1]),
        (kept_ref, half + tokens, tokens, resp_at[2]),
        (back_ref, half, tokens, resp_at[3]),
        (back_ref, half + tokens, tokens, resp_at[4]),
    ]

    @pl.when(step == last)
    def _():
        for ref, start, size, at in targets:
            ref[start : start + size, k_cols] = (dk[at : at + size] * score_scale).astype(ref.dtype)
            ref[start : start + size, v_cols] = dv[at : at + size].astype(ref.dtype)


def attention(lengths, resp_q, grad_out, sent, got, own, far):
    tokens = resp_q.shape[0]
    half = sent.shape[0] - 2 * tokens
    total_keys = 2 * half + 5 * tokens
    kv_heads = sent.shape[1] // (2 * HD)
    steps = resp_q.shape[1] // HD // kv_heads
    head_spec = pl.BlockSpec((tokens, HD), lambda n, g: (0, n * steps + g))
    pairs = tokens * kv_heads * steps * total_keys
    return pl.pallas_call(
        functools.partial(attention_kernel, tokens),
        grid=(kv_heads, steps),
        in_specs=[pl.BlockSpec(memory_space=pltpu.SMEM), head_spec, head_spec] + whole(4),
        out_specs=[head_spec, head_spec] + whole(2),
        out_shape=[
            jax.ShapeDtypeStruct(resp_q.shape, BF16),
            jax.ShapeDtypeStruct(resp_q.shape, BF16),
            jax.ShapeDtypeStruct((half + 3 * tokens, sent.shape[1]), F32),
            jax.ShapeDtypeStruct((half + 2 * tokens, sent.shape[1]), BF16),
        ],
        scratch_shapes=[
            pltpu.VMEM((5, tokens, tokens), F32),
            pltpu.VMEM((total_keys, HD), BF16),
            pltpu.VMEM((total_keys, HD), BF16),
            pltpu.VMEM((HD, total_keys), BF16),
            pltpu.VMEM((HD, total_keys), BF16),
            pltpu.VMEM((total_keys, tokens), F32),
            pltpu.VMEM((total_keys, tokens), BF16),
            pltpu.VMEM((total_keys, HD), F32),
            pltpu.VMEM((total_keys, HD), F32),
        ],
        compiler_params=pltpu.CompilerParams(vmem_limit_bytes=44 * 1024 * 1024),
        cost_estimate=pl.CostEstimate(
            flops=12 * HD * pairs, bytes_accessed=8 * resp_q.size, transcendentals=pairs
        ),
        name="attention",
    )(lengths, resp_q, grad_out, sent, got, own, far)


def swap_heads(array, by):
    devices = lax.axis_size("head")
    return lax.ppermute(array, "head", [(i, i ^ by) for i in range(devices)])


def swap_chips(array, by):
    devices = lax.axis_size("seq")
    return lax.ppermute(array, "seq", [(i, i ^ (by * CORES)) for i in range(devices)])


def swap_cores(array):
    devices = lax.axis_size("seq")
    return lax.ppermute(array, "seq", [(i, i ^ 1) for i in range(devices)])


def shift_chips(array, by):
    devices = lax.axis_size("seq")
    by = by * CORES
    return lax.ppermute(array, "seq", [(i, i + by) for i in range(devices) if 0 <= i + by < devices])


def shards(prompt_k, prompt_v, resp_q, resp_k, resp_v, grad_out, resp_lengths):
    tokens, kv_cols = resp_k.shape
    wide = 2 * kv_cols
    groups = lax.axis_size("head")
    chips = lax.axis_size("seq") // CORES
    block = prompt_k.shape[0]
    core = lax.rem(lax.axis_index("seq"), CORES)

    *pieces, own = pack([prompt_k, prompt_v, resp_k, resp_v], groups)
    pieces = [pieces[0]] + [swap_heads(pieces[k], k) for k in range(1, groups)]
    near = shift_chips(own, 1)
    far = shift_chips(own, 2)
    pieces, near, far = lax.optimization_barrier((pieces, near, far))
    mine = jnp.concatenate(pieces, axis=0)
    parts = [mine] + [swap_chips(mine, k) for k in range(1, chips)]
    chosen = jnp.where(core == 1, far, own)
    sent = jnp.concatenate(parts + [near, chosen], axis=0)
    got = swap_cores(sent)

    resp_out, grad_q, kept, back = attention(
        resp_lengths, resp_q, grad_out, sent, got, own, far
    )

    back = swap_cores(back)
    share = groups * block
    *parts, near, far, own = local_call(
        functools.partial(merge_kernel, chips, tokens),
        "merge",
        [kept, back],
        [((share, wide), BF16)] * chips
        + [((tokens, wide), BF16)] * 2
        + [((tokens, wide), F32)],
    )
    parts = [parts[0]] + [swap_chips(parts[k], k) for k in range(1, chips)]
    parts, near, far = lax.optimization_barrier((parts, near, far))
    near = shift_chips(near, -1)
    far = shift_chips(far, -2)
    pieces = local_call(
        functools.partial(sum_kernel, chips),
        "sum_chips",
        parts,
        [((block, wide), BF16)] * groups,
        [pltpu.VMEM((share, wide), F32)],
    )
    pieces = [pieces[0]] + [swap_heads(pieces[k], k) for k in range(1, groups)]
    grad_k_prompt, grad_v_prompt, grad_k_resp, grad_v_resp = local_call(
        finish_kernel,
        "finish",
        [own, near, far] + pieces,
        [(prompt_k.shape, BF16)] * 2 + [((tokens, kv_cols), BF16)] * 2,
    )
    return (resp_out, grad_q, grad_k_resp, grad_v_resp, grad_k_prompt, grad_v_prompt)


def solution(mesh):
    placed = (
        P(("seq", "head"), None),
        P(("seq", "head"), None),
        P("seq", "head"),
        P("seq", "head"),
        P("seq", "head"),
        P("seq", "head"),
        P(),
    )
    return jax.shard_map(
        shards,
        mesh=mesh,
        in_specs=placed,
        out_specs=(
            P("seq", "head"),
            P("seq", "head"),
            P("seq", "head"),
            P("seq", "head"),
            P(("seq", "head"), None),
            P(("seq", "head"), None),
        ),
        check_vma=False,
    )
```

```python
import functools
import math

import jax
import jax.numpy as jnp
from jax import lax
from jax.experimental import pallas as pl
from jax.experimental.pallas import tpu as pltpu
from jax.sharding import PartitionSpec as P

HD = 128
CORES = 2
FAR = 4
CHUNK = 256
NEG = -1e30
NT = (((1,), (1,)), ((), ()))
BF16 = jnp.bfloat16
F32 = jnp.float32


def dot(a, b):
    return jnp.dot(a, b, preferred_element_type=F32)


def dot_nt(a, b):
    return lax.dot_general(a, b, NT, preferred_element_type=F32)


def whole(count):
    return [pl.BlockSpec(memory_space=pltpu.VMEM)] * count


def local_call(kernel, name, inputs, outputs, scratch=()):
    return pl.pallas_call(
        kernel,
        in_specs=whole(len(inputs)),
        out_specs=whole(len(outputs)),
        out_shape=[jax.ShapeDtypeStruct(shape, kind) for shape, kind in outputs],
        scratch_shapes=list(scratch),
        compiler_params=pltpu.CompilerParams(vmem_limit_bytes=40 * 1024 * 1024),
        name=name,
    )(*inputs)


def pack_kernel(pk_ref, pv_ref, rk_ref, rv_ref, *outs):
    pieces, resp = outs[:-1], outs[-1]
    head = lax.axis_index("head")
    width = pieces[0].shape[1]
    for k, piece in enumerate(pieces):
        start = pl.multiple_of((head ^ k) * (width // 2), HD)
        for n in range(width // (2 * HD)):
            at = pl.multiple_of(start + n * HD, HD)
            piece[:, 2 * n * HD : (2 * n + 1) * HD] = pk_ref[:, pl.ds(at, HD)]
            piece[:, (2 * n + 1) * HD : (2 * n + 2) * HD] = pv_ref[:, pl.ds(at, HD)]
    for n in range(width // (2 * HD)):
        resp[:, 2 * n * HD : (2 * n + 1) * HD] = rk_ref[:, n * HD : (n + 1) * HD]
        resp[:, (2 * n + 1) * HD : (2 * n + 2) * HD] = rv_ref[:, n * HD : (n + 1) * HD]


def pack(inputs, groups):
    def one(array):
        return pl.BlockSpec(array.shape, lambda i: (0, 0))

    block, tokens = inputs[0].shape[0], inputs[2].shape[0]
    wide = 2 * inputs[2].shape[1]
    shapes = [(block, wide)] * groups + [(tokens, wide)]
    return pl.pallas_call(
        pack_kernel,
        grid=(1,),
        in_specs=[one(array) for array in inputs],
        out_specs=whole(groups + 1),
        out_shape=[jax.ShapeDtypeStruct(shape, BF16) for shape in shapes],
        compiler_params=pltpu.CompilerParams(vmem_limit_bytes=56 * 1024 * 1024),
        name="pack",
    )(*inputs)


def merge_kernel(parts, rows, kept_ref, got_ref, *outs):
    pieces, back1, back2, own = outs[:parts], outs[parts], outs[parts + 1], outs[parts + 2]
    core = lax.rem(lax.axis_index("seq"), CORES)
    to_own = jnp.where(core == 0, 1.0, 0.0)
    half = kept_ref.shape[0] - 3 * rows
    share = half // parts
    for k, piece in enumerate(pieces):
        at = slice(k * share, (k + 1) * share)
        piece[...] = (kept_ref[at] + got_ref[at].astype(F32)).astype(BF16)
    one, two, three = half + rows, half + 2 * rows, half + 3 * rows
    back1[...] = (kept_ref[half:one] + got_ref[half:one].astype(F32)).astype(BF16)
    chosen = got_ref[one:two].astype(F32)
    back2[...] = (kept_ref[one:two] + chosen * (1.0 - to_own)).astype(BF16)
    own[...] = kept_ref[two:three] + chosen * to_own


def sum_kernel(parts, *refs):
    ins, outs, total = refs[:parts], refs[parts:-1], refs[-1]
    acc = ins[0][...].astype(F32)
    for ref in ins[1:]:
        acc = acc + ref[...].astype(F32)
    total[...] = acc
    share = total.shape[0] // len(outs)
    for k, out in enumerate(outs):
        out[...] = total[k * share : (k + 1) * share].astype(BF16)


def finish_kernel(own_ref, one_ref, two_ref, *refs):
    pieces, (gk_ref, gv_ref, rk_ref, rv_ref) = refs[:-4], refs[-4:]
    head = lax.axis_index("head")
    width = pieces[0].shape[1]
    for k, piece in enumerate(pieces):
        start = pl.multiple_of((head ^ k) * (width // 2), HD)
        for n in range(width // (2 * HD)):
            at = pl.multiple_of(start + n * HD, HD)
            gk_ref[:, pl.ds(at, HD)] = piece[:, 2 * n * HD : (2 * n + 1) * HD]
            gv_ref[:, pl.ds(at, HD)] = piece[:, (2 * n + 1) * HD : (2 * n + 2) * HD]
    total = (own_ref[...] + one_ref[...].astype(F32) + two_ref[...].astype(F32)).astype(BF16)
    for n in range(width // (2 * HD)):
        rk_ref[:, n * HD : (n + 1) * HD] = total[:, 2 * n * HD : (2 * n + 1) * HD]
        rv_ref[:, n * HD : (n + 1) * HD] = total[:, (2 * n + 1) * HD : (2 * n + 2) * HD]


def attention_kernel(
    tokens, lengths, q_ref, next_ref, do_ref, sent_ref, got_ref, own_ref, far_ref,
    o_ref, dq_ref, kept_ref, back_ref,
    bias, keys, values, s_even, s_odd, p_even, p_odd, top_even, dk_t, dv_t,
):
    total_keys = keys.shape[1]
    prompt_len = total_keys - 5 * tokens
    half = prompt_len // 2
    head = pl.program_id(0)
    step = pl.program_id(1)
    last = pl.num_programs(1) - 1
    score_scale = 1.0 / math.sqrt(HD)
    exp_scale = score_scale * math.log2(math.e)
    resp_at = [prompt_len + i * tokens for i in range(6)]
    chunks = [slice(at, at + CHUNK) for at in range(0, total_keys, CHUNK)]

    def front(q, at, which, s_buf, top):
        s = dot_nt(q, keys[which, at])
        if at.start >= prompt_len:
            s = s + bias[(at.start - prompt_len) // tokens]
        s_buf[:, at] = s
        for col in range(0, CHUNK, HD):
            part = s[:, col : col + HD]
            top = part if top is None else jnp.maximum(top, part)
        return top

    def middle(at, s_buf, p_buf, top, total, out):
        p = jnp.exp2(s_buf[:, at] * exp_scale - top)
        for col in range(0, CHUNK, HD):
            part = p[:, col : col + HD]
            total = part if total is None else total + part
        p = p.astype(BF16)
        p_buf[:, at] = p
        more = dot(p, values[head, at])
        return total, more if out is None else out + more

    def settle(q, cot, total, out):
        inverse = 1.0 / jnp.sum(total, axis=1, keepdims=True)
        out = (out * inverse).astype(BF16)
        wide = cot.astype(F32)
        delta = jnp.sum(wide * out.astype(F32), axis=1, keepdims=True)
        cot_t = (wide * inverse).astype(BF16).T
        q_t = (q.astype(F32) * inverse).astype(BF16).T
        return inverse, out, delta, cot_t, q_t

    def behind(at, p_buf, cot, delta, cot_t, q_t, dq):
        p = p_buf[:, at]
        dp = dot_nt(cot, values[head, at])
        ds = (p.astype(F32) * (dp - delta)).astype(BF16)
        dv_t[:, at] += dot(cot_t, p)
        dk_t[:, at] += dot(q_t, ds)
        more = dot(ds, keys[head, at])
        return more if dq is None else dq + more

    @pl.when((step == 0) & (head == 0))
    def _():
        place = lax.axis_index("seq")
        core = lax.rem(place, CORES)
        first_row = place * tokens
        row_pos = first_row + lax.broadcasted_iota(jnp.int32, (tokens, tokens), 0)
        seg_start = jnp.zeros((tokens, tokens), jnp.int32)
        end = jnp.int32(0)
        for i in range(lengths.shape[0]):
            end = end + lengths[i]
            seg_start = jnp.where(row_pos >= end, end, seg_start)
        near = 1 + 2 * core
        for i, distance in enumerate((0, 2, FAR, near, 4 - near)):
            key_pos = (first_row - distance * tokens) + lax.broadcasted_iota(
                jnp.int32, (tokens, tokens), 1
            )
            allowed = (key_pos >= seg_start) & (key_pos <= row_pos)
            bias[i] = jnp.where(allowed, 0.0, NEG)
        for n in range(keys.shape[0]):
            k_at, v_at = 2 * n * HD, (2 * n + 1) * HD
            for ref, start, size, at in (
                (sent_ref, 0, half, 0),
                (got_ref, 0, half, half),
                (own_ref, 0, tokens, resp_at[0]),
                (sent_ref, half, tokens, resp_at[1]),
                (far_ref, 0, tokens, resp_at[2]),
                (got_ref, half, tokens, resp_at[3]),
                (got_ref, half + tokens, tokens, resp_at[4]),
            ):
                keys[n, at : at + size] = ref[start : start + size, k_at : k_at + HD]
                values[n, at : at + size] = ref[start : start + size, v_at : v_at + HD]
        top = None
        for at in chunks:
            top = front(q_ref[:, :HD], at, 0, s_even, top)
        top_even[...] = top

    @pl.when(step == 0)
    def _():
        dk_t[...] = jnp.zeros_like(dk_t)
        dv_t[...] = jnp.zeros_like(dv_t)

    q_even, q_odd = q_ref[:, :HD], q_ref[:, HD:]
    cot_even, cot_odd = do_ref[:, :HD], do_ref[:, HD:]
    top = jnp.max(top_even[...], axis=1, keepdims=True) * exp_scale
    total, out, other = None, None, None
    for at in chunks:
        total, out = middle(at, s_even, p_even, top, total, out)
        other = front(q_odd, at, head, s_odd, other)
    inverse, out, delta, cot_t, q_t = settle(q_even, cot_even, total, out)
    o_ref[:, :HD] = out
    top = jnp.max(other, axis=1, keepdims=True) * exp_scale
    total, out, dq = None, None, None
    for at in chunks:
        dq = behind(at, p_even, cot_even, delta, cot_t, q_t, dq)
        total, out = middle(at, s_odd, p_odd, top, total, out)
    dq_ref[:, :HD] = (dq * (inverse * score_scale)).astype(BF16)
    inverse, out, delta, cot_t, q_t = settle(q_odd, cot_odd, total, out)
    o_ref[:, HD:] = out
    upcoming = jnp.minimum(head + (step == last).astype(jnp.int32), pl.num_programs(0) - 1)
    dq, other = None, None
    for at in chunks:
        dq = behind(at, p_odd, cot_odd, delta, cot_t, q_t, dq)
        other = front(next_ref[...], at, upcoming, s_even, other)
    dq_ref[:, HD:] = (dq * (inverse * score_scale)).astype(BF16)
    top_even[...] = other

    @pl.when(step == last)
    def _():
        k_cols = pl.ds(pl.multiple_of(head * 2 * HD, HD), HD)
        v_cols = pl.ds(pl.multiple_of(head * 2 * HD + HD, HD), HD)
        for ref, start, size, at in (
            (kept_ref, 0, half, 0),
            (back_ref, 0, half, half),
            (kept_ref, half + 2 * tokens, tokens, resp_at[0]),
            (kept_ref, half, tokens, resp_at[1]),
            (kept_ref, half + tokens, tokens, resp_at[2]),
            (back_ref, half, tokens, resp_at[3]),
            (back_ref, half + tokens, tokens, resp_at[4]),
        ):
            grad_k = (dk_t[:, at : at + size] * score_scale).T
            ref[start : start + size, k_cols] = grad_k.astype(ref.dtype)
            ref[start : start + size, v_cols] = dv_t[:, at : at + size].T.astype(ref.dtype)


def attention(lengths, resp_q, grad_out, sent, got, own, far):
    tokens = resp_q.shape[0]
    half = sent.shape[0] - 2 * tokens
    total_keys = 2 * half + 5 * tokens
    kv_heads = sent.shape[1] // (2 * HD)
    q_heads = resp_q.shape[1] // HD
    steps = q_heads // kv_heads // 2
    pair_spec = pl.BlockSpec((tokens, 2 * HD), lambda n, g: (0, n * steps + g))
    next_spec = pl.BlockSpec(
        (tokens, HD), lambda n, g: (0, jnp.minimum((n * steps + g) * 2 + 2, q_heads - 2))
    )
    pairs = tokens * q_heads * total_keys
    return pl.pallas_call(
        functools.partial(attention_kernel, tokens),
        grid=(kv_heads, steps),
        in_specs=[pl.BlockSpec(memory_space=pltpu.SMEM), pair_spec, next_spec, pair_spec]
        + whole(4),
        out_specs=[pair_spec, pair_spec] + whole(2),
        out_shape=[
            jax.ShapeDtypeStruct(resp_q.shape, BF16),
            jax.ShapeDtypeStruct(resp_q.shape, BF16),
            jax.ShapeDtypeStruct((half + 3 * tokens, sent.shape[1]), F32),
            jax.ShapeDtypeStruct((half + 2 * tokens, sent.shape[1]), BF16),
        ],
        scratch_shapes=[
            pltpu.VMEM((5, tokens, tokens), F32),
            pltpu.VMEM((kv_heads, total_keys, HD), BF16),
            pltpu.VMEM((kv_heads, total_keys, HD), BF16),
            pltpu.VMEM((tokens, total_keys), F32),
            pltpu.VMEM((tokens, total_keys), F32),
            pltpu.VMEM((tokens, total_keys), BF16),
            pltpu.VMEM((tokens, total_keys), BF16),
            pltpu.VMEM((tokens, HD), F32),
            pltpu.VMEM((HD, total_keys), F32),
            pltpu.VMEM((HD, total_keys), F32),
        ],
        compiler_params=pltpu.CompilerParams(vmem_limit_bytes=44 * 1024 * 1024),
        cost_estimate=pl.CostEstimate(
            flops=12 * HD * pairs, bytes_accessed=8 * resp_q.size, transcendentals=pairs
        ),
        name="attention",
    )(lengths, resp_q, resp_q, grad_out, sent, got, own, far)


def swap_heads(array, by):
    devices = lax.axis_size("head")
    return lax.ppermute(array, "head", [(i, i ^ by) for i in range(devices)])


def swap_chips(array, by):
    devices = lax.axis_size("seq")
    return lax.ppermute(array, "seq", [(i, i ^ (by * CORES)) for i in range(devices)])


def swap_cores(array):
    devices = lax.axis_size("seq")
    return lax.ppermute(array, "seq", [(i, i ^ 1) for i in range(devices)])


def shift_chips(array, by):
    devices = lax.axis_size("seq")
    by = by * CORES
    return lax.ppermute(array, "seq", [(i, i + by) for i in range(devices) if 0 <= i + by < devices])


def shards(prompt_k, prompt_v, resp_q, resp_k, resp_v, grad_out, resp_lengths):
    tokens, kv_cols = resp_k.shape
    wide = 2 * kv_cols
    groups = lax.axis_size("head")
    chips = lax.axis_size("seq") // CORES
    block = prompt_k.shape[0]
    core = lax.rem(lax.axis_index("seq"), CORES)

    *pieces, own = pack([prompt_k, prompt_v, resp_k, resp_v], groups)
    pieces = [pieces[0]] + [swap_heads(pieces[k], k) for k in range(1, groups)]
    near = shift_chips(own, 1)
    far = shift_chips(own, 2)
    pieces, near, far = lax.optimization_barrier((pieces, near, far))
    mine = jnp.concatenate(pieces, axis=0)
    parts = [mine] + [swap_chips(mine, k) for k in range(1, chips)]
    chosen = jnp.where(core == 1, far, own)
    sent = jnp.concatenate(parts + [near, chosen], axis=0)
    got = swap_cores(sent)

    resp_out, grad_q, kept, back = attention(
        resp_lengths, resp_q, grad_out, sent, got, own, far
    )

    back = swap_cores(back)
    share = groups * block
    *parts, near, far, own = local_call(
        functools.partial(merge_kernel, chips, tokens),
        "merge",
        [kept, back],
        [((share, wide), BF16)] * chips
        + [((tokens, wide), BF16)] * 2
        + [((tokens, wide), F32)],
    )
    parts = [parts[0]] + [swap_chips(parts[k], k) for k in range(1, chips)]
    parts, near, far = lax.optimization_barrier((parts, near, far))
    near = shift_chips(near, -1)
    far = shift_chips(far, -2)
    pieces = local_call(
        functools.partial(sum_kernel, chips),
        "sum_chips",
        parts,
        [((block, wide), BF16)] * groups,
        [pltpu.VMEM((share, wide), F32)],
    )
    pieces = [pieces[0]] + [swap_heads(pieces[k], k) for k in range(1, groups)]
    grad_k_prompt, grad_v_prompt, grad_k_resp, grad_v_resp = local_call(
        finish_kernel,
        "finish",
        [own, near, far] + pieces,
        [(prompt_k.shape, BF16)] * 2 + [((tokens, kv_cols), BF16)] * 2,
    )
    return (resp_out, grad_q, grad_k_resp, grad_v_resp, grad_k_prompt, grad_v_prompt)


def solution(mesh):
    placed = (
        P(("seq", "head"), None),
        P(("seq", "head"), None),
        P("seq", "head"),
        P("seq", "head"),
        P("seq", "head"),
        P("seq", "head"),
        P(),
    )
    return jax.shard_map(
        shards,
        mesh=mesh,
        in_specs=placed,
        out_specs=(
            P("seq", "head"),
            P("seq", "head"),
            P("seq", "head"),
            P("seq", "head"),
            P(("seq", "head"), None),
            P(("seq", "head"), None),
        ),
        check_vma=False,
    )
```

```python
import functools
import math

import jax
import jax.numpy as jnp
from jax import lax
from jax.experimental import pallas as pl
from jax.experimental.pallas import tpu as pltpu
from jax.sharding import PartitionSpec as P

HD = 128
CORES = 2
FAR = 4
TILE = 128
MOST_HEADS = 2
MOST_SCORES = 4 * 2560 * 256
NEG = -1e30
BF16 = jnp.bfloat16
F32 = jnp.float32


def dot(a, b):
    return jnp.dot(a, b, preferred_element_type=F32)


def whole(count):
    return [pl.BlockSpec(memory_space=pltpu.VMEM)] * count


def local_call(kernel, name, inputs, outputs, scratch=()):
    return pl.pallas_call(
        kernel,
        in_specs=whole(len(inputs)),
        out_specs=whole(len(outputs)),
        out_shape=[jax.ShapeDtypeStruct(shape, kind) for shape, kind in outputs],
        scratch_shapes=list(scratch),
        compiler_params=pltpu.CompilerParams(vmem_limit_bytes=40 * 1024 * 1024),
        name=name,
    )(*inputs)


def pack_kernel(pk_ref, pv_ref, rk_ref, rv_ref, *outs):
    pieces, resp = outs[:-1], outs[-1]
    head = lax.axis_index("head")
    width = pieces[0].shape[1]
    for k, piece in enumerate(pieces):
        start = pl.multiple_of((head ^ k) * (width // 2), HD)
        for n in range(width // (2 * HD)):
            at = pl.multiple_of(start + n * HD, HD)
            piece[:, 2 * n * HD : (2 * n + 1) * HD] = pk_ref[:, pl.ds(at, HD)]
            piece[:, (2 * n + 1) * HD : (2 * n + 2) * HD] = pv_ref[:, pl.ds(at, HD)]
    for n in range(width // (2 * HD)):
        resp[:, 2 * n * HD : (2 * n + 1) * HD] = rk_ref[:, n * HD : (n + 1) * HD]
        resp[:, (2 * n + 1) * HD : (2 * n + 2) * HD] = rv_ref[:, n * HD : (n + 1) * HD]


def pack(inputs, groups):
    def one(array):
        return pl.BlockSpec(array.shape, lambda i: (0, 0))

    block, tokens = inputs[0].shape[0], inputs[2].shape[0]
    wide = 2 * inputs[2].shape[1]
    shapes = [(block, wide)] * groups + [(tokens, wide)]
    return pl.pallas_call(
        pack_kernel,
        grid=(1,),
        in_specs=[one(array) for array in inputs],
        out_specs=whole(groups + 1),
        out_shape=[jax.ShapeDtypeStruct(shape, BF16) for shape in shapes],
        compiler_params=pltpu.CompilerParams(vmem_limit_bytes=56 * 1024 * 1024),
        name="pack",
    )(*inputs)


def merge_kernel(parts, rows, kept_ref, got_ref, *outs):
    pieces, back1, back2, own = outs[:parts], outs[parts], outs[parts + 1], outs[parts + 2]
    core = lax.rem(lax.axis_index("seq"), CORES)
    to_own = jnp.where(core == 0, 1.0, 0.0)
    half = kept_ref.shape[0] - 3 * rows
    share = half // parts
    for k, piece in enumerate(pieces):
        at = slice(k * share, (k + 1) * share)
        piece[...] = (kept_ref[at] + got_ref[at].astype(F32)).astype(BF16)
    one, two, three = half + rows, half + 2 * rows, half + 3 * rows
    back1[...] = (kept_ref[half:one] + got_ref[half:one].astype(F32)).astype(BF16)
    chosen = got_ref[one:two].astype(F32)
    back2[...] = (kept_ref[one:two] + chosen * (1.0 - to_own)).astype(BF16)
    own[...] = kept_ref[two:three] + chosen * to_own


def sum_kernel(parts, *refs):
    ins, outs, total = refs[:parts], refs[parts:-1], refs[-1]
    acc = ins[0][...].astype(F32)
    for ref in ins[1:]:
        acc = acc + ref[...].astype(F32)
    total[...] = acc
    share = total.shape[0] // len(outs)
    for k, out in enumerate(outs):
        out[...] = total[k * share : (k + 1) * share].astype(BF16)


def finish_kernel(own_ref, one_ref, two_ref, *refs):
    pieces, (gk_ref, gv_ref, rk_ref, rv_ref) = refs[:-4], refs[-4:]
    head = lax.axis_index("head")
    width = pieces[0].shape[1]
    for k, piece in enumerate(pieces):
        start = pl.multiple_of((head ^ k) * (width // 2), HD)
        for n in range(width // (2 * HD)):
            at = pl.multiple_of(start + n * HD, HD)
            gk_ref[:, pl.ds(at, HD)] = piece[:, 2 * n * HD : (2 * n + 1) * HD]
            gv_ref[:, pl.ds(at, HD)] = piece[:, (2 * n + 1) * HD : (2 * n + 2) * HD]
    total = (own_ref[...] + one_ref[...].astype(F32) + two_ref[...].astype(F32)).astype(BF16)
    for n in range(width // (2 * HD)):
        rk_ref[:, n * HD : (n + 1) * HD] = total[:, 2 * n * HD : (2 * n + 1) * HD]
        rv_ref[:, n * HD : (n + 1) * HD] = total[:, (2 * n + 1) * HD : (2 * n + 2) * HD]


def attention_kernel(
    tokens, lengths, q_ref, do_ref, sent_ref, got_ref, own_ref, far_ref,
    o_ref, dq_ref, kept_ref, back_ref,
    bias, keys, values, keys_t, values_t, q_t, cot_t, q_all, cot_all,
    s_buf, g_buf, p_buf, d_buf, dk, dv,
):
    total_keys = keys.shape[0]
    heads = q_ref.shape[1] // HD
    prompt_len = total_keys - 5 * tokens
    half = prompt_len // 2
    head = pl.program_id(0)
    step = pl.program_id(1)
    last = pl.num_programs(1) - 1
    score_scale = 1.0 / math.sqrt(HD)
    exp_scale = score_scale * math.log2(math.e)
    k_cols = pl.ds(pl.multiple_of(head * 2 * HD, HD), HD)
    v_cols = pl.ds(pl.multiple_of(head * 2 * HD + HD, HD), HD)
    resp_at = [prompt_len + i * tokens for i in range(6)]
    tiles = [slice(at, at + TILE) for at in range(0, total_keys, TILE)]

    @pl.when((step == 0) & (head == 0))
    def _():
        place = lax.axis_index("seq")
        core = lax.rem(place, CORES)
        first_row = place * tokens
        row_pos = first_row + lax.broadcasted_iota(jnp.int32, (tokens, tokens), 1)
        seg_start = jnp.zeros((tokens, tokens), jnp.int32)
        end = jnp.int32(0)
        for i in range(lengths.shape[0]):
            end = end + lengths[i]
            seg_start = jnp.where(row_pos >= end, end, seg_start)
        near = 1 + 2 * core
        for i, distance in enumerate((0, 2, FAR, near, 4 - near)):
            key_pos = (first_row - distance * tokens) + lax.broadcasted_iota(
                jnp.int32, (tokens, tokens), 0
            )
            allowed = (key_pos >= seg_start) & (key_pos <= row_pos)
            bias[i * tokens : (i + 1) * tokens] = jnp.where(allowed, 0.0, NEG)

    @pl.when(step == 0)
    def _():
        dk[...] = jnp.zeros_like(dk)
        dv[...] = jnp.zeros_like(dv)
        for ref, start, size, at in (
            (sent_ref, 0, half, 0),
            (got_ref, 0, half, half),
            (own_ref, 0, tokens, resp_at[0]),
            (sent_ref, half, tokens, resp_at[1]),
            (far_ref, 0, tokens, resp_at[2]),
            (got_ref, half, tokens, resp_at[3]),
            (got_ref, half + tokens, tokens, resp_at[4]),
        ):
            k_rows = ref[start : start + size, k_cols]
            v_rows = ref[start : start + size, v_cols]
            keys[at : at + size] = k_rows
            values[at : at + size] = v_rows
            keys_t[:, at : at + size] = k_rows.T
            values_t[:, at : at + size] = v_rows.T

    def lanes(h):
        return slice(h * tokens, (h + 1) * tokens)

    def cols(h):
        return slice(h * HD, (h + 1) * HD)

    for h in range(heads):
        q_t[:, lanes(h)] = q_ref[:, cols(h)].T
        cot_t[:, lanes(h)] = do_ref[:, cols(h)].T
    s_buf[...] = dot(keys[...], q_t[...])
    g_buf[...] = dot(values[...], cot_t[...])

    def scores(at, h):
        s = s_buf[at, lanes(h)]
        if at.start >= prompt_len:
            s = s + bias[at.start - prompt_len : at.stop - prompt_len]
        return s

    totals = []
    for h in range(heads):
        top = None
        for at in tiles:
            part = jnp.max(scores(at, h).reshape(TILE // 8, 8, tokens), axis=0)
            top = part if top is None else jnp.maximum(top, part)
        top = jnp.max(top, axis=0, keepdims=True) * exp_scale
        total = None
        for at in tiles:
            p = jnp.exp2(scores(at, h) * exp_scale - top)
            part = jnp.sum(p.reshape(TILE // 8, 8, tokens), axis=0)
            total = part if total is None else total + part
            p_buf[at, lanes(h)] = p.astype(BF16)
        totals.append(total)
    out_t = dot(values_t[...], p_buf[...])
    inverses = []
    for h in range(heads):
        inverse = 1.0 / jnp.sum(totals[h], axis=0, keepdims=True)
        inverses.append(inverse)
        out = (out_t[:, lanes(h)] * inverse).astype(BF16)
        o_ref[:, cols(h)] = out.T
        wide = cot_t[:, lanes(h)].astype(F32)
        delta = jnp.sum(wide * out.astype(F32), axis=0, keepdims=True)
        cot_all[lanes(h)] = (wide * inverse).astype(BF16).T
        q_all[lanes(h)] = (q_t[:, lanes(h)].astype(F32) * inverse).astype(BF16).T
        for at in tiles:
            p = p_buf[at, lanes(h)].astype(F32)
            d_buf[at, lanes(h)] = (p * (g_buf[at, lanes(h)] - delta)).astype(BF16)
    dv[...] += dot(p_buf[...], cot_all[...])
    dk[...] += dot(d_buf[...], q_all[...])
    dq_t = dot(keys_t[...], d_buf[...])
    for h in range(heads):
        dq = (dq_t[:, lanes(h)] * (inverses[h] * score_scale)).astype(BF16)
        dq_ref[:, cols(h)] = dq.T

    @pl.when(step == last)
    def _():
        for ref, start, size, at in (
            (kept_ref, 0, half, 0),
            (back_ref, 0, half, half),
            (kept_ref, half + 2 * tokens, tokens, resp_at[0]),
            (kept_ref, half, tokens, resp_at[1]),
            (kept_ref, half + tokens, tokens, resp_at[2]),
            (back_ref, half, tokens, resp_at[3]),
            (back_ref, half + tokens, tokens, resp_at[4]),
        ):
            ref[start : start + size, k_cols] = (dk[at : at + size] * score_scale).astype(ref.dtype)
            ref[start : start + size, v_cols] = dv[at : at + size].astype(ref.dtype)


def attention(lengths, resp_q, grad_out, sent, got, own, far):
    tokens = resp_q.shape[0]
    half = sent.shape[0] - 2 * tokens
    total_keys = 2 * half + 5 * tokens
    kv_heads = sent.shape[1] // (2 * HD)
    q_heads = resp_q.shape[1] // HD
    heads = 1
    while heads < MOST_HEADS and 2 * heads * total_keys * tokens <= MOST_SCORES:
        heads = 2 * heads
    steps = q_heads // kv_heads // heads
    lanes = heads * tokens
    head_spec = pl.BlockSpec((tokens, heads * HD), lambda n, g: (0, n * steps + g))
    pairs = tokens * q_heads * total_keys
    return pl.pallas_call(
        functools.partial(attention_kernel, tokens),
        grid=(kv_heads, steps),
        in_specs=[pl.BlockSpec(memory_space=pltpu.SMEM), head_spec, head_spec] + whole(4),
        out_specs=[head_spec, head_spec] + whole(2),
        out_shape=[
            jax.ShapeDtypeStruct(resp_q.shape, BF16),
            jax.ShapeDtypeStruct(resp_q.shape, BF16),
            jax.ShapeDtypeStruct((half + 3 * tokens, sent.shape[1]), F32),
            jax.ShapeDtypeStruct((half + 2 * tokens, sent.shape[1]), BF16),
        ],
        scratch_shapes=[
            pltpu.VMEM((5 * tokens, tokens), F32),
            pltpu.VMEM((total_keys, HD), BF16),
            pltpu.VMEM((total_keys, HD), BF16),
            pltpu.VMEM((HD, total_keys), BF16),
            pltpu.VMEM((HD, total_keys), BF16),
            pltpu.VMEM((HD, lanes), BF16),
            pltpu.VMEM((HD, lanes), BF16),
            pltpu.VMEM((lanes, HD), BF16),
            pltpu.VMEM((lanes, HD), BF16),
            pltpu.VMEM((total_keys, lanes), F32),
            pltpu.VMEM((total_keys, lanes), F32),
            pltpu.VMEM((total_keys, lanes), BF16),
            pltpu.VMEM((total_keys, lanes), BF16),
            pltpu.VMEM((total_keys, HD), F32),
            pltpu.VMEM((total_keys, HD), F32),
        ],
        compiler_params=pltpu.CompilerParams(vmem_limit_bytes=50 * 1024 * 1024),
        cost_estimate=pl.CostEstimate(
            flops=12 * HD * pairs, bytes_accessed=8 * resp_q.size, transcendentals=pairs
        ),
        name="attention",
    )(lengths, resp_q, grad_out, sent, got, own, far)


def swap_heads(array, by):
    devices = lax.axis_size("head")
    return lax.ppermute(array, "head", [(i, i ^ by) for i in range(devices)])


def swap_chips(array, by):
    devices = lax.axis_size("seq")
    return lax.ppermute(array, "seq", [(i, i ^ (by * CORES)) for i in range(devices)])


def swap_cores(array):
    devices = lax.axis_size("seq")
    return lax.ppermute(array, "seq", [(i, i ^ 1) for i in range(devices)])


def shift_chips(array, by):
    devices = lax.axis_size("seq")
    by = by * CORES
    return lax.ppermute(array, "seq", [(i, i + by) for i in range(devices) if 0 <= i + by < devices])


def shards(prompt_k, prompt_v, resp_q, resp_k, resp_v, grad_out, resp_lengths):
    tokens, kv_cols = resp_k.shape
    wide = 2 * kv_cols
    groups = lax.axis_size("head")
    chips = lax.axis_size("seq") // CORES
    block = prompt_k.shape[0]
    core = lax.rem(lax.axis_index("seq"), CORES)

    *pieces, own = pack([prompt_k, prompt_v, resp_k, resp_v], groups)
    pieces = [pieces[0]] + [swap_heads(pieces[k], k) for k in range(1, groups)]
    near = shift_chips(own, 1)
    far = shift_chips(own, 2)
    pieces, near, far = lax.optimization_barrier((pieces, near, far))
    mine = jnp.concatenate(pieces, axis=0)
    parts = [mine] + [swap_chips(mine, k) for k in range(1, chips)]
    chosen = jnp.where(core == 1, far, own)
    sent = jnp.concatenate(parts + [near, chosen], axis=0)
    got = swap_cores(sent)

    resp_out, grad_q, kept, back = attention(
        resp_lengths, resp_q, grad_out, sent, got, own, far
    )

    back = swap_cores(back)
    share = groups * block
    *parts, near, far, own = local_call(
        functools.partial(merge_kernel, chips, tokens),
        "merge",
        [kept, back],
        [((share, wide), BF16)] * chips
        + [((tokens, wide), BF16)] * 2
        + [((tokens, wide), F32)],
    )
    parts = [parts[0]] + [swap_chips(parts[k], k) for k in range(1, chips)]
    parts, near, far = lax.optimization_barrier((parts, near, far))
    near = shift_chips(near, -1)
    far = shift_chips(far, -2)
    pieces = local_call(
        functools.partial(sum_kernel, chips),
        "sum_chips",
        parts,
        [((block, wide), BF16)] * groups,
        [pltpu.VMEM((share, wide), F32)],
    )
    pieces = [pieces[0]] + [swap_heads(pieces[k], k) for k in range(1, groups)]
    grad_k_prompt, grad_v_prompt, grad_k_resp, grad_v_resp = local_call(
        finish_kernel,
        "finish",
        [own, near, far] + pieces,
        [(prompt_k.shape, BF16)] * 2 + [((tokens, kv_cols), BF16)] * 2,
    )
    return (resp_out, grad_q, grad_k_resp, grad_v_resp, grad_k_prompt, grad_v_prompt)


def solution(mesh):
    placed = (
        P(("seq", "head"), None),
        P(("seq", "head"), None),
        P("seq", "head"),
        P("seq", "head"),
        P("seq", "head"),
        P("seq", "head"),
        P(),
    )
    return jax.shard_map(
        shards,
        mesh=mesh,
        in_specs=placed,
        out_specs=(
            P("seq", "head"),
            P("seq", "head"),
            P("seq", "head"),
            P("seq", "head"),
            P(("seq", "head"), None),
            P(("seq", "head"), None),
        ),
        check_vma=False,
    )
```

```python
import functools
import math

import jax
import jax.numpy as jnp
from jax import lax
from jax.experimental import pallas as pl
from jax.experimental.pallas import tpu as pltpu
from jax.sharding import PartitionSpec as P

HD = 128
CORES = 2
FAR = 4
CHUNK = 256
ROWS = 64
MOST_SCORES = 2560 * 256
NEG = -1e30
NT = (((1,), (1,)), ((), ()))
BF16 = jnp.bfloat16
F32 = jnp.float32


def dot(a, b):
    return jnp.dot(a, b, preferred_element_type=F32)


def dot_nt(a, b):
    return lax.dot_general(a, b, NT, preferred_element_type=F32)


def whole(count):
    return [pl.BlockSpec(memory_space=pltpu.VMEM)] * count


def local_call(kernel, name, inputs, outputs, scratch=()):
    return pl.pallas_call(
        kernel,
        in_specs=whole(len(inputs)),
        out_specs=whole(len(outputs)),
        out_shape=[jax.ShapeDtypeStruct(shape, kind) for shape, kind in outputs],
        scratch_shapes=list(scratch),
        compiler_params=pltpu.CompilerParams(vmem_limit_bytes=40 * 1024 * 1024),
        name=name,
    )(*inputs)


def pack_kernel(pk_ref, pv_ref, rk_ref, rv_ref, *outs):
    pieces, resp = outs[:-1], outs[-1]
    head = lax.axis_index("head")
    width = pieces[0].shape[1]
    for k, piece in enumerate(pieces):
        start = pl.multiple_of((head ^ k) * (width // 2), HD)
        for n in range(width // (2 * HD)):
            at = pl.multiple_of(start + n * HD, HD)
            piece[:, 2 * n * HD : (2 * n + 1) * HD] = pk_ref[:, pl.ds(at, HD)]
            piece[:, (2 * n + 1) * HD : (2 * n + 2) * HD] = pv_ref[:, pl.ds(at, HD)]
    for n in range(width // (2 * HD)):
        resp[:, 2 * n * HD : (2 * n + 1) * HD] = rk_ref[:, n * HD : (n + 1) * HD]
        resp[:, (2 * n + 1) * HD : (2 * n + 2) * HD] = rv_ref[:, n * HD : (n + 1) * HD]


def pack(inputs, groups):
    def one(array):
        return pl.BlockSpec(array.shape, lambda i: (0, 0))

    block, tokens = inputs[0].shape[0], inputs[2].shape[0]
    wide = 2 * inputs[2].shape[1]
    shapes = [(block, wide)] * groups + [(tokens, wide)]
    return pl.pallas_call(
        pack_kernel,
        grid=(1,),
        in_specs=[one(array) for array in inputs],
        out_specs=whole(groups + 1),
        out_shape=[jax.ShapeDtypeStruct(shape, BF16) for shape in shapes],
        compiler_params=pltpu.CompilerParams(vmem_limit_bytes=56 * 1024 * 1024),
        name="pack",
    )(*inputs)


def merge_kernel(parts, rows, kept_ref, got_ref, *outs):
    pieces, back1, back2, own = outs[:parts], outs[parts], outs[parts + 1], outs[parts + 2]
    core = lax.rem(lax.axis_index("seq"), CORES)
    to_own = jnp.where(core == 0, 1.0, 0.0)
    half = kept_ref.shape[0] - 3 * rows
    share = half // parts
    for k, piece in enumerate(pieces):
        at = slice(k * share, (k + 1) * share)
        piece[...] = (kept_ref[at] + got_ref[at].astype(F32)).astype(BF16)
    one, two, three = half + rows, half + 2 * rows, half + 3 * rows
    back1[...] = (kept_ref[half:one] + got_ref[half:one].astype(F32)).astype(BF16)
    chosen = got_ref[one:two].astype(F32)
    back2[...] = (kept_ref[one:two] + chosen * (1.0 - to_own)).astype(BF16)
    own[...] = kept_ref[two:three] + chosen * to_own


def sum_kernel(parts, *refs):
    ins, outs, total = refs[:parts], refs[parts:-1], refs[-1]
    acc = ins[0][...].astype(F32)
    for ref in ins[1:]:
        acc = acc + ref[...].astype(F32)
    total[...] = acc
    share = total.shape[0] // len(outs)
    for k, out in enumerate(outs):
        out[...] = total[k * share : (k + 1) * share].astype(BF16)


def finish_kernel(own_ref, one_ref, two_ref, *refs):
    pieces, (gk_ref, gv_ref, rk_ref, rv_ref) = refs[:-4], refs[-4:]
    head = lax.axis_index("head")
    width = pieces[0].shape[1]
    for k, piece in enumerate(pieces):
        start = pl.multiple_of((head ^ k) * (width // 2), HD)
        for n in range(width // (2 * HD)):
            at = pl.multiple_of(start + n * HD, HD)
            gk_ref[:, pl.ds(at, HD)] = piece[:, 2 * n * HD : (2 * n + 1) * HD]
            gv_ref[:, pl.ds(at, HD)] = piece[:, (2 * n + 1) * HD : (2 * n + 2) * HD]
    total = (own_ref[...] + one_ref[...].astype(F32) + two_ref[...].astype(F32)).astype(BF16)
    for n in range(width // (2 * HD)):
        rk_ref[:, n * HD : (n + 1) * HD] = total[:, 2 * n * HD : (2 * n + 1) * HD]
        rv_ref[:, n * HD : (n + 1) * HD] = total[:, (2 * n + 1) * HD : (2 * n + 2) * HD]


def attention_kernel(
    tokens, halves, steps_per_kv,
    lengths, q_ref, next_q_ref, do_ref, next_do_ref, sent_ref, got_ref, own_ref, far_ref,
    o_ref, dq_ref, kept_ref, back_ref,
    bias, keys, values, s_bufs, g_bufs, p_bufs, d_bufs, inv_bufs, scaled, q_ts, cot_ts, dk_t, dv_t,
):
    kv_heads, total_keys = keys.shape[0], keys.shape[1]
    rows = tokens // halves
    prompt_len = total_keys - 5 * tokens
    half = prompt_len // 2
    step = pl.program_id(0)
    last = pl.num_programs(0) - 1
    score_scale = 1.0 / math.sqrt(HD)
    exp_scale = score_scale * math.log2(math.e)
    resp_at = [prompt_len + i * tokens for i in range(6)]
    chunks = [slice(at, at + CHUNK) for at in range(0, total_keys, CHUNK)]

    def unit(ref, which):
        if halves == 1:
            return ref[:, which * HD : (which + 1) * HD]
        return ref[which * rows : (which + 1) * rows, :HD]

    def kv_of(at_step):
        return jnp.clip(at_step // steps_per_kv, 0, kv_heads - 1)

    def ahead(which, kv, q, cot):
        def scores(at):
            s_bufs[which, :, at] = dot_nt(q, keys[kv, at])

        def grads(at):
            g_bufs[which, :, at] = dot_nt(cot, values[kv, at])

        return [functools.partial(f, at) for at in chunks for f in (scores, grads)]

    def behind(which, kv, at_step):
        head = jnp.maximum(at_step, 0) * (2 // halves) + (which if halves == 1 else 0)
        cols = pl.ds(pl.multiple_of(head * HD, HD), HD)
        rows_at = slice(0, rows) if halves == 1 else slice(which * rows, (which + 1) * rows)

        def output():
            out = dot(p_bufs[which], values[kv])
            o_ref[rows_at, cols] = (out * inv_bufs[which]).astype(BF16)

        def query():
            dq = dot(d_bufs[which], keys[kv])
            dq_ref[rows_at, cols] = (dq * (inv_bufs[which] * score_scale)).astype(BF16)

        def value_grad(at):
            dv_t[kv, :, at] += dot(cot_ts[which], p_bufs[which, :, at])

        def key_grad(at):
            dk_t[kv, :, at] += dot(q_ts[which], d_bufs[which, :, at])

        work = [functools.partial(f, at) for at in chunks for f in (value_grad, key_grad)]
        return [output] + work[: len(work) // 2] + [query] + work[len(work) // 2 :]

    def weigh(which, q, cot):
        work = []

        def scores(r, at):
            s = s_bufs[which, r, at]
            if at.start >= prompt_len:
                row = which * rows * (halves - 1)
                s = s + bias[r.start + row : r.stop + row, at.start - prompt_len : at.stop - prompt_len]
            return s

        def parts(x):
            return [x[:, col : col + HD] for col in range(0, CHUNK, HD)]

        for start in range(0, rows, ROWS):
            r = slice(start, start + ROWS)
            state = {}

            def highest(at, r=r, state=state):
                top = functools.reduce(jnp.maximum, parts(scores(r, at)))
                state["top"] = jnp.maximum(state["top"], top) if "top" in state else top

            def settle(r=r, state=state):
                state["top"] = jnp.max(state["top"], axis=1, keepdims=True) * exp_scale
                state["sum"] = jnp.zeros((ROWS, HD), F32)
                state["dot"] = jnp.zeros((ROWS, HD), F32)

            def weights(at, r=r, state=state):
                p = jnp.exp2(scores(r, at) * exp_scale - state["top"])
                for part in parts(p):
                    state["sum"] = state["sum"] + part
                for part in parts(p * g_bufs[which, r, at]):
                    state["dot"] = state["dot"] + part
                p_bufs[which, r, at] = p.astype(BF16)

            def finish(r=r, state=state):
                inverse = 1.0 / jnp.sum(state["sum"], axis=1, keepdims=True)
                state["delta"] = jnp.sum(state["dot"], axis=1, keepdims=True) * inverse
                inv_bufs[which, r] = jnp.broadcast_to(inverse, (ROWS, HD))
                scaled[0, r] = (q[r].astype(F32) * inverse).astype(BF16)
                scaled[1, r] = (cot[r].astype(F32) * inverse).astype(BF16)

            def slopes(at, r=r, state=state):
                p = p_bufs[which, r, at].astype(F32)
                d_bufs[which, r, at] = (p * (g_bufs[which, r, at] - state["delta"])).astype(BF16)

            work += [functools.partial(highest, at) for at in chunks] + [settle]
            work += [functools.partial(weights, at) for at in chunks] + [finish]
            work += [functools.partial(slopes, at) for at in chunks]

        def turn():
            q_ts[which] = scaled[0].T
            cot_ts[which] = scaled[1].T

        return work + [turn]

    def together(vector, matrix):
        done = 0
        for i, work in enumerate(vector):
            work()
            while done * len(vector) < (i + 1) * len(matrix):
                matrix[done]()
                done += 1

    def mixed(first, second):
        return [work for pair in zip(first, second) for work in pair] + (
            first[len(second) :] + second[len(first) :]
        )

    @pl.when(step == 0)
    def _():
        place = lax.axis_index("seq")
        core = lax.rem(place, CORES)
        first_row = place * tokens
        row_pos = first_row + lax.broadcasted_iota(jnp.int32, (tokens, HD), 0)
        seg_start = jnp.zeros((tokens, HD), jnp.int32)
        end = jnp.int32(0)
        for i in range(lengths.shape[0]):
            end = end + lengths[i]
            seg_start = jnp.where(row_pos >= end, end, seg_start)
        near = 1 + 2 * core
        for i, distance in enumerate((0, 2, FAR, near, 4 - near)):
            for col in range(0, tokens, HD):
                key_pos = (first_row - distance * tokens + col) + lax.broadcasted_iota(
                    jnp.int32, (tokens, HD), 1
                )
                allowed = (key_pos >= seg_start) & (key_pos <= row_pos)
                at = i * tokens + col
                bias[:, at : at + HD] = jnp.where(allowed, 0.0, NEG)
        for n in range(kv_heads):
            k_at, v_at = 2 * n * HD, (2 * n + 1) * HD
            for ref, start, size, at in (
                (sent_ref, 0, half, 0),
                (got_ref, 0, half, half),
                (own_ref, 0, tokens, resp_at[0]),
                (sent_ref, half, tokens, resp_at[1]),
                (far_ref, 0, tokens, resp_at[2]),
                (got_ref, half, tokens, resp_at[3]),
                (got_ref, half + tokens, tokens, resp_at[4]),
            ):
                keys[n, at : at + size] = ref[start : start + size, k_at : k_at + HD]
                values[n, at : at + size] = ref[start : start + size, v_at : v_at + HD]
        dk_t[...] = jnp.zeros_like(dk_t)
        dv_t[...] = jnp.zeros_like(dv_t)
        for ref in (p_bufs, d_bufs, inv_bufs, q_ts, cot_ts):
            ref[1] = jnp.zeros(ref.shape[1:], ref.dtype)
        for work in ahead(0, 0, unit(q_ref, 0), unit(do_ref, 0)):
            work()

    @pl.when(step < last)
    def _():
        kv = kv_of(step)
        together(
            weigh(0, unit(q_ref, 0), unit(do_ref, 0)),
            mixed(
                behind(1, kv_of(step - 1), step - 1),
                ahead(1, kv, unit(q_ref, 1), unit(do_ref, 1)),
            ),
        )
        together(
            weigh(1, unit(q_ref, 1), unit(do_ref, 1)),
            mixed(
                behind(0, kv, step),
                ahead(0, kv_of(step + 1), unit(next_q_ref, 0), unit(next_do_ref, 0)),
            ),
        )

    @pl.when(step == last)
    def _():
        for work in behind(1, kv_of(step - 1), step - 1):
            work()
        for n in range(kv_heads):
            k_cols = slice(2 * n * HD, (2 * n + 1) * HD)
            v_cols = slice((2 * n + 1) * HD, (2 * n + 2) * HD)
            for ref, start, size, at in (
                (kept_ref, 0, half, 0),
                (back_ref, 0, half, half),
                (kept_ref, half + 2 * tokens, tokens, resp_at[0]),
                (kept_ref, half, tokens, resp_at[1]),
                (kept_ref, half + tokens, tokens, resp_at[2]),
                (back_ref, half, tokens, resp_at[3]),
                (back_ref, half + tokens, tokens, resp_at[4]),
            ):
                grad_k = (dk_t[n, :, at : at + size] * score_scale).T
                ref[start : start + size, k_cols] = grad_k.astype(ref.dtype)
                grad_v = dv_t[n, :, at : at + size].T
                ref[start : start + size, v_cols] = grad_v.astype(ref.dtype)


def attention(lengths, resp_q, grad_out, sent, got, own, far):
    tokens = resp_q.shape[0]
    half = sent.shape[0] - 2 * tokens
    total_keys = 2 * half + 5 * tokens
    kv_heads = sent.shape[1] // (2 * HD)
    q_heads = resp_q.shape[1] // HD
    halves = 1 if tokens * total_keys <= MOST_SCORES else 2
    rows = tokens // halves
    steps = q_heads * halves // 2
    width = 2 // halves * HD

    def block(later):
        return pl.BlockSpec((tokens, width), lambda i: (0, jnp.minimum(i + later, steps - 1)))

    pairs = tokens * q_heads * total_keys
    return pl.pallas_call(
        functools.partial(attention_kernel, tokens, halves, steps // kv_heads),
        grid=(steps + 1,),
        in_specs=[pl.BlockSpec(memory_space=pltpu.SMEM), block(0), block(1), block(0), block(1)]
        + whole(4),
        out_specs=whole(4),
        out_shape=[
            jax.ShapeDtypeStruct(resp_q.shape, BF16),
            jax.ShapeDtypeStruct(resp_q.shape, BF16),
            jax.ShapeDtypeStruct((half + 3 * tokens, sent.shape[1]), F32),
            jax.ShapeDtypeStruct((half + 2 * tokens, sent.shape[1]), BF16),
        ],
        scratch_shapes=[
            pltpu.VMEM((tokens, 5 * tokens), F32),
            pltpu.VMEM((kv_heads, total_keys, HD), BF16),
            pltpu.VMEM((kv_heads, total_keys, HD), BF16),
            pltpu.VMEM((2, rows, total_keys), F32),
            pltpu.VMEM((2, rows, total_keys), F32),
            pltpu.VMEM((2, rows, total_keys), BF16),
            pltpu.VMEM((2, rows, total_keys), BF16),
            pltpu.VMEM((2, rows, HD), F32),
            pltpu.VMEM((2, rows, HD), BF16),
            pltpu.VMEM((2, HD, rows), BF16),
            pltpu.VMEM((2, HD, rows), BF16),
            pltpu.VMEM((kv_heads, HD, total_keys), F32),
            pltpu.VMEM((kv_heads, HD, total_keys), F32),
        ],
        compiler_params=pltpu.CompilerParams(vmem_limit_bytes=40 * 1024 * 1024),
        cost_estimate=pl.CostEstimate(
            flops=12 * HD * pairs, bytes_accessed=8 * resp_q.size, transcendentals=pairs
        ),
        name="attention",
    )(lengths, resp_q, resp_q, grad_out, grad_out, sent, got, own, far)


def swap_heads(array, by):
    devices = lax.axis_size("head")
    return lax.ppermute(array, "head", [(i, i ^ by) for i in range(devices)])


def swap_chips(array, by):
    devices = lax.axis_size("seq")
    return lax.ppermute(array, "seq", [(i, i ^ (by * CORES)) for i in range(devices)])


def swap_cores(array):
    devices = lax.axis_size("seq")
    return lax.ppermute(array, "seq", [(i, i ^ 1) for i in range(devices)])


def shift_chips(array, by):
    devices = lax.axis_size("seq")
    by = by * CORES
    return lax.ppermute(array, "seq", [(i, i + by) for i in range(devices) if 0 <= i + by < devices])


def shards(prompt_k, prompt_v, resp_q, resp_k, resp_v, grad_out, resp_lengths):
    tokens, kv_cols = resp_k.shape
    wide = 2 * kv_cols
    groups = lax.axis_size("head")
    chips = lax.axis_size("seq") // CORES
    block = prompt_k.shape[0]
    core = lax.rem(lax.axis_index("seq"), CORES)

    *pieces, own = pack([prompt_k, prompt_v, resp_k, resp_v], groups)
    pieces = [pieces[0]] + [swap_heads(pieces[k], k) for k in range(1, groups)]
    near = shift_chips(own, 1)
    far = shift_chips(own, 2)
    pieces, near, far = lax.optimization_barrier((pieces, near, far))
    mine = jnp.concatenate(pieces, axis=0)
    parts = [mine] + [swap_chips(mine, k) for k in range(1, chips)]
    chosen = jnp.where(core == 1, far, own)
    sent = jnp.concatenate(parts + [near, chosen], axis=0)
    got = swap_cores(sent)

    resp_out, grad_q, kept, back = attention(
        resp_lengths, resp_q, grad_out, sent, got, own, far
    )

    back = swap_cores(back)
    share = groups * block
    *parts, near, far, own = local_call(
        functools.partial(merge_kernel, chips, tokens),
        "merge",
        [kept, back],
        [((share, wide), BF16)] * chips
        + [((tokens, wide), BF16)] * 2
        + [((tokens, wide), F32)],
    )
    parts = [parts[0]] + [swap_chips(parts[k], k) for k in range(1, chips)]
    parts, near, far = lax.optimization_barrier((parts, near, far))
    near = shift_chips(near, -1)
    far = shift_chips(far, -2)
    pieces = local_call(
        functools.partial(sum_kernel, chips),
        "sum_chips",
        parts,
        [((block, wide), BF16)] * groups,
        [pltpu.VMEM((share, wide), F32)],
    )
    pieces = [pieces[0]] + [swap_heads(pieces[k], k) for k in range(1, groups)]
    grad_k_prompt, grad_v_prompt, grad_k_resp, grad_v_resp = local_call(
        finish_kernel,
        "finish",
        [own, near, far] + pieces,
        [(prompt_k.shape, BF16)] * 2 + [((tokens, kv_cols), BF16)] * 2,
    )
    return (resp_out, grad_q, grad_k_resp, grad_v_resp, grad_k_prompt, grad_v_prompt)


def solution(mesh):
    placed = (
        P(("seq", "head"), None),
        P(("seq", "head"), None),
        P("seq", "head"),
        P("seq", "head"),
        P("seq", "head"),
        P("seq", "head"),
        P(),
    )
    return jax.shard_map(
        shards,
        mesh=mesh,
        in_specs=placed,
        out_specs=(
            P("seq", "head"),
            P("seq", "head"),
            P("seq", "head"),
            P("seq", "head"),
            P(("seq", "head"), None),
            P(("seq", "head"), None),
        ),
        check_vma=False,
    )
```

```python
import functools
import math

import jax
import jax.numpy as jnp
from jax import lax
from jax.experimental import pallas as pl
from jax.experimental.pallas import tpu as pltpu
from jax.sharding import PartitionSpec as P

HD = 128
CORES = 2
FAR = 4
CHUNK = 640
TILE = 64
MOST_SCORES = 2560 * 256
NEG = -1e30
BF16 = jnp.bfloat16
F32 = jnp.float32


def dot(a, b):
    return jnp.dot(a, b, preferred_element_type=F32)


def whole(count):
    return [pl.BlockSpec(memory_space=pltpu.VMEM)] * count


def local_call(kernel, name, inputs, outputs, scratch=()):
    return pl.pallas_call(
        kernel,
        in_specs=whole(len(inputs)),
        out_specs=whole(len(outputs)),
        out_shape=[jax.ShapeDtypeStruct(shape, kind) for shape, kind in outputs],
        scratch_shapes=list(scratch),
        compiler_params=pltpu.CompilerParams(vmem_limit_bytes=40 * 1024 * 1024),
        name=name,
    )(*inputs)


def pack_kernel(pk_ref, pv_ref, rk_ref, rv_ref, *outs):
    pieces, resp = outs[:-1], outs[-1]
    head = lax.axis_index("head")
    width = pieces[0].shape[1]
    for k, piece in enumerate(pieces):
        start = pl.multiple_of((head ^ k) * (width // 2), HD)
        for n in range(width // (2 * HD)):
            at = pl.multiple_of(start + n * HD, HD)
            piece[:, 2 * n * HD : (2 * n + 1) * HD] = pk_ref[:, pl.ds(at, HD)]
            piece[:, (2 * n + 1) * HD : (2 * n + 2) * HD] = pv_ref[:, pl.ds(at, HD)]
    for n in range(width // (2 * HD)):
        resp[:, 2 * n * HD : (2 * n + 1) * HD] = rk_ref[:, n * HD : (n + 1) * HD]
        resp[:, (2 * n + 1) * HD : (2 * n + 2) * HD] = rv_ref[:, n * HD : (n + 1) * HD]


def pack(inputs, groups):
    def one(array):
        return pl.BlockSpec(array.shape, lambda i: (0, 0))

    block, tokens = inputs[0].shape[0], inputs[2].shape[0]
    wide = 2 * inputs[2].shape[1]
    shapes = [(block, wide)] * groups + [(tokens, wide)]
    return pl.pallas_call(
        pack_kernel,
        grid=(1,),
        in_specs=[one(array) for array in inputs],
        out_specs=whole(groups + 1),
        out_shape=[jax.ShapeDtypeStruct(shape, BF16) for shape in shapes],
        compiler_params=pltpu.CompilerParams(vmem_limit_bytes=56 * 1024 * 1024),
        name="pack",
    )(*inputs)


def merge_kernel(parts, rows, kept_ref, got_ref, *outs):
    pieces, back1, back2, own = outs[:parts], outs[parts], outs[parts + 1], outs[parts + 2]
    core = lax.rem(lax.axis_index("seq"), CORES)
    to_own = jnp.where(core == 0, 1.0, 0.0)
    half = kept_ref.shape[0] - 3 * rows
    share = half // parts
    for k, piece in enumerate(pieces):
        at = slice(k * share, (k + 1) * share)
        piece[...] = (kept_ref[at] + got_ref[at].astype(F32)).astype(BF16)
    one, two, three = half + rows, half + 2 * rows, half + 3 * rows
    back1[...] = (kept_ref[half:one] + got_ref[half:one].astype(F32)).astype(BF16)
    chosen = got_ref[one:two].astype(F32)
    back2[...] = (kept_ref[one:two] + chosen * (1.0 - to_own)).astype(BF16)
    own[...] = kept_ref[two:three] + chosen * to_own


def sum_kernel(parts, *refs):
    ins, outs, total = refs[:parts], refs[parts:-1], refs[-1]
    acc = ins[0][...].astype(F32)
    for ref in ins[1:]:
        acc = acc + ref[...].astype(F32)
    total[...] = acc
    share = total.shape[0] // len(outs)
    for k, out in enumerate(outs):
        out[...] = total[k * share : (k + 1) * share].astype(BF16)


def finish_kernel(own_ref, one_ref, two_ref, *refs):
    pieces, (gk_ref, gv_ref, rk_ref, rv_ref) = refs[:-4], refs[-4:]
    head = lax.axis_index("head")
    width = pieces[0].shape[1]
    for k, piece in enumerate(pieces):
        start = pl.multiple_of((head ^ k) * (width // 2), HD)
        for n in range(width // (2 * HD)):
            at = pl.multiple_of(start + n * HD, HD)
            gk_ref[:, pl.ds(at, HD)] = piece[:, 2 * n * HD : (2 * n + 1) * HD]
            gv_ref[:, pl.ds(at, HD)] = piece[:, (2 * n + 1) * HD : (2 * n + 2) * HD]
    total = (own_ref[...] + one_ref[...].astype(F32) + two_ref[...].astype(F32)).astype(BF16)
    for n in range(width // (2 * HD)):
        rk_ref[:, n * HD : (n + 1) * HD] = total[:, 2 * n * HD : (2 * n + 1) * HD]
        rv_ref[:, n * HD : (n + 1) * HD] = total[:, (2 * n + 1) * HD : (2 * n + 2) * HD]


def attention_kernel(
    tokens, halves, steps_per_kv,
    lengths, q_ref, next_q_ref, do_ref, next_do_ref, sent_ref, got_ref, own_ref, far_ref,
    o_ref, dq_ref, kept_ref, back_ref,
    bias, keys, values, keys_t, values_t, s_bufs, g_bufs, p_bufs, d_bufs, inv_bufs,
    q_ts, cot_ts, q_ns, cot_ns, dk, dv,
):
    kv_heads, total_keys = keys.shape[0], keys.shape[1]
    rows = tokens // halves
    prompt_len = total_keys - 5 * tokens
    half = prompt_len // 2
    step = pl.program_id(0)
    last = pl.num_programs(0) - 1
    score_scale = 1.0 / math.sqrt(HD)
    exp_scale = score_scale * math.log2(math.e)
    resp_at = [prompt_len + i * tokens for i in range(6)]
    tiles = [slice(at, at + TILE) for at in range(0, total_keys, TILE)]
    chunks = [slice(at, at + CHUNK) for at in range(0, total_keys, CHUNK)]

    def unit(ref, which):
        if halves == 1:
            return ref[:, which * HD : (which + 1) * HD]
        return ref[which * rows : (which + 1) * rows, :HD]

    def kv_of(at_step):
        return jnp.clip(at_step // steps_per_kv, 0, kv_heads - 1)

    def ahead(which, kv, q_from, cot_from):
        def lift():
            q_ts[which] = unit(q_from, which).T
            cot_ts[which] = unit(cot_from, which).T

        def scores(at):
            s_bufs[which, at] = dot(keys[kv, at], q_ts[which])

        def grads(at):
            g_bufs[which, at] = dot(values[kv, at], cot_ts[which])

        return [lift] + [functools.partial(f, at) for at in chunks for f in (scores, grads)]

    def behind(which, kv, at_step):
        head = jnp.maximum(at_step, 0) * (2 // halves) + (which if halves == 1 else 0)
        cols = pl.ds(pl.multiple_of(head * HD, HD), HD)
        rows_at = slice(0, rows) if halves == 1 else slice(which * rows, (which + 1) * rows)
        cuts = [slice(at, at + total_keys // 2) for at in (0, total_keys // 2)]
        state = {}

        def output(at):
            more = dot(values_t[kv, :, at], p_bufs[which, at])
            state["out"] = state["out"] + more if "out" in state else more

        def query(at):
            more = dot(keys_t[kv, :, at], d_bufs[which, at])
            state["dq"] = state["dq"] + more if "dq" in state else more

        def put_output():
            o_ref[rows_at, cols] = (state["out"] * inv_bufs[which, :1]).astype(BF16).T

        def put_query():
            dq = state["dq"] * (inv_bufs[which, :1] * score_scale)
            dq_ref[rows_at, cols] = dq.astype(BF16).T

        def value_grad(at):
            dv[kv, at] += dot(p_bufs[which, at], cot_ns[which])

        def key_grad(at):
            dk[kv, at] += dot(d_bufs[which, at], q_ns[which])

        work = [functools.partial(f, at) for at in chunks for f in (value_grad, key_grad)]
        first = [functools.partial(output, at) for at in cuts] + [put_output]
        second = [functools.partial(query, at) for at in cuts] + [put_query]
        return first + work[: len(work) // 2] + second + work[len(work) // 2 :]

    def weigh(which):
        state = {}

        def scores(at):
            s = s_bufs[which, at]
            if at.start >= prompt_len:
                row = which * rows * (halves - 1)
                s = s + bias[at.start - prompt_len : at.stop - prompt_len, row : row + rows]
            return s

        def folded(x):
            return x.reshape(TILE // 8, 8, rows)

        def highest(at):
            top = jnp.max(folded(scores(at)), axis=0)
            state["top"] = jnp.maximum(state["top"], top) if "top" in state else top

        def settle():
            state["top"] = jnp.max(state["top"], axis=0, keepdims=True) * exp_scale
            state["sum"] = jnp.zeros((8, rows), F32)
            state["dot"] = jnp.zeros((8, rows), F32)

        def weights(at):
            p = jnp.exp2(scores(at) * exp_scale - state["top"])
            state["sum"] = state["sum"] + jnp.sum(folded(p), axis=0)
            state["dot"] = state["dot"] + jnp.sum(folded(p * g_bufs[which, at]), axis=0)
            p_bufs[which, at] = p.astype(BF16)

        def finish():
            inverse = 1.0 / jnp.sum(state["sum"], axis=0, keepdims=True)
            state["delta"] = jnp.sum(state["dot"], axis=0, keepdims=True) * inverse
            inv_bufs[which] = jnp.broadcast_to(inverse, (8, rows))
            q_ns[which] = (q_ts[which].astype(F32) * inverse).astype(BF16).T
            cot_ns[which] = (cot_ts[which].astype(F32) * inverse).astype(BF16).T

        def slopes(at):
            p = p_bufs[which, at].astype(F32)
            d_bufs[which, at] = (p * (g_bufs[which, at] - state["delta"])).astype(BF16)

        work = [functools.partial(highest, at) for at in tiles] + [settle]
        work += [functools.partial(weights, at) for at in tiles] + [finish]
        return work + [functools.partial(slopes, at) for at in tiles]

    def together(vector, matrix):
        done = 0
        for i, work in enumerate(vector):
            work()
            while done * len(vector) < (i + 1) * len(matrix):
                matrix[done]()
                done += 1

    def mixed(first, second):
        return [work for pair in zip(first, second) for work in pair] + (
            first[len(second) :] + second[len(first) :]
        )

    @pl.when(step == 0)
    def _():
        place = lax.axis_index("seq")
        core = lax.rem(place, CORES)
        first_row = place * tokens
        row_pos = first_row + lax.broadcasted_iota(jnp.int32, (8, tokens), 1)
        seg_start = jnp.zeros((8, tokens), jnp.int32)
        end = jnp.int32(0)
        for i in range(lengths.shape[0]):
            end = end + lengths[i]
            seg_start = jnp.where(row_pos >= end, end, seg_start)
        seg_start, row_pos = seg_start[:1], row_pos[:1]
        near = 1 + 2 * core
        for i, distance in enumerate((0, 2, FAR, near, 4 - near)):
            for row in range(0, tokens, TILE):
                key_pos = (first_row - distance * tokens + row) + lax.broadcasted_iota(
                    jnp.int32, (TILE, tokens), 0
                )
                allowed = (key_pos >= seg_start) & (key_pos <= row_pos)
                at = i * tokens + row
                bias[at : at + TILE] = jnp.where(allowed, 0.0, NEG)
        for n in range(kv_heads):
            k_at, v_at = 2 * n * HD, (2 * n + 1) * HD
            for ref, start, size, at in (
                (sent_ref, 0, half, 0),
                (got_ref, 0, half, half),
                (own_ref, 0, tokens, resp_at[0]),
                (sent_ref, half, tokens, resp_at[1]),
                (far_ref, 0, tokens, resp_at[2]),
                (got_ref, half, tokens, resp_at[3]),
                (got_ref, half + tokens, tokens, resp_at[4]),
            ):
                k_rows = ref[start : start + size, k_at : k_at + HD]
                v_rows = ref[start : start + size, v_at : v_at + HD]
                keys[n, at : at + size] = k_rows
                values[n, at : at + size] = v_rows
                keys_t[n, :, at : at + size] = k_rows.T
                values_t[n, :, at : at + size] = v_rows.T
        dk[...] = jnp.zeros_like(dk)
        dv[...] = jnp.zeros_like(dv)
        for ref in (p_bufs, d_bufs, inv_bufs, q_ns, cot_ns):
            ref[1] = jnp.zeros(ref.shape[1:], ref.dtype)
        for work in ahead(0, 0, q_ref, do_ref):
            work()

    @pl.when(step < last)
    def _():
        kv = kv_of(step)
        together(
            weigh(0),
            mixed(behind(1, kv_of(step - 1), step - 1), ahead(1, kv, q_ref, do_ref)),
        )
        together(
            weigh(1),
            mixed(behind(0, kv, step), ahead(0, kv_of(step + 1), next_q_ref, next_do_ref)),
        )

    @pl.when(step == last)
    def _():
        for work in behind(1, kv_of(step - 1), step - 1):
            work()
        for n in range(kv_heads):
            k_cols = slice(2 * n * HD, (2 * n + 1) * HD)
            v_cols = slice((2 * n + 1) * HD, (2 * n + 2) * HD)
            for ref, start, size, at in (
                (kept_ref, 0, half, 0),
                (back_ref, 0, half, half),
                (kept_ref, half + 2 * tokens, tokens, resp_at[0]),
                (kept_ref, half, tokens, resp_at[1]),
                (kept_ref, half + tokens, tokens, resp_at[2]),
                (back_ref, half, tokens, resp_at[3]),
                (back_ref, half + tokens, tokens, resp_at[4]),
            ):
                grad_k = dk[n, at : at + size] * score_scale
                ref[start : start + size, k_cols] = grad_k.astype(ref.dtype)
                ref[start : start + size, v_cols] = dv[n, at : at + size].astype(ref.dtype)


def attention(lengths, resp_q, grad_out, sent, got, own, far):
    tokens = resp_q.shape[0]
    half = sent.shape[0] - 2 * tokens
    total_keys = 2 * half + 5 * tokens
    kv_heads = sent.shape[1] // (2 * HD)
    q_heads = resp_q.shape[1] // HD
    halves = 1 if tokens * total_keys <= MOST_SCORES else 2
    rows = tokens // halves
    steps = q_heads * halves // 2
    width = 2 // halves * HD

    def block(later):
        return pl.BlockSpec((tokens, width), lambda i: (0, jnp.minimum(i + later, steps - 1)))

    pairs = tokens * q_heads * total_keys
    return pl.pallas_call(
        functools.partial(attention_kernel, tokens, halves, steps // kv_heads),
        grid=(steps + 1,),
        in_specs=[pl.BlockSpec(memory_space=pltpu.SMEM), block(0), block(1), block(0), block(1)]
        + whole(4),
        out_specs=whole(4),
        out_shape=[
            jax.ShapeDtypeStruct(resp_q.shape, BF16),
            jax.ShapeDtypeStruct(resp_q.shape, BF16),
            jax.ShapeDtypeStruct((half + 3 * tokens, sent.shape[1]), F32),
            jax.ShapeDtypeStruct((half + 2 * tokens, sent.shape[1]), BF16),
        ],
        scratch_shapes=[
            pltpu.VMEM((5 * tokens, tokens), F32),
            pltpu.VMEM((kv_heads, total_keys, HD), BF16),
            pltpu.VMEM((kv_heads, total_keys, HD), BF16),
            pltpu.VMEM((kv_heads, HD, total_keys), BF16),
            pltpu.VMEM((kv_heads, HD, total_keys), BF16),
            pltpu.VMEM((2, total_keys, rows), F32),
            pltpu.VMEM((2, total_keys, rows), F32),
            pltpu.VMEM((2, total_keys, rows), BF16),
            pltpu.VMEM((2, total_keys, rows), BF16),
            pltpu.VMEM((2, 8, rows), F32),
            pltpu.VMEM((2, HD, rows), BF16),
            pltpu.VMEM((2, HD, rows), BF16),
            pltpu.VMEM((2, rows, HD), BF16),
            pltpu.VMEM((2, rows, HD), BF16),
            pltpu.VMEM((kv_heads, total_keys, HD), F32),
            pltpu.VMEM((kv_heads, total_keys, HD), F32),
        ],
        compiler_params=pltpu.CompilerParams(vmem_limit_bytes=(40 if halves == 1 else 50) << 20),
        cost_estimate=pl.CostEstimate(
            flops=12 * HD * pairs, bytes_accessed=8 * resp_q.size, transcendentals=pairs
        ),
        name="attention",
    )(lengths, resp_q, resp_q, grad_out, grad_out, sent, got, own, far)


def swap_heads(array, by):
    devices = lax.axis_size("head")
    return lax.ppermute(array, "head", [(i, i ^ by) for i in range(devices)])


def swap_chips(array, by):
    devices = lax.axis_size("seq")
    return lax.ppermute(array, "seq", [(i, i ^ (by * CORES)) for i in range(devices)])


def swap_cores(array):
    devices = lax.axis_size("seq")
    return lax.ppermute(array, "seq", [(i, i ^ 1) for i in range(devices)])


def shift_chips(array, by):
    devices = lax.axis_size("seq")
    by = by * CORES
    return lax.ppermute(array, "seq", [(i, i + by) for i in range(devices) if 0 <= i + by < devices])


def shards(prompt_k, prompt_v, resp_q, resp_k, resp_v, grad_out, resp_lengths):
    tokens, kv_cols = resp_k.shape
    wide = 2 * kv_cols
    groups = lax.axis_size("head")
    chips = lax.axis_size("seq") // CORES
    block = prompt_k.shape[0]
    core = lax.rem(lax.axis_index("seq"), CORES)

    *pieces, own = pack([prompt_k, prompt_v, resp_k, resp_v], groups)
    pieces = [pieces[0]] + [swap_heads(pieces[k], k) for k in range(1, groups)]
    near = shift_chips(own, 1)
    far = shift_chips(own, 2)
    pieces, near, far = lax.optimization_barrier((pieces, near, far))
    mine = jnp.concatenate(pieces, axis=0)
    parts = [mine] + [swap_chips(mine, k) for k in range(1, chips)]
    chosen = jnp.where(core == 1, far, own)
    sent = jnp.concatenate(parts + [near, chosen], axis=0)
    got = swap_cores(sent)

    resp_out, grad_q, kept, back = attention(
        resp_lengths, resp_q, grad_out, sent, got, own, far
    )

    back = swap_cores(back)
    share = groups * block
    *parts, near, far, own = local_call(
        functools.partial(merge_kernel, chips, tokens),
        "merge",
        [kept, back],
        [((share, wide), BF16)] * chips
        + [((tokens, wide), BF16)] * 2
        + [((tokens, wide), F32)],
    )
    parts = [parts[0]] + [swap_chips(parts[k], k) for k in range(1, chips)]
    parts, near, far = lax.optimization_barrier((parts, near, far))
    near = shift_chips(near, -1)
    far = shift_chips(far, -2)
    pieces = local_call(
        functools.partial(sum_kernel, chips),
        "sum_chips",
        parts,
        [((block, wide), BF16)] * groups,
        [pltpu.VMEM((share, wide), F32)],
    )
    pieces = [pieces[0]] + [swap_heads(pieces[k], k) for k in range(1, groups)]
    grad_k_prompt, grad_v_prompt, grad_k_resp, grad_v_resp = local_call(
        finish_kernel,
        "finish",
        [own, near, far] + pieces,
        [(prompt_k.shape, BF16)] * 2 + [((tokens, kv_cols), BF16)] * 2,
    )
    return (resp_out, grad_q, grad_k_resp, grad_v_resp, grad_k_prompt, grad_v_prompt)


def solution(mesh):
    placed = (
        P(("seq", "head"), None),
        P(("seq", "head"), None),
        P("seq", "head"),
        P("seq", "head"),
        P("seq", "head"),
        P("seq", "head"),
        P(),
    )
    return jax.shard_map(
        shards,
        mesh=mesh,
        in_specs=placed,
        out_specs=(
            P("seq", "head"),
            P("seq", "head"),
            P("seq", "head"),
            P("seq", "head"),
            P(("seq", "head"), None),
            P(("seq", "head"), None),
        ),
        check_vma=False,
    )
```

```python
import functools
import math

import jax
import jax.numpy as jnp
from jax import lax
from jax.experimental import pallas as pl
from jax.experimental.pallas import tpu as pltpu
from jax.sharding import PartitionSpec as P

HD = 128
CORES = 2
FAR = 4
CHUNK = 1280
TILE = 64
MOST_SCORES = 2560 * 256
NEG = -1e30
BF16 = jnp.bfloat16
F32 = jnp.float32


def dot(a, b):
    return jnp.dot(a, b, preferred_element_type=F32)


def whole(count):
    return [pl.BlockSpec(memory_space=pltpu.VMEM)] * count


def local_call(kernel, name, inputs, outputs, scratch=()):
    return pl.pallas_call(
        kernel,
        in_specs=whole(len(inputs)),
        out_specs=whole(len(outputs)),
        out_shape=[jax.ShapeDtypeStruct(shape, kind) for shape, kind in outputs],
        scratch_shapes=list(scratch),
        compiler_params=pltpu.CompilerParams(vmem_limit_bytes=40 * 1024 * 1024),
        name=name,
    )(*inputs)


def pack_kernel(pk_ref, pv_ref, rk_ref, rv_ref, *outs):
    pieces, resp = outs[:-1], outs[-1]
    head = lax.axis_index("head")
    width = pieces[0].shape[1]
    for k, piece in enumerate(pieces):
        start = pl.multiple_of((head ^ k) * (width // 2), HD)
        for n in range(width // (2 * HD)):
            at = pl.multiple_of(start + n * HD, HD)
            piece[:, 2 * n * HD : (2 * n + 1) * HD] = pk_ref[:, pl.ds(at, HD)]
            piece[:, (2 * n + 1) * HD : (2 * n + 2) * HD] = pv_ref[:, pl.ds(at, HD)]
    for n in range(width // (2 * HD)):
        resp[:, 2 * n * HD : (2 * n + 1) * HD] = rk_ref[:, n * HD : (n + 1) * HD]
        resp[:, (2 * n + 1) * HD : (2 * n + 2) * HD] = rv_ref[:, n * HD : (n + 1) * HD]


def pack(inputs, groups):
    def one(array):
        return pl.BlockSpec(array.shape, lambda i: (0, 0))

    block, tokens = inputs[0].shape[0], inputs[2].shape[0]
    wide = 2 * inputs[2].shape[1]
    shapes = [(block, wide)] * groups + [(tokens, wide)]
    return pl.pallas_call(
        pack_kernel,
        grid=(1,),
        in_specs=[one(array) for array in inputs],
        out_specs=whole(groups + 1),
        out_shape=[jax.ShapeDtypeStruct(shape, BF16) for shape in shapes],
        compiler_params=pltpu.CompilerParams(vmem_limit_bytes=56 * 1024 * 1024),
        name="pack",
    )(*inputs)


def merge_kernel(parts, rows, kept_ref, got_ref, *outs):
    pieces, back1, back2, own = outs[:parts], outs[parts], outs[parts + 1], outs[parts + 2]
    core = lax.rem(lax.axis_index("seq"), CORES)
    to_own = jnp.where(core == 0, 1.0, 0.0)
    half = kept_ref.shape[0] - 3 * rows
    share = half // parts
    for k, piece in enumerate(pieces):
        at = slice(k * share, (k + 1) * share)
        piece[...] = (kept_ref[at] + got_ref[at].astype(F32)).astype(BF16)
    one, two, three = half + rows, half + 2 * rows, half + 3 * rows
    back1[...] = (kept_ref[half:one] + got_ref[half:one].astype(F32)).astype(BF16)
    chosen = got_ref[one:two].astype(F32)
    back2[...] = (kept_ref[one:two] + chosen * (1.0 - to_own)).astype(BF16)
    own[...] = kept_ref[two:three] + chosen * to_own


def sum_kernel(parts, *refs):
    ins, outs, total = refs[:parts], refs[parts:-1], refs[-1]
    acc = ins[0][...].astype(F32)
    for ref in ins[1:]:
        acc = acc + ref[...].astype(F32)
    total[...] = acc
    share = total.shape[0] // len(outs)
    for k, out in enumerate(outs):
        out[...] = total[k * share : (k + 1) * share].astype(BF16)


def finish_kernel(own_ref, one_ref, two_ref, *refs):
    pieces, (gk_ref, gv_ref, rk_ref, rv_ref) = refs[:-4], refs[-4:]
    head = lax.axis_index("head")
    width = pieces[0].shape[1]
    for k, piece in enumerate(pieces):
        start = pl.multiple_of((head ^ k) * (width // 2), HD)
        for n in range(width // (2 * HD)):
            at = pl.multiple_of(start + n * HD, HD)
            gk_ref[:, pl.ds(at, HD)] = piece[:, 2 * n * HD : (2 * n + 1) * HD]
            gv_ref[:, pl.ds(at, HD)] = piece[:, (2 * n + 1) * HD : (2 * n + 2) * HD]
    total = (own_ref[...] + one_ref[...].astype(F32) + two_ref[...].astype(F32)).astype(BF16)
    for n in range(width // (2 * HD)):
        rk_ref[:, n * HD : (n + 1) * HD] = total[:, 2 * n * HD : (2 * n + 1) * HD]
        rv_ref[:, n * HD : (n + 1) * HD] = total[:, (2 * n + 1) * HD : (2 * n + 2) * HD]


def attention_kernel(
    halves, lengths, q_ref, do_ref, sent_ref, got_ref, own_ref, far_ref,
    o_ref, dq_ref, kept_ref, back_ref,
    bias, keys, values, keys_t, values_t, s_bufs, g_bufs, p_bufs, d_bufs, top_bufs, inv_bufs,
    q_ts, cot_ts, q_ns, cot_ns, dk, dv,
):
    kv_heads, total_keys = keys.shape[0], keys.shape[1]
    tokens, q_cols = q_ref.shape
    rows = tokens // halves
    prompt_len = total_keys - 5 * tokens
    half = prompt_len // 2
    steps = q_cols // HD * halves // 2
    steps_per_kv = steps // kv_heads
    score_scale = 1.0 / math.sqrt(HD)
    exp_scale = score_scale * math.log2(math.e)
    resp_at = [prompt_len + i * tokens for i in range(6)]
    tiles = [slice(at, at + TILE) for at in range(0, total_keys, TILE)]
    chunks = [slice(at, at + CHUNK) for at in range(0, total_keys, CHUNK)]

    def place_of(which, step):
        head = step * 2 + which if halves == 1 else step
        row = 0 if halves == 1 else which * rows
        return slice(row, row + rows), pl.ds(pl.multiple_of(head * HD, HD), HD)

    def kv_of(step):
        return jnp.clip(step // steps_per_kv, 0, kv_heads - 1)

    def bias_at(which, at, size):
        row = which * rows * (halves - 1)
        return bias[at - prompt_len : at - prompt_len + size, row : row + rows]

    def folded(x):
        return x.reshape(x.shape[0] // 8, 8, rows)

    def ahead(which, step):
        kv = kv_of(step)
        where = place_of(which, jnp.minimum(step, steps - 1))

        def lift():
            q_ts[which] = q_ref[where].T
            cot_ts[which] = do_ref[where].T

        def scores(at):
            whole_s = dot(keys[kv, at], q_ts[which])
            top = None
            for start in range(at.start, at.stop, TILE):
                s = whole_s[start - at.start : start - at.start + TILE]
                if start >= prompt_len:
                    s = s + bias_at(which, start, TILE)
                s_bufs[which, start : start + TILE] = s
                part = jnp.max(folded(s), axis=0)
                top = part if top is None else jnp.maximum(top, part)
            if at.start == 0:
                top_bufs[which] = top
            else:
                top_bufs[which] = jnp.maximum(top_bufs[which], top)

        def grads(at):
            g_bufs[which, at] = dot(values[kv, at], cot_ts[which])

        return [lift] + [functools.partial(f, at) for at in chunks for f in (scores, grads)]

    def behind(which, step):
        kv = kv_of(step)
        where = place_of(which, jnp.maximum(step, 0))
        cuts = [slice(at, at + total_keys // 2) for at in (0, total_keys // 2)]
        state = {}

        def output(at):
            more = dot(values_t[kv, :, at], p_bufs[which, at])
            state["out"] = state["out"] + more if "out" in state else more

        def query(at):
            more = dot(keys_t[kv, :, at], d_bufs[which, at])
            state["dq"] = state["dq"] + more if "dq" in state else more

        def put_output():
            o_ref[where] = (state["out"] * inv_bufs[which, :1]).astype(BF16).T

        def put_query():
            dq = state["dq"] * (inv_bufs[which, :1] * score_scale)
            dq_ref[where] = dq.astype(BF16).T

        def value_grad(at):
            dv[kv, at] += dot(p_bufs[which, at], cot_ns[which])

        def key_grad(at):
            dk[kv, at] += dot(d_bufs[which, at], q_ns[which])

        work = [functools.partial(f, at) for at in chunks for f in (value_grad, key_grad)]
        first = [functools.partial(output, at) for at in cuts] + [put_output]
        second = [functools.partial(query, at) for at in cuts] + [put_query]
        return first + work[: len(work) // 2] + second + work[len(work) // 2 :]

    def weigh(which):
        state = {}

        def settle():
            state["top"] = jnp.max(top_bufs[which], axis=0, keepdims=True) * exp_scale
            state["sum"] = jnp.zeros((8, rows), F32)
            state["dot"] = jnp.zeros((8, rows), F32)

        def weights(at):
            p = jnp.exp2(s_bufs[which, at] * exp_scale - state["top"])
            state["sum"] = state["sum"] + jnp.sum(folded(p), axis=0)
            state["dot"] = state["dot"] + jnp.sum(folded(p * g_bufs[which, at]), axis=0)
            p_bufs[which, at] = p.astype(BF16)

        def finish():
            inverse = 1.0 / jnp.sum(state["sum"], axis=0, keepdims=True)
            state["delta"] = jnp.sum(state["dot"], axis=0, keepdims=True) * inverse
            inv_bufs[which] = jnp.broadcast_to(inverse, (8, rows))
            q_ns[which] = (q_ts[which].astype(F32) * inverse).astype(BF16).T
            cot_ns[which] = (cot_ts[which].astype(F32) * inverse).astype(BF16).T

        def slopes(at):
            p = p_bufs[which, at].astype(F32)
            d_bufs[which, at] = (p * (g_bufs[which, at] - state["delta"])).astype(BF16)

        work = [settle] + [functools.partial(weights, at) for at in tiles] + [finish]
        return work + [functools.partial(slopes, at) for at in tiles]

    def together(vector, matrix):
        done = 0
        for i, work in enumerate(vector):
            work()
            while done * len(vector) < (i + 1) * len(matrix):
                matrix[done]()
                done += 1

    def mixed(first, second):
        return [work for pair in zip(first, second) for work in pair] + (
            first[len(second) :] + second[len(first) :]
        )

    place = lax.axis_index("seq")
    core = lax.rem(place, CORES)
    first_row = place * tokens
    row_pos = first_row + lax.broadcasted_iota(jnp.int32, (8, tokens), 1)
    seg_start = jnp.zeros((8, tokens), jnp.int32)
    end = jnp.int32(0)
    for i in range(lengths.shape[0]):
        end = end + lengths[i]
        seg_start = jnp.where(row_pos >= end, end, seg_start)
    seg_start, row_pos = seg_start[:1], row_pos[:1]
    near = 1 + 2 * core
    for i, distance in enumerate((0, 2, FAR, near, 4 - near)):
        for row in range(0, tokens, TILE):
            key_pos = (first_row - distance * tokens + row) + lax.broadcasted_iota(
                jnp.int32, (TILE, tokens), 0
            )
            allowed = (key_pos >= seg_start) & (key_pos <= row_pos)
            at = i * tokens + row
            bias[at : at + TILE] = jnp.where(allowed, 0.0, NEG)
    for n in range(kv_heads):
        k_at, v_at = 2 * n * HD, (2 * n + 1) * HD
        for ref, start, size, at in (
            (sent_ref, 0, half, 0),
            (got_ref, 0, half, half),
            (own_ref, 0, tokens, resp_at[0]),
            (sent_ref, half, tokens, resp_at[1]),
            (far_ref, 0, tokens, resp_at[2]),
            (got_ref, half, tokens, resp_at[3]),
            (got_ref, half + tokens, tokens, resp_at[4]),
        ):
            k_rows = ref[start : start + size, k_at : k_at + HD]
            v_rows = ref[start : start + size, v_at : v_at + HD]
            keys[n, at : at + size] = k_rows
            values[n, at : at + size] = v_rows
            keys_t[n, :, at : at + size] = k_rows.T
            values_t[n, :, at : at + size] = v_rows.T
    dk[...] = jnp.zeros_like(dk)
    dv[...] = jnp.zeros_like(dv)
    for ref in (p_bufs, d_bufs, inv_bufs, q_ns, cot_ns):
        ref[1] = jnp.zeros(ref.shape[1:], ref.dtype)
    for work in ahead(0, 0):
        work()

    def pair(step, carry):
        together(weigh(0), mixed(behind(1, step - 1), ahead(1, step)))
        together(weigh(1), mixed(behind(0, step), ahead(0, step + 1)))
        return carry

    lax.fori_loop(0, steps, pair, 0)
    for work in behind(1, steps - 1):
        work()
    for n in range(kv_heads):
        k_cols = slice(2 * n * HD, (2 * n + 1) * HD)
        v_cols = slice((2 * n + 1) * HD, (2 * n + 2) * HD)
        for ref, start, size, at in (
            (kept_ref, 0, half, 0),
            (back_ref, 0, half, half),
            (kept_ref, half + 2 * tokens, tokens, resp_at[0]),
            (kept_ref, half, tokens, resp_at[1]),
            (kept_ref, half + tokens, tokens, resp_at[2]),
            (back_ref, half, tokens, resp_at[3]),
            (back_ref, half + tokens, tokens, resp_at[4]),
        ):
            grad_k = dk[n, at : at + size] * score_scale
            ref[start : start + size, k_cols] = grad_k.astype(ref.dtype)
            ref[start : start + size, v_cols] = dv[n, at : at + size].astype(ref.dtype)


def attention(lengths, resp_q, grad_out, sent, got, own, far):
    tokens = resp_q.shape[0]
    half = sent.shape[0] - 2 * tokens
    total_keys = 2 * half + 5 * tokens
    kv_heads = sent.shape[1] // (2 * HD)
    q_heads = resp_q.shape[1] // HD
    halves = 1 if tokens * total_keys <= MOST_SCORES else 2
    rows = tokens // halves
    pairs = tokens * q_heads * total_keys
    return pl.pallas_call(
        functools.partial(attention_kernel, halves),
        in_specs=[pl.BlockSpec(memory_space=pltpu.SMEM)] + whole(6),
        out_specs=whole(4),
        out_shape=[
            jax.ShapeDtypeStruct(resp_q.shape, BF16),
            jax.ShapeDtypeStruct(resp_q.shape, BF16),
            jax.ShapeDtypeStruct((half + 3 * tokens, sent.shape[1]), F32),
            jax.ShapeDtypeStruct((half + 2 * tokens, sent.shape[1]), BF16),
        ],
        scratch_shapes=[
            pltpu.VMEM((5 * tokens, tokens), F32),
            pltpu.VMEM((kv_heads, total_keys, HD), BF16),
            pltpu.VMEM((kv_heads, total_keys, HD), BF16),
            pltpu.VMEM((kv_heads, HD, total_keys), BF16),
            pltpu.VMEM((kv_heads, HD, total_keys), BF16),
            pltpu.VMEM((2, total_keys, rows), F32),
            pltpu.VMEM((2, total_keys, rows), F32),
            pltpu.VMEM((2, total_keys, rows), BF16),
            pltpu.VMEM((2, total_keys, rows), BF16),
            pltpu.VMEM((2, 8, rows), F32),
            pltpu.VMEM((2, 8, rows), F32),
            pltpu.VMEM((2, HD, rows), BF16),
            pltpu.VMEM((2, HD, rows), BF16),
            pltpu.VMEM((2, rows, HD), BF16),
            pltpu.VMEM((2, rows, HD), BF16),
            pltpu.VMEM((kv_heads, total_keys, HD), F32),
            pltpu.VMEM((kv_heads, total_keys, HD), F32),
        ],
        compiler_params=pltpu.CompilerParams(vmem_limit_bytes=(36 if halves == 1 else 48) << 20),
        cost_estimate=pl.CostEstimate(
            flops=12 * HD * pairs, bytes_accessed=8 * resp_q.size, transcendentals=pairs
        ),
        name="attention",
    )(lengths, resp_q, grad_out, sent, got, own, far)


def swap_heads(array, by):
    devices = lax.axis_size("head")
    return lax.ppermute(array, "head", [(i, i ^ by) for i in range(devices)])


def swap_chips(array, by):
    devices = lax.axis_size("seq")
    return lax.ppermute(array, "seq", [(i, i ^ (by * CORES)) for i in range(devices)])


def swap_cores(array):
    devices = lax.axis_size("seq")
    return lax.ppermute(array, "seq", [(i, i ^ 1) for i in range(devices)])


def shift_chips(array, by):
    devices = lax.axis_size("seq")
    by = by * CORES
    return lax.ppermute(array, "seq", [(i, i + by) for i in range(devices) if 0 <= i + by < devices])


def shards(prompt_k, prompt_v, resp_q, resp_k, resp_v, grad_out, resp_lengths):
    tokens, kv_cols = resp_k.shape
    wide = 2 * kv_cols
    groups = lax.axis_size("head")
    chips = lax.axis_size("seq") // CORES
    block = prompt_k.shape[0]
    core = lax.rem(lax.axis_index("seq"), CORES)

    *pieces, own = pack([prompt_k, prompt_v, resp_k, resp_v], groups)
    pieces = [pieces[0]] + [swap_heads(pieces[k], k) for k in range(1, groups)]
    near = shift_chips(own, 1)
    far = shift_chips(own, 2)
    pieces, near, far = lax.optimization_barrier((pieces, near, far))
    mine = jnp.concatenate(pieces, axis=0)
    parts = [mine] + [swap_chips(mine, k) for k in range(1, chips)]
    chosen = jnp.where(core == 1, far, own)
    sent = jnp.concatenate(parts + [near, chosen], axis=0)
    got = swap_cores(sent)

    resp_out, grad_q, kept, back = attention(
        resp_lengths, resp_q, grad_out, sent, got, own, far
    )

    back = swap_cores(back)
    share = groups * block
    *parts, near, far, own = local_call(
        functools.partial(merge_kernel, chips, tokens),
        "merge",
        [kept, back],
        [((share, wide), BF16)] * chips
        + [((tokens, wide), BF16)] * 2
        + [((tokens, wide), F32)],
    )
    parts = [parts[0]] + [swap_chips(parts[k], k) for k in range(1, chips)]
    parts, near, far = lax.optimization_barrier((parts, near, far))
    near = shift_chips(near, -1)
    far = shift_chips(far, -2)
    pieces = local_call(
        functools.partial(sum_kernel, chips),
        "sum_chips",
        parts,
        [((block, wide), BF16)] * groups,
        [pltpu.VMEM((share, wide), F32)],
    )
    pieces = [pieces[0]] + [swap_heads(pieces[k], k) for k in range(1, groups)]
    grad_k_prompt, grad_v_prompt, grad_k_resp, grad_v_resp = local_call(
        finish_kernel,
        "finish",
        [own, near, far] + pieces,
        [(prompt_k.shape, BF16)] * 2 + [((tokens, kv_cols), BF16)] * 2,
    )
    return (resp_out, grad_q, grad_k_resp, grad_v_resp, grad_k_prompt, grad_v_prompt)


def solution(mesh):
    placed = (
        P(("seq", "head"), None),
        P(("seq", "head"), None),
        P("seq", "head"),
        P("seq", "head"),
        P("seq", "head"),
        P("seq", "head"),
        P(),
    )
    return jax.shard_map(
        shards,
        mesh=mesh,
        in_specs=placed,
        out_specs=(
            P("seq", "head"),
            P("seq", "head"),
            P("seq", "head"),
            P("seq", "head"),
            P(("seq", "head"), None),
            P(("seq", "head"), None),
        ),
        check_vma=False,
    )
```

```python
import functools
import math

import jax
import jax.numpy as jnp
from jax import lax
from jax.experimental import pallas as pl
from jax.experimental.pallas import tpu as pltpu
from jax.sharding import PartitionSpec as P

HD = 128
CORES = 2
FAR = 4
CHUNK = 1280
TILE = 64
MOST_SCORES = 2560 * 256
NEG = -1e30
BF16 = jnp.bfloat16
F32 = jnp.float32


def dot(a, b):
    return jnp.dot(a, b, preferred_element_type=F32)


def whole(count):
    return [pl.BlockSpec(memory_space=pltpu.VMEM)] * count


def local_call(kernel, name, inputs, outputs, scratch=()):
    return pl.pallas_call(
        kernel,
        in_specs=whole(len(inputs)),
        out_specs=whole(len(outputs)),
        out_shape=[jax.ShapeDtypeStruct(shape, kind) for shape, kind in outputs],
        scratch_shapes=list(scratch),
        compiler_params=pltpu.CompilerParams(vmem_limit_bytes=40 * 1024 * 1024),
        name=name,
    )(*inputs)


def pack_kernel(pk_ref, pv_ref, rk_ref, rv_ref, *outs):
    pieces, resp = outs[:-1], outs[-1]
    head = lax.axis_index("head")
    width = pieces[0].shape[1]
    for k, piece in enumerate(pieces):
        start = pl.multiple_of((head ^ k) * (width // 2), HD)
        for n in range(width // (2 * HD)):
            at = pl.multiple_of(start + n * HD, HD)
            piece[:, 2 * n * HD : (2 * n + 1) * HD] = pk_ref[:, pl.ds(at, HD)]
            piece[:, (2 * n + 1) * HD : (2 * n + 2) * HD] = pv_ref[:, pl.ds(at, HD)]
    for n in range(width // (2 * HD)):
        resp[:, 2 * n * HD : (2 * n + 1) * HD] = rk_ref[:, n * HD : (n + 1) * HD]
        resp[:, (2 * n + 1) * HD : (2 * n + 2) * HD] = rv_ref[:, n * HD : (n + 1) * HD]


def pack(inputs, groups):
    def one(array):
        return pl.BlockSpec(array.shape, lambda i: (0, 0))

    block, tokens = inputs[0].shape[0], inputs[2].shape[0]
    wide = 2 * inputs[2].shape[1]
    shapes = [(block, wide)] * groups + [(tokens, wide)]
    return pl.pallas_call(
        pack_kernel,
        grid=(1,),
        in_specs=[one(array) for array in inputs],
        out_specs=whole(groups + 1),
        out_shape=[jax.ShapeDtypeStruct(shape, BF16) for shape in shapes],
        compiler_params=pltpu.CompilerParams(vmem_limit_bytes=56 * 1024 * 1024),
        name="pack",
    )(*inputs)


def merge_kernel(parts, rows, kept_ref, got_ref, *outs):
    pieces, back1, back2, own = outs[:parts], outs[parts:-3], outs[-3:-1], outs[-1]
    core = lax.rem(lax.axis_index("seq"), CORES)
    to_own = jnp.where(core == 0, 1.0, 0.0)
    half = kept_ref.shape[0] - 3 * rows
    share = half // parts
    for k, piece in enumerate(pieces):
        at = slice(k * share, (k + 1) * share)
        piece[...] = (kept_ref[at] + got_ref[at].astype(F32)).astype(BF16)
    one, two, three = half + rows, half + 2 * rows, half + 3 * rows
    near = (kept_ref[half:one] + got_ref[half:one].astype(F32)).astype(BF16)
    chosen = got_ref[one:two].astype(F32)
    far = (kept_ref[one:two] + chosen * (1.0 - to_own)).astype(BF16)
    for i in range(2):
        back1[i][...] = near[i * rows // 2 : (i + 1) * rows // 2]
        back2[i][...] = far[i * rows // 2 : (i + 1) * rows // 2]
    own[...] = kept_ref[two:three] + chosen * to_own


def sum_kernel(parts, *refs):
    ins, outs, total = refs[:parts], refs[parts:-1], refs[-1]
    acc = ins[0][...].astype(F32)
    for ref in ins[1:]:
        acc = acc + ref[...].astype(F32)
    total[...] = acc
    share = total.shape[0] // len(outs)
    for k, out in enumerate(outs):
        out[...] = total[k * share : (k + 1) * share].astype(BF16)


def finish_kernel(own_ref, *refs):
    near, far, pieces, (gk_ref, gv_ref, rk_ref, rv_ref) = refs[:2], refs[2:4], refs[4:-4], refs[-4:]
    head = lax.axis_index("head")
    width = pieces[0].shape[1]
    for k, piece in enumerate(pieces):
        start = pl.multiple_of((head ^ k) * (width // 2), HD)
        for n in range(width // (2 * HD)):
            at = pl.multiple_of(start + n * HD, HD)
            gk_ref[:, pl.ds(at, HD)] = piece[:, 2 * n * HD : (2 * n + 1) * HD]
            gv_ref[:, pl.ds(at, HD)] = piece[:, (2 * n + 1) * HD : (2 * n + 2) * HD]
    rows = near[0].shape[0]
    for i in range(2):
        at = slice(i * rows, (i + 1) * rows)
        total = own_ref[at] + near[i][...].astype(F32) + far[i][...].astype(F32)
        total = total.astype(BF16)
        for n in range(width // (2 * HD)):
            rk_ref[at, n * HD : (n + 1) * HD] = total[:, 2 * n * HD : (2 * n + 1) * HD]
            rv_ref[at, n * HD : (n + 1) * HD] = total[:, (2 * n + 1) * HD : (2 * n + 2) * HD]


def attention_kernel(
    halves, lengths, q_ref, do_ref, sent_ref, got_ref, own_ref, far_ref,
    o_ref, dq_ref, kept_ref, back_ref,
    bias, keys, values, keys_t, values_t, s_bufs, g_bufs, p_bufs, d_bufs, top_bufs, inv_bufs,
    q_ts, cot_ts, q_ns, cot_ns, dk, dv,
):
    kv_heads, total_keys = keys.shape[0], keys.shape[1]
    tokens, q_cols = q_ref.shape
    rows = tokens // halves
    prompt_len = total_keys - 5 * tokens
    half = prompt_len // 2
    steps = q_cols // HD * halves // 2
    steps_per_kv = steps // kv_heads
    score_scale = 1.0 / math.sqrt(HD)
    exp_scale = score_scale * math.log2(math.e)
    resp_at = [prompt_len + i * tokens for i in range(6)]
    tiles = [slice(at, at + TILE) for at in range(0, total_keys, TILE)]
    chunks = [slice(at, at + CHUNK) for at in range(0, total_keys, CHUNK)]

    def place_of(which, step):
        head = step * 2 + which if halves == 1 else step
        row = 0 if halves == 1 else which * rows
        return slice(row, row + rows), pl.ds(pl.multiple_of(head * HD, HD), HD)

    def kv_of(step):
        return jnp.clip(step // steps_per_kv, 0, kv_heads - 1)

    def bias_at(which, at, size):
        row = which * rows * (halves - 1)
        return bias[at - prompt_len : at - prompt_len + size, row : row + rows]

    def folded(x):
        return x.reshape(x.shape[0] // 8, 8, rows)

    def ahead(which, step):
        kv = kv_of(step)
        where = place_of(which, jnp.minimum(step, steps - 1))

        def lift():
            q_ts[which] = q_ref[where].T
            cot_ts[which] = do_ref[where].T

        def scores(at):
            whole_s = dot(keys[kv, at], q_ts[which])
            top = None
            for start in range(at.start, at.stop, TILE):
                s = whole_s[start - at.start : start - at.start + TILE]
                if start >= prompt_len:
                    s = s + bias_at(which, start, TILE)
                s_bufs[which, start : start + TILE] = s
                part = jnp.max(folded(s), axis=0)
                top = part if top is None else jnp.maximum(top, part)
            if at.start == 0:
                top_bufs[which] = top
            else:
                top_bufs[which] = jnp.maximum(top_bufs[which], top)

        def grads(at):
            g_bufs[which, at] = dot(values[kv, at], cot_ts[which])

        return [lift] + [functools.partial(f, at) for at in chunks for f in (scores, grads)]

    def behind(which, step):
        kv = kv_of(step)
        where = place_of(which, jnp.maximum(step, 0))
        cuts = [slice(at, at + total_keys // 2) for at in (0, total_keys // 2)]
        state = {}

        def output(at):
            more = dot(values_t[kv, :, at], p_bufs[which, at])
            state["out"] = state["out"] + more if "out" in state else more

        def query(at):
            more = dot(keys_t[kv, :, at], d_bufs[which, at])
            state["dq"] = state["dq"] + more if "dq" in state else more

        def put_output():
            o_ref[where] = (state["out"] * inv_bufs[which, :1]).astype(BF16).T

        def put_query():
            dq = state["dq"] * (inv_bufs[which, :1] * score_scale)
            dq_ref[where] = dq.astype(BF16).T

        def value_grad(at):
            dv[kv, at] += dot(p_bufs[which, at], cot_ns[which])

        def key_grad(at):
            dk[kv, at] += dot(d_bufs[which, at], q_ns[which])

        work = [functools.partial(f, at) for at in chunks for f in (value_grad, key_grad)]
        first = [functools.partial(output, at) for at in cuts] + [put_output]
        second = [functools.partial(query, at) for at in cuts] + [put_query]
        return first + work[: len(work) // 2] + second + work[len(work) // 2 :]

    def weigh(which):
        state = {}

        def settle():
            state["top"] = jnp.max(top_bufs[which], axis=0, keepdims=True) * exp_scale
            state["sum"] = jnp.zeros((8, rows), F32)
            state["dot"] = jnp.zeros((8, rows), F32)

        def weights(at):
            p = jnp.exp2(s_bufs[which, at] * exp_scale - state["top"])
            state["sum"] = state["sum"] + jnp.sum(folded(p), axis=0)
            state["dot"] = state["dot"] + jnp.sum(folded(p * g_bufs[which, at]), axis=0)
            p_bufs[which, at] = p.astype(BF16)

        def finish():
            inverse = 1.0 / jnp.sum(state["sum"], axis=0, keepdims=True)
            state["delta"] = jnp.sum(state["dot"], axis=0, keepdims=True) * inverse
            inv_bufs[which] = jnp.broadcast_to(inverse, (8, rows))
            q_ns[which] = (q_ts[which].astype(F32) * inverse).astype(BF16).T
            cot_ns[which] = (cot_ts[which].astype(F32) * inverse).astype(BF16).T

        def slopes(at):
            slope = (g_bufs[which, at] - state["delta"]).astype(BF16)
            d_bufs[which, at] = p_bufs[which, at] * slope

        work = [settle] + [functools.partial(weights, at) for at in tiles] + [finish]
        return work + [functools.partial(slopes, at) for at in tiles]

    def together(vector, matrix):
        done = 0
        for i, work in enumerate(vector):
            work()
            while done * len(vector) < (i + 1) * len(matrix):
                matrix[done]()
                done += 1

    def mixed(first, second):
        return [work for pair in zip(first, second) for work in pair] + (
            first[len(second) :] + second[len(first) :]
        )

    place = lax.axis_index("seq")
    core = lax.rem(place, CORES)
    first_row = place * tokens
    row_pos = first_row + lax.broadcasted_iota(jnp.int32, (8, tokens), 1)
    seg_start = jnp.zeros((8, tokens), jnp.int32)
    end = jnp.int32(0)
    for i in range(lengths.shape[0]):
        end = end + lengths[i]
        seg_start = jnp.where(row_pos >= end, end, seg_start)
    seg_start, row_pos = seg_start[:1], row_pos[:1]
    near = 1 + 2 * core
    for i, distance in enumerate((0, 2, FAR, near, 4 - near)):
        for row in range(0, tokens, TILE):
            key_pos = (first_row - distance * tokens + row) + lax.broadcasted_iota(
                jnp.int32, (TILE, tokens), 0
            )
            allowed = (key_pos >= seg_start) & (key_pos <= row_pos)
            at = i * tokens + row
            bias[at : at + TILE] = jnp.where(allowed, 0.0, NEG)
    for n in range(kv_heads):
        k_at, v_at = 2 * n * HD, (2 * n + 1) * HD
        for ref, start, size, at in (
            (sent_ref, 0, half, 0),
            (got_ref, 0, half, half),
            (own_ref, 0, tokens, resp_at[0]),
            (sent_ref, half, tokens, resp_at[1]),
            (far_ref, 0, tokens, resp_at[2]),
            (got_ref, half, tokens, resp_at[3]),
            (got_ref, half + tokens, tokens, resp_at[4]),
        ):
            k_rows = ref[start : start + size, k_at : k_at + HD]
            v_rows = ref[start : start + size, v_at : v_at + HD]
            keys[n, at : at + size] = k_rows
            values[n, at : at + size] = v_rows
            keys_t[n, :, at : at + size] = k_rows.T
            values_t[n, :, at : at + size] = v_rows.T
    dk[...] = jnp.zeros_like(dk)
    dv[...] = jnp.zeros_like(dv)
    for ref in (p_bufs, d_bufs, inv_bufs, q_ns, cot_ns):
        ref[1] = jnp.zeros(ref.shape[1:], ref.dtype)
    for work in ahead(0, 0):
        work()

    def pair(step, carry):
        together(weigh(0), mixed(behind(1, step - 1), ahead(1, step)))
        together(weigh(1), mixed(behind(0, step), ahead(0, step + 1)))
        return carry

    lax.fori_loop(0, steps, pair, 0)
    for work in behind(1, steps - 1):
        work()
    for n in range(kv_heads):
        k_cols = slice(2 * n * HD, (2 * n + 1) * HD)
        v_cols = slice((2 * n + 1) * HD, (2 * n + 2) * HD)
        for ref, start, size, at in (
            (kept_ref, 0, half, 0),
            (back_ref, 0, half, half),
            (kept_ref, half + 2 * tokens, tokens, resp_at[0]),
            (kept_ref, half, tokens, resp_at[1]),
            (kept_ref, half + tokens, tokens, resp_at[2]),
            (back_ref, half, tokens, resp_at[3]),
            (back_ref, half + tokens, tokens, resp_at[4]),
        ):
            grad_k = dk[n, at : at + size] * score_scale
            ref[start : start + size, k_cols] = grad_k.astype(ref.dtype)
            ref[start : start + size, v_cols] = dv[n, at : at + size].astype(ref.dtype)


def attention(lengths, resp_q, grad_out, sent, got, own, far):
    tokens = resp_q.shape[0]
    half = sent.shape[0] - 2 * tokens
    total_keys = 2 * half + 5 * tokens
    kv_heads = sent.shape[1] // (2 * HD)
    q_heads = resp_q.shape[1] // HD
    halves = 1 if tokens * total_keys <= MOST_SCORES else 2
    rows = tokens // halves
    pairs = tokens * q_heads * total_keys
    return pl.pallas_call(
        functools.partial(attention_kernel, halves),
        in_specs=[pl.BlockSpec(memory_space=pltpu.SMEM)] + whole(6),
        out_specs=whole(4),
        out_shape=[
            jax.ShapeDtypeStruct(resp_q.shape, BF16),
            jax.ShapeDtypeStruct(resp_q.shape, BF16),
            jax.ShapeDtypeStruct((half + 3 * tokens, sent.shape[1]), F32),
            jax.ShapeDtypeStruct((half + 2 * tokens, sent.shape[1]), BF16),
        ],
        scratch_shapes=[
            pltpu.VMEM((5 * tokens, tokens), F32),
            pltpu.VMEM((kv_heads, total_keys, HD), BF16),
            pltpu.VMEM((kv_heads, total_keys, HD), BF16),
            pltpu.VMEM((kv_heads, HD, total_keys), BF16),
            pltpu.VMEM((kv_heads, HD, total_keys), BF16),
            pltpu.VMEM((2, total_keys, rows), F32),
            pltpu.VMEM((2, total_keys, rows), F32),
            pltpu.VMEM((2, total_keys, rows), BF16),
            pltpu.VMEM((2, total_keys, rows), BF16),
            pltpu.VMEM((2, 8, rows), F32),
            pltpu.VMEM((2, 8, rows), F32),
            pltpu.VMEM((2, HD, rows), BF16),
            pltpu.VMEM((2, HD, rows), BF16),
            pltpu.VMEM((2, rows, HD), BF16),
            pltpu.VMEM((2, rows, HD), BF16),
            pltpu.VMEM((kv_heads, total_keys, HD), F32),
            pltpu.VMEM((kv_heads, total_keys, HD), F32),
        ],
        compiler_params=pltpu.CompilerParams(vmem_limit_bytes=(36 if halves == 1 else 48) << 20),
        cost_estimate=pl.CostEstimate(
            flops=12 * HD * pairs, bytes_accessed=8 * resp_q.size, transcendentals=pairs
        ),
        name="attention",
    )(lengths, resp_q, grad_out, sent, got, own, far)


def swap_heads(array, by):
    devices = lax.axis_size("head")
    return lax.ppermute(array, "head", [(i, i ^ by) for i in range(devices)])


def swap_chips(array, by):
    devices = lax.axis_size("seq")
    return lax.ppermute(array, "seq", [(i, i ^ (by * CORES)) for i in range(devices)])


def swap_cores(array):
    devices = lax.axis_size("seq")
    return lax.ppermute(array, "seq", [(i, i ^ 1) for i in range(devices)])


def shift_chips(array, by):
    devices = lax.axis_size("seq")
    by = by * CORES
    return lax.ppermute(array, "seq", [(i, i + by) for i in range(devices) if 0 <= i + by < devices])


def shards(prompt_k, prompt_v, resp_q, resp_k, resp_v, grad_out, resp_lengths):
    tokens, kv_cols = resp_k.shape
    wide = 2 * kv_cols
    groups = lax.axis_size("head")
    chips = lax.axis_size("seq") // CORES
    block = prompt_k.shape[0]
    core = lax.rem(lax.axis_index("seq"), CORES)

    *pieces, own = pack([prompt_k, prompt_v, resp_k, resp_v], groups)
    pieces = [pieces[0]] + [swap_heads(pieces[k], k) for k in range(1, groups)]
    near = shift_chips(own, 1)
    far = shift_chips(own, 2)
    pieces[1:], near, far = lax.optimization_barrier((pieces[1:], near, far))
    mine = jnp.concatenate(pieces, axis=0)
    parts = [mine] + [swap_chips(mine, k) for k in range(1, chips)]
    chosen = jnp.where(core == 1, far, own)
    sent = jnp.concatenate(parts + [near, chosen], axis=0)
    got = swap_cores(sent)

    resp_out, grad_q, kept, back = attention(
        resp_lengths, resp_q, grad_out, sent, got, own, far
    )

    back = swap_cores(back)
    share = groups * block
    *parts, own = local_call(
        functools.partial(merge_kernel, chips, tokens),
        "merge",
        [kept, back],
        [((share, wide), BF16)] * chips
        + [((tokens // 2, wide), BF16)] * 4
        + [((tokens, wide), F32)],
    )
    near, far, parts = parts[chips : chips + 2], parts[chips + 2 :], parts[:chips]
    parts = [parts[0]] + [swap_chips(parts[k], k) for k in range(1, chips)]
    near = [shift_chips(part, -1) for part in near]
    far = [shift_chips(part, -2) for part in far]
    pieces = local_call(
        functools.partial(sum_kernel, chips),
        "sum_chips",
        parts,
        [((block, wide), BF16)] * groups,
        [pltpu.VMEM((share, wide), F32)],
    )
    pieces = [pieces[0]] + [swap_heads(pieces[k], k) for k in range(1, groups)]
    grad_k_prompt, grad_v_prompt, grad_k_resp, grad_v_resp = local_call(
        finish_kernel,
        "finish",
        [own] + near + far + pieces,
        [(prompt_k.shape, BF16)] * 2 + [((tokens, kv_cols), BF16)] * 2,
    )
    return (resp_out, grad_q, grad_k_resp, grad_v_resp, grad_k_prompt, grad_v_prompt)


def solution(mesh):
    placed = (
        P(("seq", "head"), None),
        P(("seq", "head"), None),
        P("seq", "head"),
        P("seq", "head"),
        P("seq", "head"),
        P("seq", "head"),
        P(),
    )
    return jax.shard_map(
        shards,
        mesh=mesh,
        in_specs=placed,
        out_specs=(
            P("seq", "head"),
            P("seq", "head"),
            P("seq", "head"),
            P("seq", "head"),
            P(("seq", "head"), None),
            P(("seq", "head"), None),
        ),
        check_vma=False,
    )
```

```python
import functools
import math

import jax
import jax.numpy as jnp
from jax import lax
from jax.experimental import pallas as pl
from jax.experimental.pallas import tpu as pltpu
from jax.sharding import PartitionSpec as P

HD = 128
CORES = 2
FAR = 4
CHUNK = 1280
TILE = 64
MOST_SCORES = 2560 * 256
NEG = -1e30
BF16 = jnp.bfloat16
F32 = jnp.float32


def dot(a, b):
    return jnp.dot(a, b, preferred_element_type=F32)


def whole(count):
    return [pl.BlockSpec(memory_space=pltpu.VMEM)] * count


def local_call(kernel, name, inputs, outputs, scratch=()):
    return pl.pallas_call(
        kernel,
        in_specs=whole(len(inputs)),
        out_specs=whole(len(outputs)),
        out_shape=[jax.ShapeDtypeStruct(shape, kind) for shape, kind in outputs],
        scratch_shapes=list(scratch),
        compiler_params=pltpu.CompilerParams(vmem_limit_bytes=40 * 1024 * 1024),
        name=name,
    )(*inputs)


def pack_kernel(pk_ref, pv_ref, rk_ref, rv_ref, *outs):
    pieces, resp = outs[:-1], outs[-1]
    head = lax.axis_index("head")
    width = pieces[0].shape[1]
    for k, piece in enumerate(pieces):
        start = pl.multiple_of((head ^ k) * (width // 2), HD)
        for n in range(width // (2 * HD)):
            at = pl.multiple_of(start + n * HD, HD)
            piece[:, 2 * n * HD : (2 * n + 1) * HD] = pk_ref[:, pl.ds(at, HD)]
            piece[:, (2 * n + 1) * HD : (2 * n + 2) * HD] = pv_ref[:, pl.ds(at, HD)]
    for n in range(width // (2 * HD)):
        resp[:, 2 * n * HD : (2 * n + 1) * HD] = rk_ref[:, n * HD : (n + 1) * HD]
        resp[:, (2 * n + 1) * HD : (2 * n + 2) * HD] = rv_ref[:, n * HD : (n + 1) * HD]


def pack(inputs, groups):
    def one(array):
        return pl.BlockSpec(array.shape, lambda i: (0, 0))

    block, tokens = inputs[0].shape[0], inputs[2].shape[0]
    wide = 2 * inputs[2].shape[1]
    shapes = [(block, wide)] * groups + [(tokens, wide)]
    return pl.pallas_call(
        pack_kernel,
        grid=(1,),
        in_specs=[one(array) for array in inputs],
        out_specs=whole(groups + 1),
        out_shape=[jax.ShapeDtypeStruct(shape, BF16) for shape in shapes],
        compiler_params=pltpu.CompilerParams(vmem_limit_bytes=56 * 1024 * 1024),
        name="pack",
    )(*inputs)


def merge_kernel(parts, rows, kept_ref, got_ref, *outs):
    pieces, back1, back2, own = outs[:parts], outs[parts:-3], outs[-3:-1], outs[-1]
    core = lax.rem(lax.axis_index("seq"), CORES)
    to_own = jnp.where(core == 0, 1.0, 0.0)
    half = kept_ref.shape[0] - 3 * rows
    share = half // parts
    for k, piece in enumerate(pieces):
        at = slice(k * share, (k + 1) * share)
        piece[...] = (kept_ref[at] + got_ref[at].astype(F32)).astype(BF16)
    one, two, three = half + rows, half + 2 * rows, half + 3 * rows
    near = (kept_ref[half:one] + got_ref[half:one].astype(F32)).astype(BF16)
    chosen = got_ref[one:two].astype(F32)
    far = (kept_ref[one:two] + chosen * (1.0 - to_own)).astype(BF16)
    for i in range(2):
        back1[i][...] = near[i * rows // 2 : (i + 1) * rows // 2]
        back2[i][...] = far[i * rows // 2 : (i + 1) * rows // 2]
    own[...] = kept_ref[two:three] + chosen * to_own


def sum_kernel(parts, *refs):
    ins, outs, total = refs[:parts], refs[parts:-1], refs[-1]
    acc = ins[0][...].astype(F32)
    for ref in ins[1:]:
        acc = acc + ref[...].astype(F32)
    total[...] = acc
    share = total.shape[0] // len(outs)
    for k, out in enumerate(outs):
        out[...] = total[k * share : (k + 1) * share].astype(BF16)


def finish_kernel(own_ref, *refs):
    near, far, pieces, (gk_ref, gv_ref, rk_ref, rv_ref) = refs[:2], refs[2:4], refs[4:-4], refs[-4:]
    head = lax.axis_index("head")
    width = pieces[0].shape[1]
    for k, piece in enumerate(pieces):
        start = pl.multiple_of((head ^ k) * (width // 2), HD)
        for n in range(width // (2 * HD)):
            at = pl.multiple_of(start + n * HD, HD)
            gk_ref[:, pl.ds(at, HD)] = piece[:, 2 * n * HD : (2 * n + 1) * HD]
            gv_ref[:, pl.ds(at, HD)] = piece[:, (2 * n + 1) * HD : (2 * n + 2) * HD]
    rows = near[0].shape[0]
    for i in range(2):
        at = slice(i * rows, (i + 1) * rows)
        total = own_ref[at] + near[i][...].astype(F32) + far[i][...].astype(F32)
        total = total.astype(BF16)
        for n in range(width // (2 * HD)):
            rk_ref[at, n * HD : (n + 1) * HD] = total[:, 2 * n * HD : (2 * n + 1) * HD]
            rv_ref[at, n * HD : (n + 1) * HD] = total[:, (2 * n + 1) * HD : (2 * n + 2) * HD]


def kv_pieces(tokens, total_keys, sent_ref, got_ref, own_ref, far_ref):
    prompt_len = total_keys - 5 * tokens
    half = prompt_len // 2
    return [
        (sent_ref, 0, half, 0),
        (got_ref, 0, half, half),
        (own_ref, 0, tokens, prompt_len),
        (sent_ref, half, tokens, prompt_len + tokens),
        (far_ref, 0, tokens, prompt_len + 2 * tokens),
        (got_ref, half, tokens, prompt_len + 3 * tokens),
        (got_ref, half + tokens, tokens, prompt_len + 4 * tokens),
    ]


def attention_kernel(
    halves, lengths, q_ref, do_ref, sent_ref, got_ref, own_ref, far_ref,
    kept_ref, back_ref, inv_ref, p_ref, d_ref,
    bias, keys, values, s_bufs, g_bufs, p_bufs, d_bufs, top_bufs,
    q_ts, cot_ts, q_ns, cot_ns, dk, dv, sems,
):
    kv_heads, total_keys = keys.shape[0], keys.shape[1]
    tokens, q_cols = q_ref.shape
    rows = tokens // halves
    prompt_len = total_keys - 5 * tokens
    half = prompt_len // 2
    steps = q_cols // HD * halves // 2
    steps_per_kv = steps // kv_heads
    score_scale = 1.0 / math.sqrt(HD)
    exp_scale = score_scale * math.log2(math.e)
    resp_at = [prompt_len + i * tokens for i in range(5)]
    tiles = [slice(at, at + TILE) for at in range(0, total_keys, TILE)]
    chunks = [slice(at, at + CHUNK) for at in range(0, total_keys, CHUNK)]

    def place_of(which, step):
        head = step * 2 + which if halves == 1 else step
        row = 0 if halves == 1 else which * rows
        return slice(row, row + rows), pl.ds(pl.multiple_of(head * HD, HD), HD)

    def kv_of(step):
        return jnp.clip(step // steps_per_kv, 0, kv_heads - 1)

    def bias_at(which, at, size):
        row = which * rows * (halves - 1)
        return bias[at - prompt_len : at - prompt_len + size, row : row + rows]

    def folded(x):
        return x.reshape(x.shape[0] // 8, 8, rows)

    def ahead(which, step):
        kv = kv_of(step)
        where = place_of(which, jnp.minimum(step, steps - 1))

        def lift():
            q_ts[which] = q_ref[where].T
            cot_ts[which] = do_ref[where].T

        def scores(at):
            whole_s = dot(keys[kv, at], q_ts[which])
            top = None
            for start in range(at.start, at.stop, TILE):
                s = whole_s[start - at.start : start - at.start + TILE]
                if start >= prompt_len:
                    s = s + bias_at(which, start, TILE)
                s_bufs[which, start : start + TILE] = s
                part = jnp.max(folded(s), axis=0)
                top = part if top is None else jnp.maximum(top, part)
            if at.start == 0:
                top_bufs[which] = top
            else:
                top_bufs[which] = jnp.maximum(top_bufs[which], top)

        def grads(at):
            g_bufs[which, at] = dot(values[kv, at], cot_ts[which])

        return [lift] + [functools.partial(f, at) for at in chunks for f in (scores, grads)]

    def behind(which, step):
        kv = kv_of(step)

        def value_grad(at):
            dv[kv, at] += dot(p_bufs[which, at], cot_ns[which])

        def key_grad(at):
            dk[kv, at] += dot(d_bufs[which, at], q_ns[which])

        return [functools.partial(f, at) for at in chunks for f in (value_grad, key_grad)]

    def kept_copies(which, step):
        index = 2 * step + which
        return [
            pltpu.make_async_copy(p_bufs.at[which], p_ref.at[index], sems.at[which, 0]),
            pltpu.make_async_copy(d_bufs.at[which], d_ref.at[index], sems.at[which, 1]),
        ]

    def send(which, step):
        for copy in kept_copies(which, step):
            copy.start()

    def finish_sending(which, step):
        for copy in kept_copies(which, step):
            copy.wait()

    def weigh(which, step):
        state = {}

        def settle():
            state["top"] = jnp.max(top_bufs[which], axis=0, keepdims=True) * exp_scale
            state["sum"] = jnp.zeros((8, rows), F32)
            state["dot"] = jnp.zeros((8, rows), F32)

        def weights(at):
            p = jnp.exp2(s_bufs[which, at] * exp_scale - state["top"])
            state["sum"] = state["sum"] + jnp.sum(folded(p), axis=0)
            state["dot"] = state["dot"] + jnp.sum(folded(p * g_bufs[which, at]), axis=0)
            p_bufs[which, at] = p.astype(BF16)

        def finish():
            inverse = 1.0 / jnp.sum(state["sum"], axis=0, keepdims=True)
            state["delta"] = jnp.sum(state["dot"], axis=0, keepdims=True) * inverse
            inv_ref[2 * step + which] = jnp.broadcast_to(inverse, (8, rows))
            q_ns[which] = (q_ts[which].astype(F32) * inverse).astype(BF16).T
            cot_ns[which] = (cot_ts[which].astype(F32) * inverse).astype(BF16).T

        def slopes(at):
            slope = (g_bufs[which, at] - state["delta"]).astype(BF16)
            d_bufs[which, at] = p_bufs[which, at] * slope

        work = [settle] + [functools.partial(weights, at) for at in tiles] + [finish]
        return work + [functools.partial(slopes, at) for at in tiles]

    def together(vector, matrix):
        done = 0
        for i, work in enumerate(vector):
            work()
            while done * len(vector) < (i + 1) * len(matrix):
                matrix[done]()
                done += 1

    def mixed(first, second):
        return [work for pair in zip(first, second) for work in pair] + (
            first[len(second) :] + second[len(first) :]
        )

    place = lax.axis_index("seq")
    core = lax.rem(place, CORES)
    first_row = place * tokens
    row_pos = first_row + lax.broadcasted_iota(jnp.int32, (8, tokens), 1)
    seg_start = jnp.zeros((8, tokens), jnp.int32)
    end = jnp.int32(0)
    for i in range(lengths.shape[0]):
        end = end + lengths[i]
        seg_start = jnp.where(row_pos >= end, end, seg_start)
    seg_start, row_pos = seg_start[:1], row_pos[:1]
    near = 1 + 2 * core
    for i, distance in enumerate((0, 2, FAR, near, 4 - near)):
        for row in range(0, tokens, TILE):
            key_pos = (first_row - distance * tokens + row) + lax.broadcasted_iota(
                jnp.int32, (TILE, tokens), 0
            )
            allowed = (key_pos >= seg_start) & (key_pos <= row_pos)
            at = i * tokens + row
            bias[at : at + TILE] = jnp.where(allowed, 0.0, NEG)
    for n in range(kv_heads):
        k_at, v_at = 2 * n * HD, (2 * n + 1) * HD
        for ref, start, size, at in kv_pieces(tokens, total_keys, sent_ref, got_ref, own_ref, far_ref):
            keys[n, at : at + size] = ref[start : start + size, k_at : k_at + HD]
            values[n, at : at + size] = ref[start : start + size, v_at : v_at + HD]
    dk[...] = jnp.zeros_like(dk)
    dv[...] = jnp.zeros_like(dv)
    for ref in (p_bufs, d_bufs, q_ns, cot_ns):
        ref[1] = jnp.zeros(ref.shape[1:], ref.dtype)
    for work in ahead(0, 0):
        work()

    def pair(step, carry):
        @pl.when(step > 0)
        def _():
            send(1, step - 1)
            finish_sending(0, step - 1)

        together(weigh(0, step), mixed(behind(1, step - 1), ahead(1, step)))

        @pl.when(step > 0)
        def _():
            finish_sending(1, step - 1)

        send(0, step)
        together(weigh(1, step), mixed(behind(0, step), ahead(0, step + 1)))
        return carry

    lax.fori_loop(0, steps, pair, 0)
    send(1, steps - 1)
    for work in behind(1, steps - 1):
        work()
    finish_sending(0, steps - 1)
    finish_sending(1, steps - 1)
    for n in range(kv_heads):
        k_cols = slice(2 * n * HD, (2 * n + 1) * HD)
        v_cols = slice((2 * n + 1) * HD, (2 * n + 2) * HD)
        for ref, start, size, at in (
            (kept_ref, 0, half, 0),
            (back_ref, 0, half, half),
            (kept_ref, half + 2 * tokens, tokens, resp_at[0]),
            (kept_ref, half, tokens, resp_at[1]),
            (kept_ref, half + tokens, tokens, resp_at[2]),
            (back_ref, half, tokens, resp_at[3]),
            (back_ref, half + tokens, tokens, resp_at[4]),
        ):
            grad_k = dk[n, at : at + size] * score_scale
            ref[start : start + size, k_cols] = grad_k.astype(ref.dtype)
            ref[start : start + size, v_cols] = dv[n, at : at + size].astype(ref.dtype)


def attention(lengths, resp_q, grad_out, sent, got, own, far):
    tokens = resp_q.shape[0]
    half = sent.shape[0] - 2 * tokens
    total_keys = 2 * half + 5 * tokens
    kv_heads = sent.shape[1] // (2 * HD)
    q_heads = resp_q.shape[1] // HD
    halves = 1 if tokens * total_keys <= MOST_SCORES else 2
    rows = tokens // halves
    units = q_heads * halves
    pairs = tokens * q_heads * total_keys
    stored = jax.ShapeDtypeStruct((units, total_keys, rows), BF16)
    kept, back, inverses, weights, slopes = pl.pallas_call(
        functools.partial(attention_kernel, halves),
        in_specs=[pl.BlockSpec(memory_space=pltpu.SMEM)] + whole(6),
        out_specs=whole(3) + [pl.BlockSpec(memory_space=pl.ANY)] * 2,
        out_shape=[
            jax.ShapeDtypeStruct((half + 3 * tokens, sent.shape[1]), F32),
            jax.ShapeDtypeStruct((half + 2 * tokens, sent.shape[1]), BF16),
            jax.ShapeDtypeStruct((units, 8, rows), F32),
            stored,
            stored,
        ],
        scratch_shapes=[
            pltpu.VMEM((5 * tokens, tokens), F32),
            pltpu.VMEM((kv_heads, total_keys, HD), BF16),
            pltpu.VMEM((kv_heads, total_keys, HD), BF16),
            pltpu.VMEM((2, total_keys, rows), F32),
            pltpu.VMEM((2, total_keys, rows), F32),
            pltpu.VMEM((2, total_keys, rows), BF16),
            pltpu.VMEM((2, total_keys, rows), BF16),
            pltpu.VMEM((2, 8, rows), F32),
            pltpu.VMEM((2, HD, rows), BF16),
            pltpu.VMEM((2, HD, rows), BF16),
            pltpu.VMEM((2, rows, HD), BF16),
            pltpu.VMEM((2, rows, HD), BF16),
            pltpu.VMEM((kv_heads, total_keys, HD), F32),
            pltpu.VMEM((kv_heads, total_keys, HD), F32),
            pltpu.SemaphoreType.DMA((2, 2)),
        ],
        compiler_params=pltpu.CompilerParams(
            vmem_limit_bytes=(34 if halves == 1 else 44) << 20
        ),
        cost_estimate=pl.CostEstimate(
            flops=16 * HD * pairs, bytes_accessed=8 * resp_q.size, transcendentals=pairs
        ),
        name="attention",
    )(lengths, resp_q, grad_out, sent, got, own, far)

    def rows_of_tokens(name, column, scale, stored):
        per_kv = units // kv_heads
        return pl.pallas_call(
            functools.partial(product_kernel, tokens, per_kv, column, scale),
            grid=(units,),
            in_specs=[
                pl.BlockSpec((1, total_keys, rows), lambda u: (u, 0, 0)),
                pl.BlockSpec((1, 8, rows), lambda u: (u, 0, 0)),
            ]
            + whole(4),
            out_specs=pl.BlockSpec((rows, HD), lambda u: (u % halves, u // halves)),
            out_shape=jax.ShapeDtypeStruct(resp_q.shape, BF16),
            scratch_shapes=[pltpu.VMEM((kv_heads, HD, total_keys), BF16)],
            compiler_params=pltpu.CompilerParams(vmem_limit_bytes=48 << 20),
            cost_estimate=pl.CostEstimate(
                flops=8 * HD * pairs, bytes_accessed=2 * pairs, transcendentals=0
            ),
            name=name,
        )(stored, inverses, sent, got, own, far)

    resp_out = rows_of_tokens("output", HD, 1.0, weights)
    grad_q = rows_of_tokens("grad_query", 0, 1.0 / math.sqrt(HD), slopes)
    return resp_out, grad_q, kept, back


def product_kernel(
    tokens, per_kv, column, scale, stored_ref, inv_ref, sent_ref, got_ref, own_ref, far_ref,
    out_ref, rows_t,
):
    kv_heads, total_keys = rows_t.shape[0], rows_t.shape[2]
    index = pl.program_id(0)

    @pl.when(index == 0)
    def _():
        for n in range(kv_heads):
            cols = slice(2 * n * HD + column, 2 * n * HD + column + HD)
            for ref, start, size, at in kv_pieces(
                tokens, total_keys, sent_ref, got_ref, own_ref, far_ref
            ):
                rows_t[n, :, at : at + size] = ref[start : start + size, cols].T

    out = dot(rows_t[index // per_kv], stored_ref[0])
    out_ref[...] = (out * (inv_ref[0, :1] * scale)).astype(BF16).T


def swap_heads(array, by):
    devices = lax.axis_size("head")
    return lax.ppermute(array, "head", [(i, i ^ by) for i in range(devices)])


def swap_chips(array, by):
    devices = lax.axis_size("seq")
    return lax.ppermute(array, "seq", [(i, i ^ (by * CORES)) for i in range(devices)])


def swap_cores(array):
    devices = lax.axis_size("seq")
    return lax.ppermute(array, "seq", [(i, i ^ 1) for i in range(devices)])


def shift_chips(array, by):
    devices = lax.axis_size("seq")
    by = by * CORES
    return lax.ppermute(array, "seq", [(i, i + by) for i in range(devices) if 0 <= i + by < devices])


def shards(prompt_k, prompt_v, resp_q, resp_k, resp_v, grad_out, resp_lengths):
    tokens, kv_cols = resp_k.shape
    wide = 2 * kv_cols
    groups = lax.axis_size("head")
    chips = lax.axis_size("seq") // CORES
    block = prompt_k.shape[0]
    core = lax.rem(lax.axis_index("seq"), CORES)

    *pieces, own = pack([prompt_k, prompt_v, resp_k, resp_v], groups)
    pieces = [pieces[0]] + [swap_heads(pieces[k], k) for k in range(1, groups)]
    near = shift_chips(own, 1)
    far = shift_chips(own, 2)
    pieces[1:], near, far = lax.optimization_barrier((pieces[1:], near, far))
    mine = jnp.concatenate(pieces, axis=0)
    parts = [mine] + [swap_chips(mine, k) for k in range(1, chips)]
    chosen = jnp.where(core == 1, far, own)
    sent = jnp.concatenate(parts + [near, chosen], axis=0)
    got = swap_cores(sent)

    resp_out, grad_q, kept, back = attention(
        resp_lengths, resp_q, grad_out, sent, got, own, far
    )

    back = swap_cores(back)
    share = groups * block
    *parts, own = local_call(
        functools.partial(merge_kernel, chips, tokens),
        "merge",
        [kept, back],
        [((share, wide), BF16)] * chips
        + [((tokens // 2, wide), BF16)] * 4
        + [((tokens, wide), F32)],
    )
    near, far, parts = parts[chips : chips + 2], parts[chips + 2 :], parts[:chips]
    parts = [parts[0]] + [swap_chips(parts[k], k) for k in range(1, chips)]
    near = [shift_chips(part, -1) for part in near]
    far = [shift_chips(part, -2) for part in far]
    pieces = local_call(
        functools.partial(sum_kernel, chips),
        "sum_chips",
        parts,
        [((block, wide), BF16)] * groups,
        [pltpu.VMEM((share, wide), F32)],
    )
    pieces = [pieces[0]] + [swap_heads(pieces[k], k) for k in range(1, groups)]
    grad_k_prompt, grad_v_prompt, grad_k_resp, grad_v_resp = local_call(
        finish_kernel,
        "finish",
        [own] + near + far + pieces,
        [(prompt_k.shape, BF16)] * 2 + [((tokens, kv_cols), BF16)] * 2,
    )
    return (resp_out, grad_q, grad_k_resp, grad_v_resp, grad_k_prompt, grad_v_prompt)


def solution(mesh):
    placed = (
        P(("seq", "head"), None),
        P(("seq", "head"), None),
        P("seq", "head"),
        P("seq", "head"),
        P("seq", "head"),
        P("seq", "head"),
        P(),
    )
    return jax.shard_map(
        shards,
        mesh=mesh,
        in_specs=placed,
        out_specs=(
            P("seq", "head"),
            P("seq", "head"),
            P("seq", "head"),
            P("seq", "head"),
            P(("seq", "head"), None),
            P(("seq", "head"), None),
        ),
        check_vma=False,
    )
```

```python
import functools
import math

import jax
import jax.numpy as jnp
from jax import lax
from jax.experimental import pallas as pl
from jax.experimental.pallas import tpu as pltpu
from jax.sharding import PartitionSpec as P

HD = 128
CORES = 2
FAR = 4
CHUNK = 256
LONGER = 640
SAFE_SCORE = 40.0
TILE = 64
MOST_SCORES = 2560 * 256
NEG = -1e30
BF16 = jnp.bfloat16
F32 = jnp.float32


def dot(a, b):
    return jnp.dot(a, b, preferred_element_type=F32)


def whole(count):
    return [pl.BlockSpec(memory_space=pltpu.VMEM)] * count


def local_call(kernel, name, inputs, outputs, scratch=()):
    return pl.pallas_call(
        kernel,
        in_specs=whole(len(inputs)),
        out_specs=whole(len(outputs)),
        out_shape=[jax.ShapeDtypeStruct(shape, kind) for shape, kind in outputs],
        scratch_shapes=list(scratch),
        compiler_params=pltpu.CompilerParams(vmem_limit_bytes=40 * 1024 * 1024),
        name=name,
    )(*inputs)


def pack_kernel(pk_ref, pv_ref, rk_ref, rv_ref, *outs):
    pieces, resp = outs[:-1], outs[-1]
    head = lax.axis_index("head")
    width = pieces[0].shape[1]
    for k, piece in enumerate(pieces):
        start = pl.multiple_of((head ^ k) * (width // 2), HD)
        for n in range(width // (2 * HD)):
            at = pl.multiple_of(start + n * HD, HD)
            piece[:, 2 * n * HD : (2 * n + 1) * HD] = pk_ref[:, pl.ds(at, HD)]
            piece[:, (2 * n + 1) * HD : (2 * n + 2) * HD] = pv_ref[:, pl.ds(at, HD)]
    for n in range(width // (2 * HD)):
        resp[:, 2 * n * HD : (2 * n + 1) * HD] = rk_ref[:, n * HD : (n + 1) * HD]
        resp[:, (2 * n + 1) * HD : (2 * n + 2) * HD] = rv_ref[:, n * HD : (n + 1) * HD]


def pack(inputs, groups):
    def one(array):
        return pl.BlockSpec(array.shape, lambda i: (0, 0))

    block, tokens = inputs[0].shape[0], inputs[2].shape[0]
    wide = 2 * inputs[2].shape[1]
    shapes = [(block, wide)] * groups + [(tokens, wide)]
    return pl.pallas_call(
        pack_kernel,
        grid=(1,),
        in_specs=[one(array) for array in inputs],
        out_specs=whole(groups + 1),
        out_shape=[jax.ShapeDtypeStruct(shape, BF16) for shape in shapes],
        compiler_params=pltpu.CompilerParams(vmem_limit_bytes=56 * 1024 * 1024),
        name="pack",
    )(*inputs)


def merge_kernel(parts, rows, kept_ref, got_ref, *outs):
    pieces, back1, back2, own = outs[:parts], outs[parts:-3], outs[-3:-1], outs[-1]
    core = lax.rem(lax.axis_index("seq"), CORES)
    to_own = jnp.where(core == 0, 1.0, 0.0)
    half = kept_ref.shape[0] - 3 * rows
    share = half // parts
    for k, piece in enumerate(pieces):
        at = slice(k * share, (k + 1) * share)
        piece[...] = (kept_ref[at] + got_ref[at].astype(F32)).astype(BF16)
    one, two, three = half + rows, half + 2 * rows, half + 3 * rows
    near = (kept_ref[half:one] + got_ref[half:one].astype(F32)).astype(BF16)
    chosen = got_ref[one:two].astype(F32)
    far = (kept_ref[one:two] + chosen * (1.0 - to_own)).astype(BF16)
    for i in range(2):
        back1[i][...] = near[i * rows // 2 : (i + 1) * rows // 2]
        back2[i][...] = far[i * rows // 2 : (i + 1) * rows // 2]
    own[...] = kept_ref[two:three] + chosen * to_own


def sum_kernel(parts, *refs):
    ins, outs, total = refs[:parts], refs[parts:-1], refs[-1]
    acc = ins[0][...].astype(F32)
    for ref in ins[1:]:
        acc = acc + ref[...].astype(F32)
    total[...] = acc
    share = total.shape[0] // len(outs)
    for k, out in enumerate(outs):
        out[...] = total[k * share : (k + 1) * share].astype(BF16)


def finish_kernel(own_ref, *refs):
    near, far, pieces, (gk_ref, gv_ref, rk_ref, rv_ref) = refs[:2], refs[2:4], refs[4:-4], refs[-4:]
    head = lax.axis_index("head")
    width = pieces[0].shape[1]
    for k, piece in enumerate(pieces):
        start = pl.multiple_of((head ^ k) * (width // 2), HD)
        for n in range(width // (2 * HD)):
            at = pl.multiple_of(start + n * HD, HD)
            gk_ref[:, pl.ds(at, HD)] = piece[:, 2 * n * HD : (2 * n + 1) * HD]
            gv_ref[:, pl.ds(at, HD)] = piece[:, (2 * n + 1) * HD : (2 * n + 2) * HD]
    rows = near[0].shape[0]
    for i in range(2):
        at = slice(i * rows, (i + 1) * rows)
        total = own_ref[at] + near[i][...].astype(F32) + far[i][...].astype(F32)
        total = total.astype(BF16)
        for n in range(width // (2 * HD)):
            rk_ref[at, n * HD : (n + 1) * HD] = total[:, 2 * n * HD : (2 * n + 1) * HD]
            rv_ref[at, n * HD : (n + 1) * HD] = total[:, (2 * n + 1) * HD : (2 * n + 2) * HD]


def attention_kernel(
    halves, lengths, q_ref, do_ref, sent_ref, got_ref, own_ref, far_ref,
    o_ref, dq_ref, kept_ref, back_ref,
    bias, keys, values, keys_t, values_t, s_buf, p_bufs, d_bufs, inv_bufs,
    q_ts, cot_ts, q_ns, cot_ns, dk, dv,
):
    kv_heads, total_keys = keys.shape[0], keys.shape[1]
    tokens, q_cols = q_ref.shape
    rows = tokens // halves
    prompt_len = total_keys - 5 * tokens
    half = prompt_len // 2
    steps = q_cols // HD * halves // 2
    steps_per_kv = steps // kv_heads
    score_scale = 1.0 / math.sqrt(HD)
    exp_scale = score_scale * math.log2(math.e)
    resp_at = [prompt_len + i * tokens for i in range(6)]
    chunks = [slice(at, at + CHUNK) for at in range(0, total_keys, CHUNK)]
    longer = [slice(at, at + LONGER) for at in range(0, total_keys, LONGER)]
    cuts = [slice(at, at + total_keys // 2) for at in (0, total_keys // 2)]

    def place_of(which, step):
        head = step * 2 + which if halves == 1 else step
        row = 0 if halves == 1 else which * rows
        return slice(row, row + rows), pl.ds(pl.multiple_of(head * HD, HD), HD)

    def kv_of(step):
        return jnp.clip(step // steps_per_kv, 0, kv_heads - 1)

    def bias_at(which, at, size):
        row = which * rows * (halves - 1)
        return bias[at - prompt_len : at - prompt_len + size, row : row + rows]

    def folded(x):
        return x.reshape(x.shape[0] // 8, 8, rows)

    def within(at):
        return [slice(start, start + TILE) for start in range(at.start, at.stop, TILE)]

    def weigh(which, step, fast):
        kv = kv_of(step)
        where = place_of(which, step)
        state = {"sum": jnp.zeros((8, rows), F32)}

        def lift():
            q_ts[which] = q_ref[where].T
            cot_ts[which] = do_ref[where].T

        def masked(s, at, tile):
            s = s[tile.start - at.start : tile.stop - at.start]
            return s if tile.start < prompt_len else s + bias_at(which, tile.start, TILE)

        def put(tile, p):
            state["sum"] = state["sum"] + jnp.sum(folded(p), axis=0)
            p_bufs[which, tile] = p.astype(BF16)

        def direct(at):
            s = dot(keys[kv, at], q_ts[which])
            for tile in within(at):
                put(tile, jnp.exp2(masked(s, at, tile) * exp_scale))

        def highest(at):
            s = dot(keys[kv, at], q_ts[which])
            for tile in within(at):
                part = masked(s, at, tile)
                s_buf[tile] = part
                top = jnp.max(folded(part), axis=0)
                state["top"] = jnp.maximum(state["top"], top) if "top" in state else top

        def settle():
            state["top"] = jnp.max(state["top"], axis=0, keepdims=True) * exp_scale

        def reduced(at):
            for tile in within(at):
                put(tile, jnp.exp2(s_buf[tile] * exp_scale - state["top"]))

        def finish():
            inverse = 1.0 / jnp.sum(state["sum"], axis=0, keepdims=True)
            inv_bufs[which] = jnp.broadcast_to(inverse, (8, rows))
            q_ns[which] = (q_ts[which].astype(F32) * inverse).astype(BF16).T
            cot_ns[which] = (cot_ts[which].astype(F32) * inverse).astype(BF16).T

        if fast:
            return [lift] + [functools.partial(direct, at) for at in chunks], finish
        work = [lift] + [functools.partial(highest, at) for at in chunks] + [settle]
        return work + [functools.partial(reduced, at) for at in chunks], finish

    def settled(which, step, state):
        kv = kv_of(step)
        where = place_of(which, jnp.maximum(step, 0))

        def output(at):
            more = dot(values_t[kv, :, at], p_bufs[which, at])
            state["out"] = state["out"] + more if "out" in state else more

        def put():
            out = (state["out"] * inv_bufs[which, :1]).astype(BF16)
            o_ref[where] = out.T
            wide = cot_ts[which].astype(F32)
            state["delta"] = jnp.sum(wide * out.astype(F32), axis=0, keepdims=True)

        return [functools.partial(output, at) for at in cuts] + [put]

    def slopes(which, step, state):
        kv = kv_of(step)

        def slope(at):
            grads = dot(values[kv, at], cot_ts[which])
            for tile in within(at):
                part = grads[tile.start - at.start : tile.stop - at.start] - state["delta"]
                d_bufs[which, tile] = p_bufs[which, tile] * part.astype(BF16)

        return [functools.partial(slope, at) for at in chunks]

    def value_grads(which, step):
        kv = kv_of(step)

        def value_grad(at):
            dv[kv, at] += dot(p_bufs[which, at], cot_ns[which])

        return [functools.partial(value_grad, at) for at in longer]

    def key_grads(which, step):
        kv = kv_of(step)

        def key_grad(at):
            dk[kv, at] += dot(d_bufs[which, at], q_ns[which])

        return [functools.partial(key_grad, at) for at in longer]

    def query_grads(which, step):
        kv = kv_of(step)
        where = place_of(which, jnp.maximum(step, 0))
        state = {}

        def query(at):
            more = dot(keys_t[kv, :, at], d_bufs[which, at])
            state["dq"] = state["dq"] + more if "dq" in state else more

        def put():
            dq = state["dq"] * (inv_bufs[which, :1] * score_scale)
            dq_ref[where] = dq.astype(BF16).T

        return [functools.partial(query, at) for at in cuts] + [put]

    def slot(which, step, fast):
        before, before_step = 1 - which, step - 1 + which
        state = {}
        work, finish = weigh(which, step, fast)
        late = key_grads(which, step - 1)
        first = settled(before, before_step, state) + query_grads(which, step - 1)
        together(work, first + late[: len(late) // 2])
        together(
            slopes(before, before_step, state),
            late[len(late) // 2 :] + value_grads(before, before_step),
        )
        finish()

    def together(vector, matrix):
        done = 0
        for i, work in enumerate(vector):
            work()
            while done * len(vector) < (i + 1) * len(matrix):
                matrix[done]()
                done += 1

    place = lax.axis_index("seq")
    core = lax.rem(place, CORES)
    first_row = place * tokens
    row_pos = first_row + lax.broadcasted_iota(jnp.int32, (8, tokens), 1)
    seg_start = jnp.zeros((8, tokens), jnp.int32)
    end = jnp.int32(0)
    for i in range(lengths.shape[0]):
        end = end + lengths[i]
        seg_start = jnp.where(row_pos >= end, end, seg_start)
    seg_start, row_pos = seg_start[:1], row_pos[:1]
    near = 1 + 2 * core
    for i, distance in enumerate((0, 2, FAR, near, 4 - near)):
        for row in range(0, tokens, TILE):
            key_pos = (first_row - distance * tokens + row) + lax.broadcasted_iota(
                jnp.int32, (TILE, tokens), 0
            )
            allowed = (key_pos >= seg_start) & (key_pos <= row_pos)
            at = i * tokens + row
            bias[at : at + TILE] = jnp.where(allowed, 0.0, NEG)
    for n in range(kv_heads):
        k_at, v_at = 2 * n * HD, (2 * n + 1) * HD
        for ref, start, size, at in (
            (sent_ref, 0, half, 0),
            (got_ref, 0, half, half),
            (own_ref, 0, tokens, resp_at[0]),
            (sent_ref, half, tokens, resp_at[1]),
            (far_ref, 0, tokens, resp_at[2]),
            (got_ref, half, tokens, resp_at[3]),
            (got_ref, half + tokens, tokens, resp_at[4]),
        ):
            k_rows = ref[start : start + size, k_at : k_at + HD]
            v_rows = ref[start : start + size, v_at : v_at + HD]
            keys[n, at : at + size] = k_rows
            values[n, at : at + size] = v_rows
            keys_t[n, :, at : at + size] = k_rows.T
            values_t[n, :, at : at + size] = v_rows.T
    dk[...] = jnp.zeros_like(dk)
    dv[...] = jnp.zeros_like(dv)
    p_bufs[1] = jnp.zeros(p_bufs.shape[1:], BF16)
    cot_ts[1] = jnp.zeros(cot_ts.shape[1:], BF16)
    for ref in (d_bufs, inv_bufs, q_ns, cot_ns):
        ref[...] = jnp.zeros_like(ref)
    q_most = jnp.zeros((tokens, 1), F32)
    for at in range(0, q_cols, HD):
        part = q_ref[:, at : at + HD].astype(F32)
        q_most = jnp.maximum(q_most, jnp.sum(part * part, axis=1, keepdims=True))
    k_most = jnp.zeros((CHUNK, 1), F32)
    for n in range(kv_heads):
        for at in chunks:
            part = keys[n, at].astype(F32)
            k_most = jnp.maximum(k_most, jnp.sum(part * part, axis=1, keepdims=True))
    most = jnp.max(q_most) * jnp.max(k_most) * (score_scale * score_scale)
    small = most <= SAFE_SCORE * SAFE_SCORE
    def run(fast):
        def pair(step, carry):
            slot(0, step, fast)
            slot(1, step, fast)
            return carry

        lax.fori_loop(0, steps, pair, 0)

    pl.when(small)(functools.partial(run, True))
    pl.when(jnp.logical_not(small))(functools.partial(run, False))
    state = {}
    for work in settled(1, steps - 1, state) + query_grads(0, steps - 1):
        work()
    together(
        slopes(1, steps - 1, state), key_grads(0, steps - 1) + value_grads(1, steps - 1)
    )
    for work in key_grads(1, steps - 1) + query_grads(1, steps - 1):
        work()
    for n in range(kv_heads):
        k_cols = slice(2 * n * HD, (2 * n + 1) * HD)
        v_cols = slice((2 * n + 1) * HD, (2 * n + 2) * HD)
        for ref, start, size, at in (
            (kept_ref, 0, half, 0),
            (back_ref, 0, half, half),
            (kept_ref, half + 2 * tokens, tokens, resp_at[0]),
            (kept_ref, half, tokens, resp_at[1]),
            (kept_ref, half + tokens, tokens, resp_at[2]),
            (back_ref, half, tokens, resp_at[3]),
            (back_ref, half + tokens, tokens, resp_at[4]),
        ):
            grad_k = dk[n, at : at + size] * score_scale
            ref[start : start + size, k_cols] = grad_k.astype(ref.dtype)
            ref[start : start + size, v_cols] = dv[n, at : at + size].astype(ref.dtype)


def attention(lengths, resp_q, grad_out, sent, got, own, far):
    tokens = resp_q.shape[0]
    half = sent.shape[0] - 2 * tokens
    total_keys = 2 * half + 5 * tokens
    kv_heads = sent.shape[1] // (2 * HD)
    q_heads = resp_q.shape[1] // HD
    halves = 1 if tokens * total_keys <= MOST_SCORES else 2
    rows = tokens // halves
    pairs = tokens * q_heads * total_keys
    return pl.pallas_call(
        functools.partial(attention_kernel, halves),
        in_specs=[pl.BlockSpec(memory_space=pltpu.SMEM)] + whole(6),
        out_specs=whole(4),
        out_shape=[
            jax.ShapeDtypeStruct(resp_q.shape, BF16),
            jax.ShapeDtypeStruct(resp_q.shape, BF16),
            jax.ShapeDtypeStruct((half + 3 * tokens, sent.shape[1]), F32),
            jax.ShapeDtypeStruct((half + 2 * tokens, sent.shape[1]), BF16),
        ],
        scratch_shapes=[
            pltpu.VMEM((5 * tokens, tokens), F32),
            pltpu.VMEM((kv_heads, total_keys, HD), BF16),
            pltpu.VMEM((kv_heads, total_keys, HD), BF16),
            pltpu.VMEM((kv_heads, HD, total_keys), BF16),
            pltpu.VMEM((kv_heads, HD, total_keys), BF16),
            pltpu.VMEM((total_keys, rows), F32),
            pltpu.VMEM((2, total_keys, rows), BF16),
            pltpu.VMEM((2, total_keys, rows), BF16),
            pltpu.VMEM((2, 8, rows), F32),
            pltpu.VMEM((2, HD, rows), BF16),
            pltpu.VMEM((2, HD, rows), BF16),
            pltpu.VMEM((2, rows, HD), BF16),
            pltpu.VMEM((2, rows, HD), BF16),
            pltpu.VMEM((kv_heads, total_keys, HD), F32),
            pltpu.VMEM((kv_heads, total_keys, HD), F32),
        ],
        compiler_params=pltpu.CompilerParams(vmem_limit_bytes=(36 if halves == 1 else 48) << 20),
        cost_estimate=pl.CostEstimate(
            flops=12 * HD * pairs, bytes_accessed=8 * resp_q.size, transcendentals=pairs
        ),
        name="attention",
    )(lengths, resp_q, grad_out, sent, got, own, far)


def swap_heads(array, by):
    devices = lax.axis_size("head")
    return lax.ppermute(array, "head", [(i, i ^ by) for i in range(devices)])


def swap_chips(array, by):
    devices = lax.axis_size("seq")
    return lax.ppermute(array, "seq", [(i, i ^ (by * CORES)) for i in range(devices)])


def swap_cores(array):
    devices = lax.axis_size("seq")
    return lax.ppermute(array, "seq", [(i, i ^ 1) for i in range(devices)])


def shift_chips(array, by):
    devices = lax.axis_size("seq")
    by = by * CORES
    return lax.ppermute(array, "seq", [(i, i + by) for i in range(devices) if 0 <= i + by < devices])


def shards(prompt_k, prompt_v, resp_q, resp_k, resp_v, grad_out, resp_lengths):
    tokens, kv_cols = resp_k.shape
    wide = 2 * kv_cols
    groups = lax.axis_size("head")
    chips = lax.axis_size("seq") // CORES
    block = prompt_k.shape[0]
    core = lax.rem(lax.axis_index("seq"), CORES)

    *pieces, own = pack([prompt_k, prompt_v, resp_k, resp_v], groups)
    pieces = [pieces[0]] + [swap_heads(pieces[k], k) for k in range(1, groups)]
    near = shift_chips(own, 1)
    far = shift_chips(own, 2)
    pieces[1:], near, far = lax.optimization_barrier((pieces[1:], near, far))
    mine = jnp.concatenate(pieces, axis=0)
    parts = [mine] + [swap_chips(mine, k) for k in range(1, chips)]
    chosen = jnp.where(core == 1, far, own)
    sent = jnp.concatenate(parts + [near, chosen], axis=0)
    got = swap_cores(sent)

    resp_out, grad_q, kept, back = attention(
        resp_lengths, resp_q, grad_out, sent, got, own, far
    )

    back = swap_cores(back)
    share = groups * block
    *parts, own = local_call(
        functools.partial(merge_kernel, chips, tokens),
        "merge",
        [kept, back],
        [((share, wide), BF16)] * chips
        + [((tokens // 2, wide), BF16)] * 4
        + [((tokens, wide), F32)],
    )
    near, far, parts = parts[chips : chips + 2], parts[chips + 2 :], parts[:chips]
    parts = [parts[0]] + [swap_chips(parts[k], k) for k in range(1, chips)]
    near = [shift_chips(part, -1) for part in near]
    far = [shift_chips(part, -2) for part in far]
    pieces = local_call(
        functools.partial(sum_kernel, chips),
        "sum_chips",
        parts,
        [((block, wide), BF16)] * groups,
        [pltpu.VMEM((share, wide), F32)],
    )
    pieces = [pieces[0]] + [swap_heads(pieces[k], k) for k in range(1, groups)]
    grad_k_prompt, grad_v_prompt, grad_k_resp, grad_v_resp = local_call(
        finish_kernel,
        "finish",
        [own] + near + far + pieces,
        [(prompt_k.shape, BF16)] * 2 + [((tokens, kv_cols), BF16)] * 2,
    )
    return (resp_out, grad_q, grad_k_resp, grad_v_resp, grad_k_prompt, grad_v_prompt)


def solution(mesh):
    placed = (
        P(("seq", "head"), None),
        P(("seq", "head"), None),
        P("seq", "head"),
        P("seq", "head"),
        P("seq", "head"),
        P("seq", "head"),
        P(),
    )
    return jax.shard_map(
        shards,
        mesh=mesh,
        in_specs=placed,
        out_specs=(
            P("seq", "head"),
            P("seq", "head"),
            P("seq", "head"),
            P("seq", "head"),
            P(("seq", "head"), None),
            P(("seq", "head"), None),
        ),
        check_vma=False,
    )
```

```python
import functools
import math

import jax
import jax.numpy as jnp
from jax import lax
from jax.experimental import pallas as pl
from jax.experimental.pallas import tpu as pltpu
from jax.sharding import PartitionSpec as P

HD = 128
CORES = 2
FAR = 4
CHUNK = 256
LONGER = 640
SAFE_SCORE = 40.0
TILE = 64
MOST_SCORES = 2560 * 256
NEG = -1e30
BF16 = jnp.bfloat16
F32 = jnp.float32


def dot(a, b):
    return jnp.dot(a, b, preferred_element_type=F32)


def whole(count):
    return [pl.BlockSpec(memory_space=pltpu.VMEM)] * count


def local_call(kernel, name, inputs, outputs, scratch=(), scalars=0):
    return pl.pallas_call(
        kernel,
        in_specs=[pl.BlockSpec(memory_space=pltpu.SMEM)] * scalars + whole(len(inputs) - scalars),
        out_specs=whole(len(outputs)),
        out_shape=[jax.ShapeDtypeStruct(shape, kind) for shape, kind in outputs],
        scratch_shapes=list(scratch),
        compiler_params=pltpu.CompilerParams(vmem_limit_bytes=40 * 1024 * 1024),
        name=name,
    )(*inputs)


def pack_kernel(pk_ref, pv_ref, rk_ref, rv_ref, *outs):
    pieces, resp = outs[:-1], outs[-1]
    head = lax.axis_index("head")
    width = pieces[0].shape[1]
    for k, piece in enumerate(pieces):
        start = pl.multiple_of((head ^ k) * (width // 2), HD)
        for n in range(width // (2 * HD)):
            at = pl.multiple_of(start + n * HD, HD)
            piece[:, 2 * n * HD : (2 * n + 1) * HD] = pk_ref[:, pl.ds(at, HD)]
            piece[:, (2 * n + 1) * HD : (2 * n + 2) * HD] = pv_ref[:, pl.ds(at, HD)]
    for n in range(width // (2 * HD)):
        resp[:, 2 * n * HD : (2 * n + 1) * HD] = rk_ref[:, n * HD : (n + 1) * HD]
        resp[:, (2 * n + 1) * HD : (2 * n + 2) * HD] = rv_ref[:, n * HD : (n + 1) * HD]


def pack(inputs, groups):
    def one(array):
        return pl.BlockSpec(array.shape, lambda i: (0, 0))

    block, tokens = inputs[0].shape[0], inputs[2].shape[0]
    wide = 2 * inputs[2].shape[1]
    shapes = [(block, wide)] * groups + [(tokens, wide)]
    return pl.pallas_call(
        pack_kernel,
        grid=(1,),
        in_specs=[one(array) for array in inputs],
        out_specs=whole(groups + 1),
        out_shape=[jax.ShapeDtypeStruct(shape, BF16) for shape in shapes],
        compiler_params=pltpu.CompilerParams(vmem_limit_bytes=56 * 1024 * 1024),
        name="pack",
    )(*inputs)


def merge_kernel(parts, rows, kept_ref, got_ref, *outs):
    pieces, back1, back2, own = outs[:parts], outs[parts:-3], outs[-3:-1], outs[-1]
    core = lax.rem(lax.axis_index("seq"), CORES)
    to_own = jnp.where(core == 0, 1.0, 0.0)
    half = kept_ref.shape[0] - 3 * rows
    share = half // parts
    for k, piece in enumerate(pieces):
        at = slice(k * share, (k + 1) * share)
        piece[...] = (kept_ref[at] + got_ref[at].astype(F32)).astype(BF16)
    one, two, three = half + rows, half + 2 * rows, half + 3 * rows
    near = (kept_ref[half:one] + got_ref[half:one].astype(F32)).astype(BF16)
    chosen = got_ref[one:two].astype(F32)
    far = (kept_ref[one:two] + chosen * (1.0 - to_own)).astype(BF16)
    for i in range(2):
        back1[i][...] = near[i * rows // 2 : (i + 1) * rows // 2]
        back2[i][...] = far[i * rows // 2 : (i + 1) * rows // 2]
    own[...] = kept_ref[two:three] + chosen * to_own


def sum_kernel(parts, *refs):
    ins, outs, total = refs[:parts], refs[parts:-1], refs[-1]
    acc = ins[0][...].astype(F32)
    for ref in ins[1:]:
        acc = acc + ref[...].astype(F32)
    total[...] = acc
    share = total.shape[0] // len(outs)
    for k, out in enumerate(outs):
        out[...] = total[k * share : (k + 1) * share].astype(BF16)


def finish_kernel(own_ref, *refs):
    near, far, pieces, (gk_ref, gv_ref, rk_ref, rv_ref) = refs[:2], refs[2:4], refs[4:-4], refs[-4:]
    head = lax.axis_index("head")
    width = pieces[0].shape[1]
    for k, piece in enumerate(pieces):
        start = pl.multiple_of((head ^ k) * (width // 2), HD)
        for n in range(width // (2 * HD)):
            at = pl.multiple_of(start + n * HD, HD)
            gk_ref[:, pl.ds(at, HD)] = piece[:, 2 * n * HD : (2 * n + 1) * HD]
            gv_ref[:, pl.ds(at, HD)] = piece[:, (2 * n + 1) * HD : (2 * n + 2) * HD]
    rows = near[0].shape[0]
    for i in range(2):
        at = slice(i * rows, (i + 1) * rows)
        total = own_ref[at] + near[i][...].astype(F32) + far[i][...].astype(F32)
        total = total.astype(BF16)
        for n in range(width // (2 * HD)):
            rk_ref[at, n * HD : (n + 1) * HD] = total[:, 2 * n * HD : (2 * n + 1) * HD]
            rv_ref[at, n * HD : (n + 1) * HD] = total[:, (2 * n + 1) * HD : (2 * n + 2) * HD]


def mask_kernel(lengths, q_ref, bias, most_ref):
    tokens, q_cols = q_ref.shape
    place = lax.axis_index("seq")
    core = lax.rem(place, CORES)
    first_row = place * tokens
    row_pos = first_row + lax.broadcasted_iota(jnp.int32, (8, tokens), 1)
    seg_start = jnp.zeros((8, tokens), jnp.int32)
    end = jnp.int32(0)
    for i in range(lengths.shape[0]):
        end = end + lengths[i]
        seg_start = jnp.where(row_pos >= end, end, seg_start)
    seg_start, row_pos = seg_start[:1], row_pos[:1]
    near = 1 + 2 * core
    for i, distance in enumerate((0, 2, FAR, near, 4 - near)):
        for row in range(0, tokens, TILE):
            key_pos = (first_row - distance * tokens + row) + lax.broadcasted_iota(
                jnp.int32, (TILE, tokens), 0
            )
            allowed = (key_pos >= seg_start) & (key_pos <= row_pos)
            at = i * tokens + row
            bias[at : at + TILE] = jnp.where(allowed, 0.0, NEG)
    most = jnp.zeros((tokens, 1), F32)
    for at in range(0, q_cols, HD):
        part = q_ref[:, at : at + HD].astype(F32)
        most = jnp.maximum(most, jnp.sum(part * part, axis=1, keepdims=True))
    most_ref[...] = jnp.broadcast_to(jnp.max(most, axis=0, keepdims=True), most_ref.shape)


def largest(ref, most, cols):
    for at in range(0, ref.shape[0], HD):
        part = ref[at : at + HD, cols].astype(F32)
        most = jnp.maximum(most, jnp.sum(part * part, axis=1, keepdims=True))
    return most


def turn_kernel(kv_heads, sent_ref, own_ref, far_ref, turned, most_ref):
    tokens = own_ref.shape[0]
    most = jnp.zeros((HD, 1), F32)
    for n in range(2 * kv_heads):
        cols = slice(n * HD, (n + 1) * HD)
        at = 0
        for ref, size in ((sent_ref, sent_ref.shape[0] - tokens), (far_ref, tokens), (own_ref, tokens)):
            turned[n, :, at : at + size] = ref[:size, cols].T
            at += size
            if n % 2 == 0:
                most = largest(ref, most, cols)
    most_ref[...] = jnp.broadcast_to(jnp.max(most, axis=0, keepdims=True), most_ref.shape)


def attention_kernel(
    halves, q_ref, do_ref, sent_ref, got_ref, own_ref, far_ref,
    bias, turned, q_most, k_most,
    o_ref, dq_ref, kept_ref, back_ref,
    keys, values, keys_t, values_t, s_buf, p_bufs, d_bufs, inv_bufs,
    q_ts, cot_ts, q_ns, cot_ns, dk, dv,
):
    kv_heads, total_keys = keys.shape[0], keys.shape[1]
    tokens, q_cols = q_ref.shape
    rows = tokens // halves
    prompt_len = total_keys - 5 * tokens
    half = prompt_len // 2
    steps = q_cols // HD * halves // 2
    steps_per_kv = steps // kv_heads
    score_scale = 1.0 / math.sqrt(HD)
    exp_scale = score_scale * math.log2(math.e)
    resp_at = [prompt_len + i * tokens for i in range(6)]
    chunks = [slice(at, at + CHUNK) for at in range(0, total_keys, CHUNK)]
    longer = [slice(at, at + LONGER) for at in range(0, total_keys, LONGER)]
    cuts = [slice(at, at + total_keys // 2) for at in (0, total_keys // 2)]

    def columns(head):
        if isinstance(head, int):
            return slice(head * HD, (head + 1) * HD)
        return pl.ds(pl.multiple_of(head * HD, HD), HD)

    def place_of(which, step):
        head = step * 2 + which if halves == 1 else step
        row = 0 if halves == 1 else which * rows
        return slice(row, row + rows), columns(head)

    def kv_of(step):
        return step // steps_per_kv

    def bias_at(which, at, size):
        row = which * rows * (halves - 1)
        return bias[at - prompt_len : at - prompt_len + size, row : row + rows]

    def folded(x):
        return x.reshape(x.shape[0] // 8, 8, rows)

    def within(at):
        return [slice(start, start + TILE) for start in range(at.start, at.stop, TILE)]

    def weigh(which, step, fast):
        kv = kv_of(step)
        where = place_of(which, step)
        state = {"sum": jnp.zeros((8, rows), F32)}

        def lift():
            q_ts[which] = q_ref[where].T
            cot_ts[which] = do_ref[where].T

        def masked(s, at, tile):
            s = s[tile.start - at.start : tile.stop - at.start]
            return s if tile.start < prompt_len else s + bias_at(which, tile.start, TILE)

        def put(tile, p):
            state["sum"] = state["sum"] + jnp.sum(folded(p), axis=0)
            p_bufs[which, tile] = p.astype(BF16)

        def direct(at):
            s = dot(keys[kv, at], q_ts[which])
            for tile in within(at):
                put(tile, jnp.exp2(masked(s, at, tile) * exp_scale))

        def highest(at):
            s = dot(keys[kv, at], q_ts[which])
            for tile in within(at):
                part = masked(s, at, tile)
                s_buf[tile] = part
                top = jnp.max(folded(part), axis=0)
                state["top"] = jnp.maximum(state["top"], top) if "top" in state else top

        def settle():
            state["top"] = jnp.max(state["top"], axis=0, keepdims=True) * exp_scale

        def reduced(at):
            for tile in within(at):
                put(tile, jnp.exp2(s_buf[tile] * exp_scale - state["top"]))

        def finish():
            inverse = 1.0 / jnp.sum(state["sum"], axis=0, keepdims=True)
            inv_bufs[which] = jnp.broadcast_to(inverse, (8, rows))
            q_ns[which] = (q_ts[which].astype(F32) * inverse).astype(BF16).T
            cot_ns[which] = (cot_ts[which].astype(F32) * inverse).astype(BF16).T

        if fast:
            return [lift] + [functools.partial(direct, at) for at in chunks], finish
        work = [lift] + [functools.partial(highest, at) for at in chunks] + [settle]
        return work + [functools.partial(reduced, at) for at in chunks], finish

    def settled(which, step, state):
        kv = kv_of(step)
        where = place_of(which, step)

        def output(at):
            more = dot(values_t[kv, :, at], p_bufs[which, at])
            state["out"] = state["out"] + more if "out" in state else more

        def put():
            out = (state["out"] * inv_bufs[which, :1]).astype(BF16)
            o_ref[where] = out.T
            wide = cot_ts[which].astype(F32)
            state["delta"] = jnp.sum(wide * out.astype(F32), axis=0, keepdims=True)

        return [functools.partial(output, at) for at in cuts] + [put]

    def slopes(which, step, state):
        kv = kv_of(step)

        def slope(at):
            grads = dot(values[kv, at], cot_ts[which])
            for tile in within(at):
                part = grads[tile.start - at.start : tile.stop - at.start] - state["delta"]
                d_bufs[which, tile] = p_bufs[which, tile] * part.astype(BF16)

        return [functools.partial(slope, at) for at in chunks]

    def value_grads(which, step):
        kv = kv_of(step)

        def value_grad(at):
            dv[kv, at] += dot(p_bufs[which, at], cot_ns[which])

        return [functools.partial(value_grad, at) for at in longer]

    def key_grads(which, step):
        kv = kv_of(step)

        def key_grad(at):
            dk[kv, at] += dot(d_bufs[which, at], q_ns[which])

        return [functools.partial(key_grad, at) for at in longer]

    def query_grads(which, step):
        kv = kv_of(step)
        where = place_of(which, step)
        state = {}

        def query(at):
            more = dot(keys_t[kv, :, at], d_bufs[which, at])
            state["dq"] = state["dq"] + more if "dq" in state else more

        def put():
            dq = state["dq"] * (inv_bufs[which, :1] * score_scale)
            dq_ref[where] = dq.astype(BF16).T

        return [functools.partial(query, at) for at in cuts] + [put]

    def slot(which, step, fast):
        before, before_step = 1 - which, step - 1 + which
        state = {}
        work, finish = weigh(which, step, fast)
        started = not isinstance(step, int)
        late = key_grads(which, step - 1) if started else []
        first = query_grads(which, step - 1) if started else []
        if started or which == 1:
            first = settled(before, before_step, state) + first
        together(work, first + late[: len(late) // 2])
        if started or which == 1:
            together(
                slopes(before, before_step, state),
                late[len(late) // 2 :] + value_grads(before, before_step),
            )
        finish()

    def together(vector, matrix):
        done = 0
        for i, work in enumerate(vector):
            work()
            while done * len(vector) < (i + 1) * len(matrix):
                matrix[done]()
                done += 1

    most = jnp.zeros((HD, 1), F32)
    for n in range(kv_heads):
        k_cols = slice(2 * n * HD, (2 * n + 1) * HD)
        v_cols = slice((2 * n + 1) * HD, (2 * n + 2) * HD)
        for ref, start, size, at, turned_at in (
            (sent_ref, 0, half, 0, 0),
            (got_ref, 0, half, half, None),
            (own_ref, 0, tokens, resp_at[0], half + 2 * tokens),
            (sent_ref, half, tokens, resp_at[1], half),
            (far_ref, 0, tokens, resp_at[2], half + tokens),
            (got_ref, half, tokens, resp_at[3], None),
            (got_ref, half + tokens, tokens, resp_at[4], None),
        ):
            k_rows = ref[start : start + size, k_cols]
            v_rows = ref[start : start + size, v_cols]
            keys[n, at : at + size] = k_rows
            values[n, at : at + size] = v_rows
            if turned_at is None:
                keys_t[n, :, at : at + size] = k_rows.T
                values_t[n, :, at : at + size] = v_rows.T
            else:
                there = slice(turned_at, turned_at + size)
                keys_t[n, :, at : at + size] = turned[2 * n, :, there]
                values_t[n, :, at : at + size] = turned[2 * n + 1, :, there]
        most = largest(got_ref, most, k_cols)
    dk[...] = jnp.zeros_like(dk)
    dv[...] = jnp.zeros_like(dv)
    keys_most = jnp.maximum(jnp.max(most), jnp.max(k_most[...]))
    most = jnp.max(q_most[...]) * keys_most * (score_scale * score_scale)
    small = most <= SAFE_SCORE * SAFE_SCORE
    def run(fast):
        def pair(step, carry):
            slot(0, step, fast)
            slot(1, step, fast)
            return carry

        slot(0, 0, fast)
        slot(1, 0, fast)
        lax.fori_loop(1, steps, pair, 0)

    pl.when(small)(functools.partial(run, True))
    pl.when(jnp.logical_not(small))(functools.partial(run, False))
    state = {}
    for work in settled(1, steps - 1, state) + query_grads(0, steps - 1):
        work()
    together(
        slopes(1, steps - 1, state), key_grads(0, steps - 1) + value_grads(1, steps - 1)
    )
    for work in key_grads(1, steps - 1) + query_grads(1, steps - 1):
        work()
    for n in range(kv_heads):
        k_cols = slice(2 * n * HD, (2 * n + 1) * HD)
        v_cols = slice((2 * n + 1) * HD, (2 * n + 2) * HD)
        for ref, start, size, at in (
            (kept_ref, 0, half, 0),
            (back_ref, 0, half, half),
            (kept_ref, half + 2 * tokens, tokens, resp_at[0]),
            (kept_ref, half, tokens, resp_at[1]),
            (kept_ref, half + tokens, tokens, resp_at[2]),
            (back_ref, half, tokens, resp_at[3]),
            (back_ref, half + tokens, tokens, resp_at[4]),
        ):
            grad_k = dk[n, at : at + size] * score_scale
            ref[start : start + size, k_cols] = grad_k.astype(ref.dtype)
            ref[start : start + size, v_cols] = dv[n, at : at + size].astype(ref.dtype)


def attention(lengths, resp_q, grad_out, sent, got, own, far):
    tokens = resp_q.shape[0]
    half = sent.shape[0] - 2 * tokens
    total_keys = 2 * half + 5 * tokens
    kv_heads = sent.shape[1] // (2 * HD)
    q_heads = resp_q.shape[1] // HD
    halves = 1 if tokens * total_keys <= MOST_SCORES else 2
    rows = tokens // halves
    pairs = tokens * q_heads * total_keys
    most = ((8, HD), F32)
    bias, q_most = local_call(
        mask_kernel, "mask", [lengths, resp_q], [((5 * tokens, tokens), F32), most], scalars=1
    )
    turned, k_most = local_call(
        functools.partial(turn_kernel, kv_heads),
        "turn",
        [sent, own, far],
        [((2 * kv_heads, HD, half + 3 * tokens), BF16), most],
    )
    return pl.pallas_call(
        functools.partial(attention_kernel, halves),
        in_specs=whole(10),
        out_specs=whole(4),
        out_shape=[
            jax.ShapeDtypeStruct(resp_q.shape, BF16),
            jax.ShapeDtypeStruct(resp_q.shape, BF16),
            jax.ShapeDtypeStruct((half + 3 * tokens, sent.shape[1]), F32),
            jax.ShapeDtypeStruct((half + 2 * tokens, sent.shape[1]), BF16),
        ],
        scratch_shapes=[
            pltpu.VMEM((kv_heads, total_keys, HD), BF16),
            pltpu.VMEM((kv_heads, total_keys, HD), BF16),
            pltpu.VMEM((kv_heads, HD, total_keys), BF16),
            pltpu.VMEM((kv_heads, HD, total_keys), BF16),
            pltpu.VMEM((total_keys, rows), F32),
            pltpu.VMEM((2, total_keys, rows), BF16),
            pltpu.VMEM((2, total_keys, rows), BF16),
            pltpu.VMEM((2, 8, rows), F32),
            pltpu.VMEM((2, HD, rows), BF16),
            pltpu.VMEM((2, HD, rows), BF16),
            pltpu.VMEM((2, rows, HD), BF16),
            pltpu.VMEM((2, rows, HD), BF16),
            pltpu.VMEM((kv_heads, total_keys, HD), F32),
            pltpu.VMEM((kv_heads, total_keys, HD), F32),
        ],
        compiler_params=pltpu.CompilerParams(vmem_limit_bytes=(36 if halves == 1 else 48) << 20),
        cost_estimate=pl.CostEstimate(
            flops=12 * HD * pairs, bytes_accessed=8 * resp_q.size, transcendentals=pairs
        ),
        name="attention",
    )(resp_q, grad_out, sent, got, own, far, bias, turned, q_most, k_most)


def swap_heads(array, by):
    devices = lax.axis_size("head")
    return lax.ppermute(array, "head", [(i, i ^ by) for i in range(devices)])


def swap_chips(array, by):
    devices = lax.axis_size("seq")
    return lax.ppermute(array, "seq", [(i, i ^ (by * CORES)) for i in range(devices)])


def swap_cores(array):
    devices = lax.axis_size("seq")
    return lax.ppermute(array, "seq", [(i, i ^ 1) for i in range(devices)])


def shift_chips(array, by):
    devices = lax.axis_size("seq")
    by = by * CORES
    return lax.ppermute(array, "seq", [(i, i + by) for i in range(devices) if 0 <= i + by < devices])


def shards(prompt_k, prompt_v, resp_q, resp_k, resp_v, grad_out, resp_lengths):
    tokens, kv_cols = resp_k.shape
    wide = 2 * kv_cols
    groups = lax.axis_size("head")
    chips = lax.axis_size("seq") // CORES
    block = prompt_k.shape[0]
    core = lax.rem(lax.axis_index("seq"), CORES)

    *pieces, own = pack([prompt_k, prompt_v, resp_k, resp_v], groups)
    pieces = [pieces[0]] + [swap_heads(pieces[k], k) for k in range(1, groups)]
    near = shift_chips(own, 1)
    far = shift_chips(own, 2)
    pieces[1:], near, far = lax.optimization_barrier((pieces[1:], near, far))
    mine = jnp.concatenate(pieces, axis=0)
    parts = [mine] + [swap_chips(mine, k) for k in range(1, chips)]
    chosen = jnp.where(core == 1, far, own)
    sent = jnp.concatenate(parts + [near, chosen], axis=0)
    got = swap_cores(sent)

    resp_out, grad_q, kept, back = attention(
        resp_lengths, resp_q, grad_out, sent, got, own, far
    )

    back = swap_cores(back)
    share = groups * block
    *parts, own = local_call(
        functools.partial(merge_kernel, chips, tokens),
        "merge",
        [kept, back],
        [((share, wide), BF16)] * chips
        + [((tokens // 2, wide), BF16)] * 4
        + [((tokens, wide), F32)],
    )
    near, far, parts = parts[chips : chips + 2], parts[chips + 2 :], parts[:chips]
    parts = [parts[0]] + [swap_chips(parts[k], k) for k in range(1, chips)]
    near = [shift_chips(part, -1) for part in near]
    far = [shift_chips(part, -2) for part in far]
    pieces = local_call(
        functools.partial(sum_kernel, chips),
        "sum_chips",
        parts,
        [((block, wide), BF16)] * groups,
        [pltpu.VMEM((share, wide), F32)],
    )
    pieces = [pieces[0]] + [swap_heads(pieces[k], k) for k in range(1, groups)]
    grad_k_prompt, grad_v_prompt, grad_k_resp, grad_v_resp = local_call(
        finish_kernel,
        "finish",
        [own] + near + far + pieces,
        [(prompt_k.shape, BF16)] * 2 + [((tokens, kv_cols), BF16)] * 2,
    )
    return (resp_out, grad_q, grad_k_resp, grad_v_resp, grad_k_prompt, grad_v_prompt)


def solution(mesh):
    placed = (
        P(("seq", "head"), None),
        P(("seq", "head"), None),
        P("seq", "head"),
        P("seq", "head"),
        P("seq", "head"),
        P("seq", "head"),
        P(),
    )
    return jax.shard_map(
        shards,
        mesh=mesh,
        in_specs=placed,
        out_specs=(
            P("seq", "head"),
            P("seq", "head"),
            P("seq", "head"),
            P("seq", "head"),
            P(("seq", "head"), None),
            P(("seq", "head"), None),
        ),
        check_vma=False,
    )
```

```python
import functools
import math

import jax
import jax.numpy as jnp
from jax import lax
from jax.experimental import pallas as pl
from jax.experimental.pallas import tpu as pltpu
from jax.sharding import PartitionSpec as P

HD = 128
CORES = 2
FAR = 4
CHUNK = 256
LONGER = 640
SAFE_SCORE = 40.0
TILE = 64
MOST_SCORES = 2560 * 256
NEG = -1e30
BF16 = jnp.bfloat16
F32 = jnp.float32


def dot(a, b):
    return jnp.dot(a, b, preferred_element_type=F32)


def whole(count):
    return [pl.BlockSpec(memory_space=pltpu.VMEM)] * count


def local_call(kernel, name, inputs, outputs, scratch=(), scalars=0):
    return pl.pallas_call(
        kernel,
        in_specs=[pl.BlockSpec(memory_space=pltpu.SMEM)] * scalars + whole(len(inputs) - scalars),
        out_specs=whole(len(outputs)),
        out_shape=[jax.ShapeDtypeStruct(shape, kind) for shape, kind in outputs],
        scratch_shapes=list(scratch),
        compiler_params=pltpu.CompilerParams(vmem_limit_bytes=40 * 1024 * 1024),
        name=name,
    )(*inputs)


def pack_kernel(pk_ref, pv_ref, rk_ref, rv_ref, *outs):
    pieces, resp = outs[:-1], outs[-1]
    head = lax.axis_index("head")
    width = pieces[0].shape[1]
    for k, piece in enumerate(pieces):
        start = pl.multiple_of((head ^ k) * (width // 2), HD)
        for n in range(width // (2 * HD)):
            at = pl.multiple_of(start + n * HD, HD)
            piece[:, 2 * n * HD : (2 * n + 1) * HD] = pk_ref[:, pl.ds(at, HD)]
            piece[:, (2 * n + 1) * HD : (2 * n + 2) * HD] = pv_ref[:, pl.ds(at, HD)]
    for n in range(width // (2 * HD)):
        resp[:, 2 * n * HD : (2 * n + 1) * HD] = rk_ref[:, n * HD : (n + 1) * HD]
        resp[:, (2 * n + 1) * HD : (2 * n + 2) * HD] = rv_ref[:, n * HD : (n + 1) * HD]


def pack(inputs, groups):
    def one(array):
        return pl.BlockSpec(array.shape, lambda i: (0, 0))

    block, tokens = inputs[0].shape[0], inputs[2].shape[0]
    wide = 2 * inputs[2].shape[1]
    shapes = [(block, wide)] * groups + [(tokens, wide)]
    return pl.pallas_call(
        pack_kernel,
        grid=(1,),
        in_specs=[one(array) for array in inputs],
        out_specs=whole(groups + 1),
        out_shape=[jax.ShapeDtypeStruct(shape, BF16) for shape in shapes],
        compiler_params=pltpu.CompilerParams(vmem_limit_bytes=56 * 1024 * 1024),
        name="pack",
    )(*inputs)


def merge_kernel(parts, rows, kept_ref, got_ref, *outs):
    pieces, back1, back2, own = outs[:parts], outs[parts:-3], outs[-3:-1], outs[-1]
    core = lax.rem(lax.axis_index("seq"), CORES)
    to_own = jnp.where(core == 0, 1.0, 0.0)
    half = kept_ref.shape[0] - 3 * rows
    share = half // parts
    for k, piece in enumerate(pieces):
        at = slice(k * share, (k + 1) * share)
        piece[...] = (kept_ref[at] + got_ref[at].astype(F32)).astype(BF16)
    one, two, three = half + rows, half + 2 * rows, half + 3 * rows
    near = (kept_ref[half:one] + got_ref[half:one].astype(F32)).astype(BF16)
    chosen = got_ref[one:two].astype(F32)
    far = (kept_ref[one:two] + chosen * (1.0 - to_own)).astype(BF16)
    for i in range(2):
        back1[i][...] = near[i * rows // 2 : (i + 1) * rows // 2]
        back2[i][...] = far[i * rows // 2 : (i + 1) * rows // 2]
    own[...] = kept_ref[two:three] + chosen * to_own


def sum_kernel(parts, *refs):
    ins, outs, total = refs[:parts], refs[parts:-1], refs[-1]
    acc = ins[0][...].astype(F32)
    for ref in ins[1:]:
        acc = acc + ref[...].astype(F32)
    total[...] = acc
    share = total.shape[0] // len(outs)
    for k, out in enumerate(outs):
        out[...] = total[k * share : (k + 1) * share].astype(BF16)


def finish_kernel(own_ref, *refs):
    near, far, pieces, (gk_ref, gv_ref, rk_ref, rv_ref) = refs[:2], refs[2:4], refs[4:-4], refs[-4:]
    head = lax.axis_index("head")
    width = pieces[0].shape[1]
    for k, piece in enumerate(pieces):
        start = pl.multiple_of((head ^ k) * (width // 2), HD)
        for n in range(width // (2 * HD)):
            at = pl.multiple_of(start + n * HD, HD)
            gk_ref[:, pl.ds(at, HD)] = piece[:, 2 * n * HD : (2 * n + 1) * HD]
            gv_ref[:, pl.ds(at, HD)] = piece[:, (2 * n + 1) * HD : (2 * n + 2) * HD]
    rows = near[0].shape[0]
    for i in range(2):
        at = slice(i * rows, (i + 1) * rows)
        total = own_ref[at] + near[i][...].astype(F32) + far[i][...].astype(F32)
        total = total.astype(BF16)
        for n in range(width // (2 * HD)):
            rk_ref[at, n * HD : (n + 1) * HD] = total[:, 2 * n * HD : (2 * n + 1) * HD]
            rv_ref[at, n * HD : (n + 1) * HD] = total[:, (2 * n + 1) * HD : (2 * n + 2) * HD]


def mask_kernel(lengths, q_ref, bias, most_ref):
    tokens, q_cols = q_ref.shape
    place = lax.axis_index("seq")
    core = lax.rem(place, CORES)
    first_row = place * tokens
    row_pos = first_row + lax.broadcasted_iota(jnp.int32, (8, tokens), 1)
    seg_start = jnp.zeros((8, tokens), jnp.int32)
    end = jnp.int32(0)
    for i in range(lengths.shape[0]):
        end = end + lengths[i]
        seg_start = jnp.where(row_pos >= end, end, seg_start)
    seg_start, row_pos = seg_start[:1], row_pos[:1]
    near = 1 + 2 * core
    for i, distance in enumerate((0, 2, FAR, near, 4 - near)):
        for row in range(0, tokens, TILE):
            key_pos = (first_row - distance * tokens + row) + lax.broadcasted_iota(
                jnp.int32, (TILE, tokens), 0
            )
            allowed = (key_pos >= seg_start) & (key_pos <= row_pos)
            at = i * tokens + row
            bias[at : at + TILE] = jnp.where(allowed, 0.0, NEG)
    most = jnp.zeros((tokens, 1), F32)
    for at in range(0, q_cols, HD):
        part = q_ref[:, at : at + HD].astype(F32)
        most = jnp.maximum(most, jnp.sum(part * part, axis=1, keepdims=True))
    most_ref[...] = jnp.broadcast_to(jnp.max(most, axis=0, keepdims=True), most_ref.shape)


def largest(ref, most, cols):
    for at in range(0, ref.shape[0], HD):
        part = ref[at : at + HD, cols].astype(F32)
        most = jnp.maximum(most, jnp.sum(part * part, axis=1, keepdims=True))
    return most


def turn_kernel(kv_heads, sent_ref, own_ref, far_ref, turned, most_ref):
    tokens = own_ref.shape[0]
    most = jnp.zeros((HD, 1), F32)
    for n in range(2 * kv_heads):
        cols = slice(n * HD, (n + 1) * HD)
        at = 0
        for ref, size in ((sent_ref, sent_ref.shape[0] - tokens), (far_ref, tokens), (own_ref, tokens)):
            turned[n, :, at : at + size] = ref[:size, cols].T
            at += size
            if n % 2 == 0:
                most = largest(ref, most, cols)
    most_ref[...] = jnp.broadcast_to(jnp.max(most, axis=0, keepdims=True), most_ref.shape)


def attention_kernel(
    halves, q_ref, do_ref, sent_ref, got_ref, own_ref, far_ref,
    bias, turned, q_most, k_most,
    o_ref, dq_ref, kept_ref, back_ref,
    keys, values, keys_t, values_t, s_buf, p_bufs, d_bufs, inv_bufs,
    q_ts, cot_ts, q_ns, cot_ns, dk, dv,
):
    kv_heads, total_keys = keys.shape[0], keys.shape[1]
    tokens, q_cols = q_ref.shape
    rows = tokens // halves
    prompt_len = total_keys - 5 * tokens
    half = prompt_len // 2
    steps = q_cols // HD * halves // 2
    steps_per_kv = steps // kv_heads
    score_scale = 1.0 / math.sqrt(HD)
    exp_scale = score_scale * math.log2(math.e)
    resp_at = [prompt_len + i * tokens for i in range(6)]
    chunks = [slice(at, at + CHUNK) for at in range(0, total_keys, CHUNK)]
    longer = [slice(at, at + LONGER) for at in range(0, total_keys, LONGER)]
    cuts = [slice(at, at + total_keys // 2) for at in (0, total_keys // 2)]

    def columns(head):
        if isinstance(head, int):
            return slice(head * HD, (head + 1) * HD)
        return pl.ds(pl.multiple_of(head * HD, HD), HD)

    def place_of(which, step):
        head = step * 2 + which if halves == 1 else step
        row = 0 if halves == 1 else which * rows
        return slice(row, row + rows), columns(head)

    def kv_of(step):
        return step // steps_per_kv

    def bias_at(which, at, size):
        row = which * rows * (halves - 1)
        return bias[at - prompt_len : at - prompt_len + size, row : row + rows]

    def folded(x):
        return x.reshape(x.shape[0] // 8, 8, rows)

    def within(at):
        return [slice(start, start + TILE) for start in range(at.start, at.stop, TILE)]

    def weigh(which, step, fast):
        kv = kv_of(step)
        where = place_of(which, step)
        state = {}

        def lift():
            q_ts[which] = q_ref[where].T
            cot_ts[which] = do_ref[where].T

        def masked(s, at, tile):
            s = s[tile.start - at.start : tile.stop - at.start]
            return s if tile.start < prompt_len else s + bias_at(which, tile.start, TILE)

        def put(tile, p):
            p_bufs[which, tile] = p.astype(BF16)

        def direct(at):
            s = dot(keys[kv, at], q_ts[which])
            for tile in within(at):
                put(tile, jnp.exp2(masked(s, at, tile) * exp_scale))

        def highest(at):
            s = dot(keys[kv, at], q_ts[which])
            for tile in within(at):
                part = masked(s, at, tile)
                s_buf[tile] = part
                top = jnp.max(folded(part), axis=0)
                state["top"] = jnp.maximum(state["top"], top) if "top" in state else top

        def settle():
            state["top"] = jnp.max(state["top"], axis=0, keepdims=True) * exp_scale

        def reduced(at):
            for tile in within(at):
                put(tile, jnp.exp2(s_buf[tile] * exp_scale - state["top"]))

        if fast:
            return [lift] + [functools.partial(direct, at) for at in chunks]
        work = [lift] + [functools.partial(highest, at) for at in chunks] + [settle]
        return work + [functools.partial(reduced, at) for at in chunks]

    def settled(which, step, state):
        kv = kv_of(step)
        where = place_of(which, step)

        def output(at):
            more = dot(values_t[kv, :, at], p_bufs[which, at])
            state["out"] = state["out"] + more if "out" in state else more

        def put():
            inverse = 1.0 / state["out"][HD : HD + 1]
            inv_bufs[which] = jnp.broadcast_to(inverse, (8, rows))
            out = (state["out"][:HD] * inverse).astype(BF16)
            o_ref[where] = out.T
            q_ns[which] = (q_ts[which].astype(F32) * inverse).astype(BF16).T
            wide = cot_ts[which].astype(F32)
            state["delta"] = jnp.sum(wide * out.astype(F32), axis=0, keepdims=True)
            cot_ns[which] = (wide * inverse).astype(BF16).T

        return [functools.partial(output, at) for at in cuts] + [put]

    def slopes(which, step, state):
        kv = kv_of(step)

        def slope(at):
            grads = dot(values[kv, at], cot_ts[which])
            for tile in within(at):
                part = grads[tile.start - at.start : tile.stop - at.start] - state["delta"]
                d_bufs[which, tile] = p_bufs[which, tile] * part.astype(BF16)

        return [functools.partial(slope, at) for at in chunks]

    def value_grads(which, step):
        kv = kv_of(step)

        def value_grad(at):
            dv[kv, at] += dot(p_bufs[which, at], cot_ns[which])

        return [functools.partial(value_grad, at) for at in longer]

    def key_grads(which, step):
        kv = kv_of(step)

        def key_grad(at):
            dk[kv, at] += dot(d_bufs[which, at], q_ns[which])

        return [functools.partial(key_grad, at) for at in longer]

    def query_grads(which, step):
        kv = kv_of(step)
        where = place_of(which, step)
        state = {}

        def query(at):
            more = dot(keys_t[kv, :, at], d_bufs[which, at])
            state["dq"] = state["dq"] + more if "dq" in state else more

        def put():
            dq = state["dq"] * (inv_bufs[which, :1] * score_scale)
            dq_ref[where] = dq.astype(BF16).T

        return [functools.partial(query, at) for at in cuts] + [put]

    def slot(which, step, fast):
        before, before_step = 1 - which, step - 1 + which
        state = {}
        work = weigh(which, step, fast)
        started = not isinstance(step, int)
        late = key_grads(which, step - 1) if started else []
        first = query_grads(which, step - 1) if started else []
        if started or which == 1:
            first = settled(before, before_step, state) + first
        together(work, first + late[: len(late) // 2])
        if started or which == 1:
            together(
                slopes(before, before_step, state),
                late[len(late) // 2 :] + value_grads(before, before_step),
            )

    def together(vector, matrix):
        done = 0
        for i, work in enumerate(vector):
            work()
            while done * len(vector) < (i + 1) * len(matrix):
                matrix[done]()
                done += 1

    most = jnp.zeros((HD, 1), F32)
    for n in range(kv_heads):
        k_cols = slice(2 * n * HD, (2 * n + 1) * HD)
        v_cols = slice((2 * n + 1) * HD, (2 * n + 2) * HD)
        for ref, start, size, at, turned_at in (
            (sent_ref, 0, half, 0, 0),
            (got_ref, 0, half, half, None),
            (own_ref, 0, tokens, resp_at[0], half + 2 * tokens),
            (sent_ref, half, tokens, resp_at[1], half),
            (far_ref, 0, tokens, resp_at[2], half + tokens),
            (got_ref, half, tokens, resp_at[3], None),
            (got_ref, half + tokens, tokens, resp_at[4], None),
        ):
            k_rows = ref[start : start + size, k_cols]
            v_rows = ref[start : start + size, v_cols]
            keys[n, at : at + size] = k_rows
            values[n, at : at + size] = v_rows
            if turned_at is None:
                keys_t[n, :, at : at + size] = k_rows.T
                values_t[n, :HD, at : at + size] = v_rows.T
            else:
                there = slice(turned_at, turned_at + size)
                keys_t[n, :, at : at + size] = turned[2 * n, :, there]
                values_t[n, :HD, at : at + size] = turned[2 * n + 1, :, there]
        values_t[n, HD:] = jnp.ones((16, total_keys), BF16)
        most = largest(got_ref, most, k_cols)
    dk[...] = jnp.zeros_like(dk)
    dv[...] = jnp.zeros_like(dv)
    keys_most = jnp.maximum(jnp.max(most), jnp.max(k_most[...]))
    most = jnp.max(q_most[...]) * keys_most * (score_scale * score_scale)
    small = most <= SAFE_SCORE * SAFE_SCORE
    def run(fast):
        def pair(step, carry):
            slot(0, step, fast)
            slot(1, step, fast)
            return carry

        slot(0, 0, fast)
        slot(1, 0, fast)
        lax.fori_loop(1, steps, pair, 0)

    pl.when(small)(functools.partial(run, True))
    pl.when(jnp.logical_not(small))(functools.partial(run, False))
    state = {}
    for work in settled(1, steps - 1, state) + query_grads(0, steps - 1):
        work()
    together(
        slopes(1, steps - 1, state), key_grads(0, steps - 1) + value_grads(1, steps - 1)
    )
    for work in key_grads(1, steps - 1) + query_grads(1, steps - 1):
        work()
    for n in range(kv_heads):
        k_cols = slice(2 * n * HD, (2 * n + 1) * HD)
        v_cols = slice((2 * n + 1) * HD, (2 * n + 2) * HD)
        for ref, start, size, at in (
            (kept_ref, 0, half, 0),
            (back_ref, 0, half, half),
            (kept_ref, half + 2 * tokens, tokens, resp_at[0]),
            (kept_ref, half, tokens, resp_at[1]),
            (kept_ref, half + tokens, tokens, resp_at[2]),
            (back_ref, half, tokens, resp_at[3]),
            (back_ref, half + tokens, tokens, resp_at[4]),
        ):
            grad_k = dk[n, at : at + size] * score_scale
            ref[start : start + size, k_cols] = grad_k.astype(ref.dtype)
            ref[start : start + size, v_cols] = dv[n, at : at + size].astype(ref.dtype)


def attention(lengths, resp_q, grad_out, sent, got, own, far):
    tokens = resp_q.shape[0]
    half = sent.shape[0] - 2 * tokens
    total_keys = 2 * half + 5 * tokens
    kv_heads = sent.shape[1] // (2 * HD)
    q_heads = resp_q.shape[1] // HD
    halves = 1 if tokens * total_keys <= MOST_SCORES else 2
    rows = tokens // halves
    pairs = tokens * q_heads * total_keys
    most = ((8, HD), F32)
    bias, q_most = local_call(
        mask_kernel, "mask", [lengths, resp_q], [((5 * tokens, tokens), F32), most], scalars=1
    )
    turned, k_most = local_call(
        functools.partial(turn_kernel, kv_heads),
        "turn",
        [sent, own, far],
        [((2 * kv_heads, HD, half + 3 * tokens), BF16), most],
    )
    return pl.pallas_call(
        functools.partial(attention_kernel, halves),
        in_specs=whole(10),
        out_specs=whole(4),
        out_shape=[
            jax.ShapeDtypeStruct(resp_q.shape, BF16),
            jax.ShapeDtypeStruct(resp_q.shape, BF16),
            jax.ShapeDtypeStruct((half + 3 * tokens, sent.shape[1]), F32),
            jax.ShapeDtypeStruct((half + 2 * tokens, sent.shape[1]), BF16),
        ],
        scratch_shapes=[
            pltpu.VMEM((kv_heads, total_keys, HD), BF16),
            pltpu.VMEM((kv_heads, total_keys, HD), BF16),
            pltpu.VMEM((kv_heads, HD, total_keys), BF16),
            pltpu.VMEM((kv_heads, HD + 16, total_keys), BF16),
            pltpu.VMEM((total_keys, rows), F32),
            pltpu.VMEM((2, total_keys, rows), BF16),
            pltpu.VMEM((2, total_keys, rows), BF16),
            pltpu.VMEM((2, 8, rows), F32),
            pltpu.VMEM((2, HD, rows), BF16),
            pltpu.VMEM((2, HD, rows), BF16),
            pltpu.VMEM((2, rows, HD), BF16),
            pltpu.VMEM((2, rows, HD), BF16),
            pltpu.VMEM((kv_heads, total_keys, HD), F32),
            pltpu.VMEM((kv_heads, total_keys, HD), F32),
        ],
        compiler_params=pltpu.CompilerParams(vmem_limit_bytes=(36 if halves == 1 else 48) << 20),
        cost_estimate=pl.CostEstimate(
            flops=12 * HD * pairs, bytes_accessed=8 * resp_q.size, transcendentals=pairs
        ),
        name="attention",
    )(resp_q, grad_out, sent, got, own, far, bias, turned, q_most, k_most)


def swap_heads(array, by):
    devices = lax.axis_size("head")
    return lax.ppermute(array, "head", [(i, i ^ by) for i in range(devices)])


def swap_chips(array, by):
    devices = lax.axis_size("seq")
    return lax.ppermute(array, "seq", [(i, i ^ (by * CORES)) for i in range(devices)])


def swap_cores(array):
    devices = lax.axis_size("seq")
    return lax.ppermute(array, "seq", [(i, i ^ 1) for i in range(devices)])


def shift_chips(array, by):
    devices = lax.axis_size("seq")
    by = by * CORES
    return lax.ppermute(array, "seq", [(i, i + by) for i in range(devices) if 0 <= i + by < devices])


def shards(prompt_k, prompt_v, resp_q, resp_k, resp_v, grad_out, resp_lengths):
    tokens, kv_cols = resp_k.shape
    wide = 2 * kv_cols
    groups = lax.axis_size("head")
    chips = lax.axis_size("seq") // CORES
    block = prompt_k.shape[0]
    core = lax.rem(lax.axis_index("seq"), CORES)

    *pieces, own = pack([prompt_k, prompt_v, resp_k, resp_v], groups)
    pieces = [pieces[0]] + [swap_heads(pieces[k], k) for k in range(1, groups)]
    near = shift_chips(own, 1)
    far = shift_chips(own, 2)
    pieces[1:], near, far = lax.optimization_barrier((pieces[1:], near, far))
    mine = jnp.concatenate(pieces, axis=0)
    parts = [mine] + [swap_chips(mine, k) for k in range(1, chips)]
    chosen = jnp.where(core == 1, far, own)
    sent = jnp.concatenate(parts + [near, chosen], axis=0)
    got = swap_cores(sent)

    resp_out, grad_q, kept, back = attention(
        resp_lengths, resp_q, grad_out, sent, got, own, far
    )

    back = swap_cores(back)
    share = groups * block
    *parts, own = local_call(
        functools.partial(merge_kernel, chips, tokens),
        "merge",
        [kept, back],
        [((share, wide), BF16)] * chips
        + [((tokens // 2, wide), BF16)] * 4
        + [((tokens, wide), F32)],
    )
    near, far, parts = parts[chips : chips + 2], parts[chips + 2 :], parts[:chips]
    parts = [parts[0]] + [swap_chips(parts[k], k) for k in range(1, chips)]
    near = [shift_chips(part, -1) for part in near]
    far = [shift_chips(part, -2) for part in far]
    pieces = local_call(
        functools.partial(sum_kernel, chips),
        "sum_chips",
        parts,
        [((block, wide), BF16)] * groups,
        [pltpu.VMEM((share, wide), F32)],
    )
    pieces = [pieces[0]] + [swap_heads(pieces[k], k) for k in range(1, groups)]
    grad_k_prompt, grad_v_prompt, grad_k_resp, grad_v_resp = local_call(
        finish_kernel,
        "finish",
        [own] + near + far + pieces,
        [(prompt_k.shape, BF16)] * 2 + [((tokens, kv_cols), BF16)] * 2,
    )
    return (resp_out, grad_q, grad_k_resp, grad_v_resp, grad_k_prompt, grad_v_prompt)


def solution(mesh):
    placed = (
        P(("seq", "head"), None),
        P(("seq", "head"), None),
        P("seq", "head"),
        P("seq", "head"),
        P("seq", "head"),
        P("seq", "head"),
        P(),
    )
    return jax.shard_map(
        shards,
        mesh=mesh,
        in_specs=placed,
        out_specs=(
            P("seq", "head"),
            P("seq", "head"),
            P("seq", "head"),
            P("seq", "head"),
            P(("seq", "head"), None),
            P(("seq", "head"), None),
        ),
        check_vma=False,
    )
```

```python
import functools
import math

import jax
import jax.numpy as jnp
from jax import lax
from jax.experimental import pallas as pl
from jax.experimental.pallas import tpu as pltpu
from jax.sharding import PartitionSpec as P

HD = 128
CORES = 2
FAR = 4
CHUNK = 640
LONGER = 1280
SAFE_SCORE = 40.0
TILE = 64
MOST_SCORES = 2560 * 256
NEG = -1e30
BF16 = jnp.bfloat16
F32 = jnp.float32


def dot(a, b):
    return jnp.dot(a, b, preferred_element_type=F32)


def whole(count):
    return [pl.BlockSpec(memory_space=pltpu.VMEM)] * count


def local_call(kernel, name, inputs, outputs, scratch=(), scalars=0):
    return pl.pallas_call(
        kernel,
        in_specs=[pl.BlockSpec(memory_space=pltpu.SMEM)] * scalars + whole(len(inputs) - scalars),
        out_specs=whole(len(outputs)),
        out_shape=[jax.ShapeDtypeStruct(shape, kind) for shape, kind in outputs],
        scratch_shapes=list(scratch),
        compiler_params=pltpu.CompilerParams(vmem_limit_bytes=40 * 1024 * 1024),
        name=name,
    )(*inputs)


def pack_kernel(pk_ref, pv_ref, rk_ref, rv_ref, *outs):
    pieces, resp = outs[:-1], outs[-1]
    head = lax.axis_index("head")
    width = pieces[0].shape[1]
    for k, piece in enumerate(pieces):
        start = pl.multiple_of((head ^ k) * (width // 2), HD)
        for n in range(width // (2 * HD)):
            at = pl.multiple_of(start + n * HD, HD)
            piece[:, 2 * n * HD : (2 * n + 1) * HD] = pk_ref[:, pl.ds(at, HD)]
            piece[:, (2 * n + 1) * HD : (2 * n + 2) * HD] = pv_ref[:, pl.ds(at, HD)]
    for n in range(width // (2 * HD)):
        resp[:, 2 * n * HD : (2 * n + 1) * HD] = rk_ref[:, n * HD : (n + 1) * HD]
        resp[:, (2 * n + 1) * HD : (2 * n + 2) * HD] = rv_ref[:, n * HD : (n + 1) * HD]


def pack(inputs, groups):
    def one(array):
        return pl.BlockSpec(array.shape, lambda i: (0, 0))

    block, tokens = inputs[0].shape[0], inputs[2].shape[0]
    wide = 2 * inputs[2].shape[1]
    shapes = [(block, wide)] * groups + [(tokens, wide)]
    return pl.pallas_call(
        pack_kernel,
        grid=(1,),
        in_specs=[one(array) for array in inputs],
        out_specs=whole(groups + 1),
        out_shape=[jax.ShapeDtypeStruct(shape, BF16) for shape in shapes],
        compiler_params=pltpu.CompilerParams(vmem_limit_bytes=56 * 1024 * 1024),
        name="pack",
    )(*inputs)


def merge_kernel(parts, rows, kept_ref, got_ref, *outs):
    pieces, back1, back2, own = outs[:parts], outs[parts:-3], outs[-3:-1], outs[-1]
    core = lax.rem(lax.axis_index("seq"), CORES)
    to_own = jnp.where(core == 0, 1.0, 0.0)
    half = kept_ref.shape[0] - 3 * rows
    share = half // parts
    for k, piece in enumerate(pieces):
        at = slice(k * share, (k + 1) * share)
        piece[...] = (kept_ref[at] + got_ref[at].astype(F32)).astype(BF16)
    one, two, three = half + rows, half + 2 * rows, half + 3 * rows
    near = (kept_ref[half:one] + got_ref[half:one].astype(F32)).astype(BF16)
    chosen = got_ref[one:two].astype(F32)
    far = (kept_ref[one:two] + chosen * (1.0 - to_own)).astype(BF16)
    for i in range(2):
        back1[i][...] = near[i * rows // 2 : (i + 1) * rows // 2]
        back2[i][...] = far[i * rows // 2 : (i + 1) * rows // 2]
    own[...] = kept_ref[two:three] + chosen * to_own


def sum_kernel(parts, *refs):
    ins, outs, total = refs[:parts], refs[parts:-1], refs[-1]
    acc = ins[0][...].astype(F32)
    for ref in ins[1:]:
        acc = acc + ref[...].astype(F32)
    total[...] = acc
    share = total.shape[0] // len(outs)
    for k, out in enumerate(outs):
        out[...] = total[k * share : (k + 1) * share].astype(BF16)


def finish_kernel(own_ref, *refs):
    near, far, pieces, (gk_ref, gv_ref, rk_ref, rv_ref) = refs[:2], refs[2:4], refs[4:-4], refs[-4:]
    head = lax.axis_index("head")
    width = pieces[0].shape[1]
    for k, piece in enumerate(pieces):
        start = pl.multiple_of((head ^ k) * (width // 2), HD)
        for n in range(width // (2 * HD)):
            at = pl.multiple_of(start + n * HD, HD)
            gk_ref[:, pl.ds(at, HD)] = piece[:, 2 * n * HD : (2 * n + 1) * HD]
            gv_ref[:, pl.ds(at, HD)] = piece[:, (2 * n + 1) * HD : (2 * n + 2) * HD]
    rows = near[0].shape[0]
    for i in range(2):
        at = slice(i * rows, (i + 1) * rows)
        total = own_ref[at] + near[i][...].astype(F32) + far[i][...].astype(F32)
        total = total.astype(BF16)
        for n in range(width // (2 * HD)):
            rk_ref[at, n * HD : (n + 1) * HD] = total[:, 2 * n * HD : (2 * n + 1) * HD]
            rv_ref[at, n * HD : (n + 1) * HD] = total[:, (2 * n + 1) * HD : (2 * n + 2) * HD]


def mask_kernel(lengths, q_ref, bias, most_ref):
    tokens, q_cols = q_ref.shape
    place = lax.axis_index("seq")
    core = lax.rem(place, CORES)
    first_row = place * tokens
    row_pos = first_row + lax.broadcasted_iota(jnp.int32, (8, tokens), 1)
    seg_start = jnp.zeros((8, tokens), jnp.int32)
    end = jnp.int32(0)
    for i in range(lengths.shape[0]):
        end = end + lengths[i]
        seg_start = jnp.where(row_pos >= end, end, seg_start)
    seg_start, row_pos = seg_start[:1], row_pos[:1]
    near = 1 + 2 * core
    for i, distance in enumerate((0, 2, FAR, near, 4 - near)):
        for row in range(0, tokens, TILE):
            key_pos = (first_row - distance * tokens + row) + lax.broadcasted_iota(
                jnp.int32, (TILE, tokens), 0
            )
            allowed = (key_pos >= seg_start) & (key_pos <= row_pos)
            at = i * tokens + row
            bias[at : at + TILE] = jnp.where(allowed, 0.0, NEG)
    most = jnp.zeros((tokens, 1), F32)
    for at in range(0, q_cols, HD):
        part = q_ref[:, at : at + HD].astype(F32)
        most = jnp.maximum(most, jnp.sum(part * part, axis=1, keepdims=True))
    most_ref[...] = jnp.broadcast_to(jnp.max(most, axis=0, keepdims=True), most_ref.shape)


def largest(ref, most, cols):
    for at in range(0, ref.shape[0], HD):
        part = ref[at : at + HD, cols].astype(F32)
        most = jnp.maximum(most, jnp.sum(part * part, axis=1, keepdims=True))
    return most


def turn_kernel(kv_heads, sent_ref, own_ref, far_ref, turned, most_ref):
    tokens = own_ref.shape[0]
    most = jnp.zeros((HD, 1), F32)
    for n in range(2 * kv_heads):
        cols = slice(n * HD, (n + 1) * HD)
        at = 0
        for ref, size in ((sent_ref, sent_ref.shape[0] - tokens), (far_ref, tokens), (own_ref, tokens)):
            turned[n, :, at : at + size] = ref[:size, cols].T
            at += size
            if n % 2 == 0:
                most = largest(ref, most, cols)
    most_ref[...] = jnp.broadcast_to(jnp.max(most, axis=0, keepdims=True), most_ref.shape)


def attention_kernel(
    halves, q_ref, do_ref, sent_ref, got_ref, own_ref, far_ref,
    bias, turned, q_most, k_most,
    o_ref, dq_ref, kept_ref, back_ref,
    keys, values, keys_t, values_t, s_buf, p_bufs, d_bufs, inv_bufs,
    q_ts, cot_ts, q_ns, cot_ns, dk, dv,
):
    kv_heads, total_keys = keys.shape[0], keys.shape[1]
    tokens, q_cols = q_ref.shape
    rows = tokens // halves
    prompt_len = total_keys - 5 * tokens
    half = prompt_len // 2
    steps = q_cols // HD * halves // 2
    steps_per_kv = steps // kv_heads
    score_scale = 1.0 / math.sqrt(HD)
    exp_scale = score_scale * math.log2(math.e)
    resp_at = [prompt_len + i * tokens for i in range(6)]
    chunks = [slice(at, at + CHUNK) for at in range(0, total_keys, CHUNK)]
    longer = [slice(at, at + LONGER) for at in range(0, total_keys, LONGER)]
    cuts = [slice(at, at + total_keys // 2) for at in (0, total_keys // 2)]

    def columns(head):
        if isinstance(head, int):
            return slice(head * HD, (head + 1) * HD)
        return pl.ds(pl.multiple_of(head * HD, HD), HD)

    def place_of(which, step):
        head = step * 2 + which if halves == 1 else step
        row = 0 if halves == 1 else which * rows
        return slice(row, row + rows), columns(head)

    def kv_of(step):
        return step // steps_per_kv

    def bias_at(which, at, size):
        row = which * rows * (halves - 1)
        return bias[at - prompt_len : at - prompt_len + size, row : row + rows]

    def folded(x):
        return x.reshape(x.shape[0] // 8, 8, rows)

    def within(at):
        return [slice(start, start + TILE) for start in range(at.start, at.stop, TILE)]

    def weigh(which, step, fast):
        kv = kv_of(step)
        where = place_of(which, step)
        state = {"sum": jnp.zeros((8, rows), F32)}

        def lift():
            q_ts[which] = q_ref[where].T
            cot_ts[which] = do_ref[where].T

        def masked(s, at, tile):
            s = s[tile.start - at.start : tile.stop - at.start]
            return s if tile.start < prompt_len else s + bias_at(which, tile.start, TILE)

        def put(tile, p):
            state["sum"] = state["sum"] + jnp.sum(folded(p), axis=0)
            p_bufs[which, tile] = p.astype(BF16)

        def direct(at):
            s = dot(keys[kv, at], q_ts[which])
            for tile in within(at):
                put(tile, jnp.exp2(masked(s, at, tile) * exp_scale))

        def highest(at):
            s = dot(keys[kv, at], q_ts[which])
            for tile in within(at):
                part = masked(s, at, tile)
                s_buf[tile] = part
                top = jnp.max(folded(part), axis=0)
                state["top"] = jnp.maximum(state["top"], top) if "top" in state else top

        def settle():
            state["top"] = jnp.max(state["top"], axis=0, keepdims=True) * exp_scale

        def reduced(at):
            for tile in within(at):
                put(tile, jnp.exp2(s_buf[tile] * exp_scale - state["top"]))

        def finish():
            inverse = 1.0 / jnp.sum(state["sum"], axis=0, keepdims=True)
            inv_bufs[which] = jnp.broadcast_to(inverse, (8, rows))
            q_ns[which] = (q_ts[which].astype(F32) * inverse).astype(BF16).T
            cot_ns[which] = (cot_ts[which].astype(F32) * inverse).astype(BF16).T

        if fast:
            return [lift] + [functools.partial(direct, at) for at in chunks], finish
        work = [lift] + [functools.partial(highest, at) for at in chunks] + [settle]
        return work + [functools.partial(reduced, at) for at in chunks], finish

    def settled(which, step, state):
        kv = kv_of(step)
        where = place_of(which, step)

        def output(at):
            more = dot(values_t[kv, :, at], p_bufs[which, at])
            state["out"] = state["out"] + more if "out" in state else more

        def put():
            out = (state["out"] * inv_bufs[which, :1]).astype(BF16)
            o_ref[where] = out.T
            wide = cot_ts[which].astype(F32)
            state["delta"] = jnp.sum(wide * out.astype(F32), axis=0, keepdims=True)

        return [functools.partial(output, at) for at in cuts] + [put]

    def slopes(which, step, state):
        kv = kv_of(step)

        def slope(at):
            grads = dot(values[kv, at], cot_ts[which])
            for tile in within(at):
                part = grads[tile.start - at.start : tile.stop - at.start] - state["delta"]
                d_bufs[which, tile] = p_bufs[which, tile] * part.astype(BF16)

        return [functools.partial(slope, at) for at in chunks]

    def value_grads(which, step):
        kv = kv_of(step)

        def value_grad(at):
            dv[kv, at] += dot(p_bufs[which, at], cot_ns[which])

        return [functools.partial(value_grad, at) for at in longer]

    def key_grads(which, step):
        kv = kv_of(step)

        def key_grad(at):
            dk[kv, at] += dot(d_bufs[which, at], q_ns[which])

        return [functools.partial(key_grad, at) for at in longer]

    def query_grads(which, step):
        kv = kv_of(step)
        where = place_of(which, step)
        state = {}

        def query(at):
            more = dot(keys_t[kv, :, at], d_bufs[which, at])
            state["dq"] = state["dq"] + more if "dq" in state else more

        def put():
            dq = state["dq"] * (inv_bufs[which, :1] * score_scale)
            dq_ref[where] = dq.astype(BF16).T

        return [functools.partial(query, at) for at in cuts] + [put]

    def slot(which, step, fast):
        before, before_step = 1 - which, step - 1 + which
        state = {}
        work, finish = weigh(which, step, fast)
        started = not isinstance(step, int)
        late = key_grads(which, step - 1) if started else []
        first = query_grads(which, step - 1) if started else []
        if started or which == 1:
            first = settled(before, before_step, state) + first
        together(work, first + late[: len(late) // 2])
        if started or which == 1:
            together(
                slopes(before, before_step, state),
                late[len(late) // 2 :] + value_grads(before, before_step),
            )
        finish()

    def together(vector, matrix):
        done = 0
        for i, work in enumerate(vector):
            work()
            while done * len(vector) < (i + 1) * len(matrix):
                matrix[done]()
                done += 1

    most = jnp.zeros((HD, 1), F32)
    for n in range(kv_heads):
        k_cols = slice(2 * n * HD, (2 * n + 1) * HD)
        v_cols = slice((2 * n + 1) * HD, (2 * n + 2) * HD)
        for ref, start, size, at, turned_at in (
            (sent_ref, 0, half, 0, 0),
            (got_ref, 0, half, half, None),
            (own_ref, 0, tokens, resp_at[0], half + 2 * tokens),
            (sent_ref, half, tokens, resp_at[1], half),
            (far_ref, 0, tokens, resp_at[2], half + tokens),
            (got_ref, half, tokens, resp_at[3], None),
            (got_ref, half + tokens, tokens, resp_at[4], None),
        ):
            k_rows = ref[start : start + size, k_cols]
            v_rows = ref[start : start + size, v_cols]
            keys[n, at : at + size] = k_rows
            values[n, at : at + size] = v_rows
            if turned_at is None:
                keys_t[n, :, at : at + size] = k_rows.T
                values_t[n, :, at : at + size] = v_rows.T
            else:
                there = slice(turned_at, turned_at + size)
                keys_t[n, :, at : at + size] = turned[2 * n, :, there]
                values_t[n, :, at : at + size] = turned[2 * n + 1, :, there]
        most = largest(got_ref, most, k_cols)
    dk[...] = jnp.zeros_like(dk)
    dv[...] = jnp.zeros_like(dv)
    keys_most = jnp.maximum(jnp.max(most), jnp.max(k_most[...]))
    most = jnp.max(q_most[...]) * keys_most * (score_scale * score_scale)
    small = most <= SAFE_SCORE * SAFE_SCORE
    def run(fast):
        def pair(step, carry):
            slot(0, step, fast)
            slot(1, step, fast)
            return carry

        slot(0, 0, fast)
        slot(1, 0, fast)
        lax.fori_loop(1, steps, pair, 0)

    pl.when(small)(functools.partial(run, True))
    pl.when(jnp.logical_not(small))(functools.partial(run, False))
    state = {}
    for work in settled(1, steps - 1, state) + query_grads(0, steps - 1):
        work()
    together(
        slopes(1, steps - 1, state), key_grads(0, steps - 1) + value_grads(1, steps - 1)
    )
    for work in key_grads(1, steps - 1) + query_grads(1, steps - 1):
        work()
    for n in range(kv_heads):
        k_cols = slice(2 * n * HD, (2 * n + 1) * HD)
        v_cols = slice((2 * n + 1) * HD, (2 * n + 2) * HD)
        for ref, start, size, at in (
            (kept_ref, 0, half, 0),
            (back_ref, 0, half, half),
            (kept_ref, half + 2 * tokens, tokens, resp_at[0]),
            (kept_ref, half, tokens, resp_at[1]),
            (kept_ref, half + tokens, tokens, resp_at[2]),
            (back_ref, half, tokens, resp_at[3]),
            (back_ref, half + tokens, tokens, resp_at[4]),
        ):
            grad_k = dk[n, at : at + size] * score_scale
            ref[start : start + size, k_cols] = grad_k.astype(ref.dtype)
            ref[start : start + size, v_cols] = dv[n, at : at + size].astype(ref.dtype)


def attention(lengths, resp_q, grad_out, sent, got, own, far):
    tokens = resp_q.shape[0]
    half = sent.shape[0] - 2 * tokens
    total_keys = 2 * half + 5 * tokens
    kv_heads = sent.shape[1] // (2 * HD)
    q_heads = resp_q.shape[1] // HD
    halves = 1 if tokens * total_keys <= MOST_SCORES else 2
    rows = tokens // halves
    pairs = tokens * q_heads * total_keys
    most = ((8, HD), F32)
    bias, q_most = local_call(
        mask_kernel, "mask", [lengths, resp_q], [((5 * tokens, tokens), F32), most], scalars=1
    )
    turned, k_most = local_call(
        functools.partial(turn_kernel, kv_heads),
        "turn",
        [sent, own, far],
        [((2 * kv_heads, HD, half + 3 * tokens), BF16), most],
    )
    return pl.pallas_call(
        functools.partial(attention_kernel, halves),
        in_specs=whole(10),
        out_specs=whole(4),
        out_shape=[
            jax.ShapeDtypeStruct(resp_q.shape, BF16),
            jax.ShapeDtypeStruct(resp_q.shape, BF16),
            jax.ShapeDtypeStruct((half + 3 * tokens, sent.shape[1]), F32),
            jax.ShapeDtypeStruct((half + 2 * tokens, sent.shape[1]), BF16),
        ],
        scratch_shapes=[
            pltpu.VMEM((kv_heads, total_keys, HD), BF16),
            pltpu.VMEM((kv_heads, total_keys, HD), BF16),
            pltpu.VMEM((kv_heads, HD, total_keys), BF16),
            pltpu.VMEM((kv_heads, HD, total_keys), BF16),
            pltpu.VMEM((total_keys, rows), F32),
            pltpu.VMEM((2, total_keys, rows), BF16),
            pltpu.VMEM((2, total_keys, rows), BF16),
            pltpu.VMEM((2, 8, rows), F32),
            pltpu.VMEM((2, HD, rows), BF16),
            pltpu.VMEM((2, HD, rows), BF16),
            pltpu.VMEM((2, rows, HD), BF16),
            pltpu.VMEM((2, rows, HD), BF16),
            pltpu.VMEM((kv_heads, total_keys, HD), F32),
            pltpu.VMEM((kv_heads, total_keys, HD), F32),
        ],
        compiler_params=pltpu.CompilerParams(vmem_limit_bytes=(36 if halves == 1 else 48) << 20),
        cost_estimate=pl.CostEstimate(
            flops=12 * HD * pairs, bytes_accessed=8 * resp_q.size, transcendentals=pairs
        ),
        name="attention",
    )(resp_q, grad_out, sent, got, own, far, bias, turned, q_most, k_most)


def swap_heads(array, by):
    devices = lax.axis_size("head")
    return lax.ppermute(array, "head", [(i, i ^ by) for i in range(devices)])


def swap_chips(array, by):
    devices = lax.axis_size("seq")
    return lax.ppermute(array, "seq", [(i, i ^ (by * CORES)) for i in range(devices)])


def swap_cores(array):
    devices = lax.axis_size("seq")
    return lax.ppermute(array, "seq", [(i, i ^ 1) for i in range(devices)])


def shift_chips(array, by):
    devices = lax.axis_size("seq")
    by = by * CORES
    return lax.ppermute(array, "seq", [(i, i + by) for i in range(devices) if 0 <= i + by < devices])


def shards(prompt_k, prompt_v, resp_q, resp_k, resp_v, grad_out, resp_lengths):
    tokens, kv_cols = resp_k.shape
    wide = 2 * kv_cols
    groups = lax.axis_size("head")
    chips = lax.axis_size("seq") // CORES
    block = prompt_k.shape[0]
    core = lax.rem(lax.axis_index("seq"), CORES)

    *pieces, own = pack([prompt_k, prompt_v, resp_k, resp_v], groups)
    pieces = [pieces[0]] + [swap_heads(pieces[k], k) for k in range(1, groups)]
    near = shift_chips(own, 1)
    far = shift_chips(own, 2)
    pieces[1:], near, far = lax.optimization_barrier((pieces[1:], near, far))
    mine = jnp.concatenate(pieces, axis=0)
    parts = [mine] + [swap_chips(mine, k) for k in range(1, chips)]
    chosen = jnp.where(core == 1, far, own)
    sent = jnp.concatenate(parts + [near, chosen], axis=0)
    got = swap_cores(sent)

    resp_out, grad_q, kept, back = attention(
        resp_lengths, resp_q, grad_out, sent, got, own, far
    )

    back = swap_cores(back)
    share = groups * block
    *parts, own = local_call(
        functools.partial(merge_kernel, chips, tokens),
        "merge",
        [kept, back],
        [((share, wide), BF16)] * chips
        + [((tokens // 2, wide), BF16)] * 4
        + [((tokens, wide), F32)],
    )
    near, far, parts = parts[chips : chips + 2], parts[chips + 2 :], parts[:chips]
    parts = [parts[0]] + [swap_chips(parts[k], k) for k in range(1, chips)]
    near = [shift_chips(part, -1) for part in near]
    far = [shift_chips(part, -2) for part in far]
    pieces = local_call(
        functools.partial(sum_kernel, chips),
        "sum_chips",
        parts,
        [((block, wide), BF16)] * groups,
        [pltpu.VMEM((share, wide), F32)],
    )
    pieces = [pieces[0]] + [swap_heads(pieces[k], k) for k in range(1, groups)]
    grad_k_prompt, grad_v_prompt, grad_k_resp, grad_v_resp = local_call(
        finish_kernel,
        "finish",
        [own] + near + far + pieces,
        [(prompt_k.shape, BF16)] * 2 + [((tokens, kv_cols), BF16)] * 2,
    )
    return (resp_out, grad_q, grad_k_resp, grad_v_resp, grad_k_prompt, grad_v_prompt)


def solution(mesh):
    placed = (
        P(("seq", "head"), None),
        P(("seq", "head"), None),
        P("seq", "head"),
        P("seq", "head"),
        P("seq", "head"),
        P("seq", "head"),
        P(),
    )
    return jax.shard_map(
        shards,
        mesh=mesh,
        in_specs=placed,
        out_specs=(
            P("seq", "head"),
            P("seq", "head"),
            P("seq", "head"),
            P("seq", "head"),
            P(("seq", "head"), None),
            P(("seq", "head"), None),
        ),
        check_vma=False,
    )
```

```python
import functools
import math

import jax
import jax.numpy as jnp
from jax import lax
from jax.experimental import pallas as pl
from jax.experimental.pallas import tpu as pltpu
from jax.sharding import PartitionSpec as P

HD = 128
CORES = 2
FAR = 4
CHUNK = 256
LONGER = 640
SAFE_SCORE = 40.0
TILE = 64
MOST_SCORES = 2560 * 256
NEG = -1e30
BF16 = jnp.bfloat16
F32 = jnp.float32


def dot(a, b):
    return jnp.dot(a, b, preferred_element_type=F32)


def whole(count):
    return [pl.BlockSpec(memory_space=pltpu.VMEM)] * count


def local_call(kernel, name, inputs, outputs, scratch=(), scalars=0):
    return pl.pallas_call(
        kernel,
        in_specs=[pl.BlockSpec(memory_space=pltpu.SMEM)] * scalars + whole(len(inputs) - scalars),
        out_specs=whole(len(outputs)),
        out_shape=[jax.ShapeDtypeStruct(shape, kind) for shape, kind in outputs],
        scratch_shapes=list(scratch),
        compiler_params=pltpu.CompilerParams(vmem_limit_bytes=40 * 1024 * 1024),
        name=name,
    )(*inputs)


def pack_kernel(pk_ref, pv_ref, rk_ref, rv_ref, *outs):
    pieces, resp = outs[:-1], outs[-1]
    head = lax.axis_index("head")
    width = pieces[0].shape[1]
    for k, piece in enumerate(pieces):
        start = pl.multiple_of((head ^ k) * (width // 2), HD)
        for n in range(width // (2 * HD)):
            at = pl.multiple_of(start + n * HD, HD)
            piece[:, 2 * n * HD : (2 * n + 1) * HD] = pk_ref[:, pl.ds(at, HD)]
            piece[:, (2 * n + 1) * HD : (2 * n + 2) * HD] = pv_ref[:, pl.ds(at, HD)]
    for n in range(width // (2 * HD)):
        resp[:, 2 * n * HD : (2 * n + 1) * HD] = rk_ref[:, n * HD : (n + 1) * HD]
        resp[:, (2 * n + 1) * HD : (2 * n + 2) * HD] = rv_ref[:, n * HD : (n + 1) * HD]


def pack(inputs, groups):
    def one(array):
        return pl.BlockSpec(array.shape, lambda i: (0, 0))

    block, tokens = inputs[0].shape[0], inputs[2].shape[0]
    wide = 2 * inputs[2].shape[1]
    shapes = [(block, wide)] * groups + [(tokens, wide)]
    return pl.pallas_call(
        pack_kernel,
        grid=(1,),
        in_specs=[one(array) for array in inputs],
        out_specs=whole(groups + 1),
        out_shape=[jax.ShapeDtypeStruct(shape, BF16) for shape in shapes],
        compiler_params=pltpu.CompilerParams(vmem_limit_bytes=56 * 1024 * 1024),
        name="pack",
    )(*inputs)


def merge_kernel(parts, rows, kept_ref, got_ref, *outs):
    pieces, back1, back2, own = outs[:parts], outs[parts:-3], outs[-3:-1], outs[-1]
    core = lax.rem(lax.axis_index("seq"), CORES)
    to_own = jnp.where(core == 0, 1.0, 0.0)
    half = kept_ref.shape[0] - 3 * rows
    share = half // parts
    for k, piece in enumerate(pieces):
        at = slice(k * share, (k + 1) * share)
        piece[...] = (kept_ref[at] + got_ref[at].astype(F32)).astype(BF16)
    one, two, three = half + rows, half + 2 * rows, half + 3 * rows
    near = (kept_ref[half:one] + got_ref[half:one].astype(F32)).astype(BF16)
    chosen = got_ref[one:two].astype(F32)
    far = (kept_ref[one:two] + chosen * (1.0 - to_own)).astype(BF16)
    for i in range(2):
        back1[i][...] = near[i * rows // 2 : (i + 1) * rows // 2]
        back2[i][...] = far[i * rows // 2 : (i + 1) * rows // 2]
    own[...] = kept_ref[two:three] + chosen * to_own


def sum_kernel(parts, *refs):
    ins, outs, total = refs[:parts], refs[parts:-1], refs[-1]
    acc = ins[0][...].astype(F32)
    for ref in ins[1:]:
        acc = acc + ref[...].astype(F32)
    total[...] = acc
    share = total.shape[0] // len(outs)
    for k, out in enumerate(outs):
        out[...] = total[k * share : (k + 1) * share].astype(BF16)


def finish_kernel(own_ref, *refs):
    near, far, pieces, (gk_ref, gv_ref, rk_ref, rv_ref) = refs[:2], refs[2:4], refs[4:-4], refs[-4:]
    head = lax.axis_index("head")
    width = pieces[0].shape[1]
    for k, piece in enumerate(pieces):
        start = pl.multiple_of((head ^ k) * (width // 2), HD)
        for n in range(width // (2 * HD)):
            at = pl.multiple_of(start + n * HD, HD)
            gk_ref[:, pl.ds(at, HD)] = piece[:, 2 * n * HD : (2 * n + 1) * HD]
            gv_ref[:, pl.ds(at, HD)] = piece[:, (2 * n + 1) * HD : (2 * n + 2) * HD]
    rows = near[0].shape[0]
    for i in range(2):
        at = slice(i * rows, (i + 1) * rows)
        total = own_ref[at] + near[i][...].astype(F32) + far[i][...].astype(F32)
        total = total.astype(BF16)
        for n in range(width // (2 * HD)):
            rk_ref[at, n * HD : (n + 1) * HD] = total[:, 2 * n * HD : (2 * n + 1) * HD]
            rv_ref[at, n * HD : (n + 1) * HD] = total[:, (2 * n + 1) * HD : (2 * n + 2) * HD]


def mask_kernel(lengths, q_ref, bias, most_ref):
    tokens, q_cols = q_ref.shape
    place = lax.axis_index("seq")
    core = lax.rem(place, CORES)
    first_row = place * tokens
    row_pos = first_row + lax.broadcasted_iota(jnp.int32, (8, tokens), 1)
    seg_start = jnp.zeros((8, tokens), jnp.int32)
    end = jnp.int32(0)
    for i in range(lengths.shape[0]):
        end = end + lengths[i]
        seg_start = jnp.where(row_pos >= end, end, seg_start)
    seg_start, row_pos = seg_start[:1], row_pos[:1]
    near = 1 + 2 * core
    for i, distance in enumerate((0, 2, FAR, near, 4 - near)):
        for row in range(0, tokens, TILE):
            key_pos = (first_row - distance * tokens + row) + lax.broadcasted_iota(
                jnp.int32, (TILE, tokens), 0
            )
            allowed = (key_pos >= seg_start) & (key_pos <= row_pos)
            at = i * tokens + row
            bias[at : at + TILE] = jnp.where(allowed, 0.0, NEG)
    most = jnp.zeros((tokens, 1), F32)
    for at in range(0, q_cols, HD):
        part = q_ref[:, at : at + HD].astype(F32)
        most = jnp.maximum(most, jnp.sum(part * part, axis=1, keepdims=True))
    most_ref[...] = jnp.broadcast_to(jnp.max(most, axis=0, keepdims=True), most_ref.shape)


def largest(ref, most, cols):
    for at in range(0, ref.shape[0], HD):
        part = ref[at : at + HD, cols].astype(F32)
        most = jnp.maximum(most, jnp.sum(part * part, axis=1, keepdims=True))
    return most


def turn_kernel(kv_heads, sent_ref, own_ref, far_ref, turned, most_ref):
    tokens = own_ref.shape[0]
    most = jnp.zeros((HD, 1), F32)
    for n in range(2 * kv_heads):
        cols = slice(n * HD, (n + 1) * HD)
        at = 0
        for ref, size in ((sent_ref, sent_ref.shape[0] - tokens), (far_ref, tokens), (own_ref, tokens)):
            turned[n, :, at : at + size] = ref[:size, cols].T
            at += size
            if n % 2 == 0:
                most = largest(ref, most, cols)
    most_ref[...] = jnp.broadcast_to(jnp.max(most, axis=0, keepdims=True), most_ref.shape)


def attention_kernel(
    halves, q_ref, do_ref, sent_ref, got_ref, own_ref, far_ref,
    bias, turned, q_most, k_most,
    o_ref, dq_ref, kept_ref, back_ref,
    keys, values, keys_t, values_t, s_buf, p_bufs, d_bufs, inv_bufs,
    q_ts, cot_ts, q_ns, cot_ns, dk, dv,
):
    kv_heads, total_keys = keys.shape[0], keys.shape[1]
    tokens, q_cols = q_ref.shape
    rows = tokens // halves
    prompt_len = total_keys - 5 * tokens
    half = prompt_len // 2
    steps = q_cols // HD * halves // 2
    steps_per_kv = steps // kv_heads
    score_scale = 1.0 / math.sqrt(HD)
    exp_scale = score_scale * math.log2(math.e)
    resp_at = [prompt_len + i * tokens for i in range(6)]
    chunks = [slice(at, at + CHUNK) for at in range(0, total_keys, CHUNK)]
    longer = [slice(at, at + LONGER) for at in range(0, total_keys, LONGER)]
    cuts = [slice(at, at + total_keys // 2) for at in (0, total_keys // 2)]

    def columns(head):
        if isinstance(head, int):
            return slice(head * HD, (head + 1) * HD)
        return pl.ds(pl.multiple_of(head * HD, HD), HD)

    def place_of(which, step):
        head = step * 2 + which if halves == 1 else step
        row = 0 if halves == 1 else which * rows
        return slice(row, row + rows), columns(head)

    def kv_of(step):
        return step // steps_per_kv

    def bias_at(which, at, size):
        row = which * rows * (halves - 1)
        return bias[at - prompt_len : at - prompt_len + size, row : row + rows]

    def folded(x):
        return x.reshape(x.shape[0] // 8, 8, rows)

    def within(at):
        return [slice(start, start + TILE) for start in range(at.start, at.stop, TILE)]

    def weigh(which, step, fast):
        kv = kv_of(step)
        where = place_of(which, step)
        state = {"sum": jnp.zeros((8, rows), F32)}

        def lift():
            q_ts[which] = q_ref[where].T
            cot_ts[which] = do_ref[where].T

        def masked(s, at, tile):
            s = s[tile.start - at.start : tile.stop - at.start]
            return s if tile.start < prompt_len else s + bias_at(which, tile.start, TILE)

        def put(tile, p):
            state["sum"] = state["sum"] + jnp.sum(folded(p), axis=0)
            p_bufs[which, tile] = p.astype(BF16)

        def direct(at):
            s = dot(keys[kv, at], q_ts[which])
            for tile in within(at):
                put(tile, jnp.exp2(masked(s, at, tile) * exp_scale))

        def highest(at):
            s = dot(keys[kv, at], q_ts[which])
            for tile in within(at):
                part = masked(s, at, tile)
                s_buf[tile] = part
                top = jnp.max(folded(part), axis=0)
                state["top"] = jnp.maximum(state["top"], top) if "top" in state else top

        def settle():
            state["top"] = jnp.max(state["top"], axis=0, keepdims=True) * exp_scale

        def reduced(at):
            for tile in within(at):
                put(tile, jnp.exp2(s_buf[tile] * exp_scale - state["top"]))

        def finish():
            inverse = 1.0 / jnp.sum(state["sum"], axis=0, keepdims=True)
            inv_bufs[which] = jnp.broadcast_to(inverse, (8, rows))
            q_ns[which] = (q_ts[which].astype(F32) * inverse).astype(BF16).T
            cot_ns[which] = (cot_ts[which].astype(F32) * inverse).astype(BF16).T

        if fast:
            return [lift] + [functools.partial(direct, at) for at in chunks], finish
        work = [lift] + [functools.partial(highest, at) for at in chunks] + [settle]
        return work + [functools.partial(reduced, at) for at in chunks], finish

    def settled(which, step, state):
        kv = kv_of(step)
        where = place_of(which, step)

        def output(at):
            more = dot(values_t[kv, :, at], p_bufs[which, at])
            state["out"] = state["out"] + more if "out" in state else more

        def put():
            out = (state["out"] * inv_bufs[which, :1]).astype(BF16)
            o_ref[where] = out.T
            wide = cot_ts[which].astype(F32)
            state["delta"] = jnp.sum(wide * out.astype(F32), axis=0, keepdims=True)

        return [functools.partial(output, at) for at in cuts] + [put]

    def slopes(which, step, state):
        kv = kv_of(step)

        def slope(at):
            grads = dot(values[kv, at], cot_ts[which])
            for tile in within(at):
                part = grads[tile.start - at.start : tile.stop - at.start] - state["delta"]
                d_bufs[which, tile] = p_bufs[which, tile] * part.astype(BF16)

        return [functools.partial(slope, at) for at in chunks]

    def value_grads(which, step):
        kv = kv_of(step)

        def value_grad(at):
            dv[kv, at] += dot(p_bufs[which, at], cot_ns[which])

        return [functools.partial(value_grad, at) for at in longer]

    def key_grads(which, step):
        kv = kv_of(step)

        def key_grad(at):
            dk[kv, at] += dot(d_bufs[which, at], q_ns[which])

        return [functools.partial(key_grad, at) for at in longer]

    def query_grads(which, step):
        kv = kv_of(step)
        where = place_of(which, step)
        state = {}

        def query(at):
            more = dot(keys_t[kv, :, at], d_bufs[which, at])
            state["dq"] = state["dq"] + more if "dq" in state else more

        def put():
            dq = state["dq"] * (inv_bufs[which, :1] * score_scale)
            dq_ref[where] = dq.astype(BF16).T

        return [functools.partial(query, at) for at in cuts] + [put]

    def slot(which, step, fast):
        before, before_step = 1 - which, step - 1 + which
        state = {}
        work, finish = weigh(which, step, fast)
        started = not isinstance(step, int)
        first = key_grads(which, step - 1) if started else []
        second = query_grads(which, step - 1) if started else []
        if started or which == 1:
            first = settled(before, before_step, state) + first
            second = second + value_grads(before, before_step)
        together(work, first)
        if started or which == 1:
            together(slopes(before, before_step, state), second)
        finish()

    def together(vector, matrix):
        done = 0
        for i, work in enumerate(vector):
            work()
            while done * len(vector) < (i + 1) * len(matrix):
                matrix[done]()
                done += 1

    most = jnp.zeros((HD, 1), F32)
    for n in range(kv_heads):
        k_cols = slice(2 * n * HD, (2 * n + 1) * HD)
        v_cols = slice((2 * n + 1) * HD, (2 * n + 2) * HD)
        for ref, start, size, at, turned_at in (
            (sent_ref, 0, half, 0, 0),
            (got_ref, 0, half, half, None),
            (own_ref, 0, tokens, resp_at[0], half + 2 * tokens),
            (sent_ref, half, tokens, resp_at[1], half),
            (far_ref, 0, tokens, resp_at[2], half + tokens),
            (got_ref, half, tokens, resp_at[3], None),
            (got_ref, half + tokens, tokens, resp_at[4], None),
        ):
            k_rows = ref[start : start + size, k_cols]
            v_rows = ref[start : start + size, v_cols]
            keys[n, at : at + size] = k_rows
            values[n, at : at + size] = v_rows
            if turned_at is None:
                keys_t[n, :, at : at + size] = k_rows.T
                values_t[n, :, at : at + size] = v_rows.T
            else:
                there = slice(turned_at, turned_at + size)
                keys_t[n, :, at : at + size] = turned[2 * n, :, there]
                values_t[n, :, at : at + size] = turned[2 * n + 1, :, there]
        most = largest(got_ref, most, k_cols)
    dk[...] = jnp.zeros_like(dk)
    dv[...] = jnp.zeros_like(dv)
    keys_most = jnp.maximum(jnp.max(most), jnp.max(k_most[...]))
    most = jnp.max(q_most[...]) * keys_most * (score_scale * score_scale)
    small = most <= SAFE_SCORE * SAFE_SCORE
    def run(fast):
        def pair(step, carry):
            slot(0, step, fast)
            slot(1, step, fast)
            return carry

        slot(0, 0, fast)
        slot(1, 0, fast)
        lax.fori_loop(1, steps, pair, 0)

    pl.when(small)(functools.partial(run, True))
    pl.when(jnp.logical_not(small))(functools.partial(run, False))
    state = {}
    for work in settled(1, steps - 1, state) + key_grads(0, steps - 1):
        work()
    together(
        slopes(1, steps - 1, state), query_grads(0, steps - 1) + value_grads(1, steps - 1)
    )
    for work in key_grads(1, steps - 1) + query_grads(1, steps - 1):
        work()
    for n in range(kv_heads):
        k_cols = slice(2 * n * HD, (2 * n + 1) * HD)
        v_cols = slice((2 * n + 1) * HD, (2 * n + 2) * HD)
        for ref, start, size, at in (
            (kept_ref, 0, half, 0),
            (back_ref, 0, half, half),
            (kept_ref, half + 2 * tokens, tokens, resp_at[0]),
            (kept_ref, half, tokens, resp_at[1]),
            (kept_ref, half + tokens, tokens, resp_at[2]),
            (back_ref, half, tokens, resp_at[3]),
            (back_ref, half + tokens, tokens, resp_at[4]),
        ):
            grad_k = dk[n, at : at + size] * score_scale
            ref[start : start + size, k_cols] = grad_k.astype(ref.dtype)
            ref[start : start + size, v_cols] = dv[n, at : at + size].astype(ref.dtype)


def attention(lengths, resp_q, grad_out, sent, got, own, far):
    tokens = resp_q.shape[0]
    half = sent.shape[0] - 2 * tokens
    total_keys = 2 * half + 5 * tokens
    kv_heads = sent.shape[1] // (2 * HD)
    q_heads = resp_q.shape[1] // HD
    halves = 1 if tokens * total_keys <= MOST_SCORES else 2
    rows = tokens // halves
    pairs = tokens * q_heads * total_keys
    most = ((8, HD), F32)
    bias, q_most = local_call(
        mask_kernel, "mask", [lengths, resp_q], [((5 * tokens, tokens), F32), most], scalars=1
    )
    turned, k_most = local_call(
        functools.partial(turn_kernel, kv_heads),
        "turn",
        [sent, own, far],
        [((2 * kv_heads, HD, half + 3 * tokens), BF16), most],
    )
    return pl.pallas_call(
        functools.partial(attention_kernel, halves),
        in_specs=whole(10),
        out_specs=whole(4),
        out_shape=[
            jax.ShapeDtypeStruct(resp_q.shape, BF16),
            jax.ShapeDtypeStruct(resp_q.shape, BF16),
            jax.ShapeDtypeStruct((half + 3 * tokens, sent.shape[1]), F32),
            jax.ShapeDtypeStruct((half + 2 * tokens, sent.shape[1]), BF16),
        ],
        scratch_shapes=[
            pltpu.VMEM((kv_heads, total_keys, HD), BF16),
            pltpu.VMEM((kv_heads, total_keys, HD), BF16),
            pltpu.VMEM((kv_heads, HD, total_keys), BF16),
            pltpu.VMEM((kv_heads, HD, total_keys), BF16),
            pltpu.VMEM((total_keys, rows), F32),
            pltpu.VMEM((2, total_keys, rows), BF16),
            pltpu.VMEM((2, total_keys, rows), BF16),
            pltpu.VMEM((2, 8, rows), F32),
            pltpu.VMEM((2, HD, rows), BF16),
            pltpu.VMEM((2, HD, rows), BF16),
            pltpu.VMEM((2, rows, HD), BF16),
            pltpu.VMEM((2, rows, HD), BF16),
            pltpu.VMEM((kv_heads, total_keys, HD), F32),
            pltpu.VMEM((kv_heads, total_keys, HD), F32),
        ],
        compiler_params=pltpu.CompilerParams(vmem_limit_bytes=(36 if halves == 1 else 48) << 20),
        cost_estimate=pl.CostEstimate(
            flops=12 * HD * pairs, bytes_accessed=8 * resp_q.size, transcendentals=pairs
        ),
        name="attention",
    )(resp_q, grad_out, sent, got, own, far, bias, turned, q_most, k_most)


def swap_heads(array, by):
    devices = lax.axis_size("head")
    return lax.ppermute(array, "head", [(i, i ^ by) for i in range(devices)])


def swap_chips(array, by):
    devices = lax.axis_size("seq")
    return lax.ppermute(array, "seq", [(i, i ^ (by * CORES)) for i in range(devices)])


def swap_cores(array):
    devices = lax.axis_size("seq")
    return lax.ppermute(array, "seq", [(i, i ^ 1) for i in range(devices)])


def shift_chips(array, by):
    devices = lax.axis_size("seq")
    by = by * CORES
    return lax.ppermute(array, "seq", [(i, i + by) for i in range(devices) if 0 <= i + by < devices])


def shards(prompt_k, prompt_v, resp_q, resp_k, resp_v, grad_out, resp_lengths):
    tokens, kv_cols = resp_k.shape
    wide = 2 * kv_cols
    groups = lax.axis_size("head")
    chips = lax.axis_size("seq") // CORES
    block = prompt_k.shape[0]
    core = lax.rem(lax.axis_index("seq"), CORES)

    *pieces, own = pack([prompt_k, prompt_v, resp_k, resp_v], groups)
    pieces = [pieces[0]] + [swap_heads(pieces[k], k) for k in range(1, groups)]
    near = shift_chips(own, 1)
    far = shift_chips(own, 2)
    pieces[1:], near, far = lax.optimization_barrier((pieces[1:], near, far))
    mine = jnp.concatenate(pieces, axis=0)
    parts = [mine] + [swap_chips(mine, k) for k in range(1, chips)]
    chosen = jnp.where(core == 1, far, own)
    sent = jnp.concatenate(parts + [near, chosen], axis=0)
    got = swap_cores(sent)

    resp_out, grad_q, kept, back = attention(
        resp_lengths, resp_q, grad_out, sent, got, own, far
    )

    back = swap_cores(back)
    share = groups * block
    *parts, own = local_call(
        functools.partial(merge_kernel, chips, tokens),
        "merge",
        [kept, back],
        [((share, wide), BF16)] * chips
        + [((tokens // 2, wide), BF16)] * 4
        + [((tokens, wide), F32)],
    )
    near, far, parts = parts[chips : chips + 2], parts[chips + 2 :], parts[:chips]
    parts = [parts[0]] + [swap_chips(parts[k], k) for k in range(1, chips)]
    near = [shift_chips(part, -1) for part in near]
    far = [shift_chips(part, -2) for part in far]
    pieces = local_call(
        functools.partial(sum_kernel, chips),
        "sum_chips",
        parts,
        [((block, wide), BF16)] * groups,
        [pltpu.VMEM((share, wide), F32)],
    )
    pieces = [pieces[0]] + [swap_heads(pieces[k], k) for k in range(1, groups)]
    grad_k_prompt, grad_v_prompt, grad_k_resp, grad_v_resp = local_call(
        finish_kernel,
        "finish",
        [own] + near + far + pieces,
        [(prompt_k.shape, BF16)] * 2 + [((tokens, kv_cols), BF16)] * 2,
    )
    return (resp_out, grad_q, grad_k_resp, grad_v_resp, grad_k_prompt, grad_v_prompt)


def solution(mesh):
    placed = (
        P(("seq", "head"), None),
        P(("seq", "head"), None),
        P("seq", "head"),
        P("seq", "head"),
        P("seq", "head"),
        P("seq", "head"),
        P(),
    )
    return jax.shard_map(
        shards,
        mesh=mesh,
        in_specs=placed,
        out_specs=(
            P("seq", "head"),
            P("seq", "head"),
            P("seq", "head"),
            P("seq", "head"),
            P(("seq", "head"), None),
            P(("seq", "head"), None),
        ),
        check_vma=False,
    )
```

```python
import functools
import math

import jax
import jax.numpy as jnp
from jax import lax
from jax.experimental import pallas as pl
from jax.experimental.pallas import tpu as pltpu
from jax.sharding import PartitionSpec as P

HD = 128
CORES = 2
FAR = 4
CHUNK = 256
LONGER = 640
SAFE_SCORE = 40.0
TILE = 32
MOST_SCORES = 2560 * 256
NEG = -1e30
BF16 = jnp.bfloat16
F32 = jnp.float32


def dot(a, b):
    return jnp.dot(a, b, preferred_element_type=F32)


def whole(count):
    return [pl.BlockSpec(memory_space=pltpu.VMEM)] * count


def local_call(kernel, name, inputs, outputs, scratch=(), scalars=0):
    return pl.pallas_call(
        kernel,
        in_specs=[pl.BlockSpec(memory_space=pltpu.SMEM)] * scalars + whole(len(inputs) - scalars),
        out_specs=whole(len(outputs)),
        out_shape=[jax.ShapeDtypeStruct(shape, kind) for shape, kind in outputs],
        scratch_shapes=list(scratch),
        compiler_params=pltpu.CompilerParams(vmem_limit_bytes=40 * 1024 * 1024),
        name=name,
    )(*inputs)


def pack_kernel(pk_ref, pv_ref, rk_ref, rv_ref, *outs):
    pieces, resp = outs[:-1], outs[-1]
    head = lax.axis_index("head")
    width = pieces[0].shape[1]
    for k, piece in enumerate(pieces):
        start = pl.multiple_of((head ^ k) * (width // 2), HD)
        for n in range(width // (2 * HD)):
            at = pl.multiple_of(start + n * HD, HD)
            piece[:, 2 * n * HD : (2 * n + 1) * HD] = pk_ref[:, pl.ds(at, HD)]
            piece[:, (2 * n + 1) * HD : (2 * n + 2) * HD] = pv_ref[:, pl.ds(at, HD)]
    for n in range(width // (2 * HD)):
        resp[:, 2 * n * HD : (2 * n + 1) * HD] = rk_ref[:, n * HD : (n + 1) * HD]
        resp[:, (2 * n + 1) * HD : (2 * n + 2) * HD] = rv_ref[:, n * HD : (n + 1) * HD]


def pack(inputs, groups):
    def one(array):
        return pl.BlockSpec(array.shape, lambda i: (0, 0))

    block, tokens = inputs[0].shape[0], inputs[2].shape[0]
    wide = 2 * inputs[2].shape[1]
    shapes = [(block, wide)] * groups + [(tokens, wide)]
    return pl.pallas_call(
        pack_kernel,
        grid=(1,),
        in_specs=[one(array) for array in inputs],
        out_specs=whole(groups + 1),
        out_shape=[jax.ShapeDtypeStruct(shape, BF16) for shape in shapes],
        compiler_params=pltpu.CompilerParams(vmem_limit_bytes=56 * 1024 * 1024),
        name="pack",
    )(*inputs)


def merge_kernel(parts, rows, kept_ref, got_ref, *outs):
    pieces, back1, back2, own = outs[:parts], outs[parts:-3], outs[-3:-1], outs[-1]
    core = lax.rem(lax.axis_index("seq"), CORES)
    to_own = jnp.where(core == 0, 1.0, 0.0)
    half = kept_ref.shape[0] - 3 * rows
    share = half // parts
    for k, piece in enumerate(pieces):
        at = slice(k * share, (k + 1) * share)
        piece[...] = (kept_ref[at] + got_ref[at].astype(F32)).astype(BF16)
    one, two, three = half + rows, half + 2 * rows, half + 3 * rows
    near = (kept_ref[half:one] + got_ref[half:one].astype(F32)).astype(BF16)
    chosen = got_ref[one:two].astype(F32)
    far = (kept_ref[one:two] + chosen * (1.0 - to_own)).astype(BF16)
    for i in range(2):
        back1[i][...] = near[i * rows // 2 : (i + 1) * rows // 2]
        back2[i][...] = far[i * rows // 2 : (i + 1) * rows // 2]
    own[...] = kept_ref[two:three] + chosen * to_own


def sum_kernel(parts, *refs):
    ins, outs, total = refs[:parts], refs[parts:-1], refs[-1]
    acc = ins[0][...].astype(F32)
    for ref in ins[1:]:
        acc = acc + ref[...].astype(F32)
    total[...] = acc
    share = total.shape[0] // len(outs)
    for k, out in enumerate(outs):
        out[...] = total[k * share : (k + 1) * share].astype(BF16)


def finish_kernel(own_ref, *refs):
    near, far, pieces, (gk_ref, gv_ref, rk_ref, rv_ref) = refs[:2], refs[2:4], refs[4:-4], refs[-4:]
    head = lax.axis_index("head")
    width = pieces[0].shape[1]
    for k, piece in enumerate(pieces):
        start = pl.multiple_of((head ^ k) * (width // 2), HD)
        for n in range(width // (2 * HD)):
            at = pl.multiple_of(start + n * HD, HD)
            gk_ref[:, pl.ds(at, HD)] = piece[:, 2 * n * HD : (2 * n + 1) * HD]
            gv_ref[:, pl.ds(at, HD)] = piece[:, (2 * n + 1) * HD : (2 * n + 2) * HD]
    rows = near[0].shape[0]
    for i in range(2):
        at = slice(i * rows, (i + 1) * rows)
        total = own_ref[at] + near[i][...].astype(F32) + far[i][...].astype(F32)
        total = total.astype(BF16)
        for n in range(width // (2 * HD)):
            rk_ref[at, n * HD : (n + 1) * HD] = total[:, 2 * n * HD : (2 * n + 1) * HD]
            rv_ref[at, n * HD : (n + 1) * HD] = total[:, (2 * n + 1) * HD : (2 * n + 2) * HD]


def mask_kernel(lengths, q_ref, bias, most_ref):
    tokens, q_cols = q_ref.shape
    place = lax.axis_index("seq")
    core = lax.rem(place, CORES)
    first_row = place * tokens
    row_pos = first_row + lax.broadcasted_iota(jnp.int32, (8, tokens), 1)
    seg_start = jnp.zeros((8, tokens), jnp.int32)
    end = jnp.int32(0)
    for i in range(lengths.shape[0]):
        end = end + lengths[i]
        seg_start = jnp.where(row_pos >= end, end, seg_start)
    seg_start, row_pos = seg_start[:1], row_pos[:1]
    near = 1 + 2 * core
    for i, distance in enumerate((0, 2, FAR, near, 4 - near)):
        for row in range(0, tokens, TILE):
            key_pos = (first_row - distance * tokens + row) + lax.broadcasted_iota(
                jnp.int32, (TILE, tokens), 0
            )
            allowed = (key_pos >= seg_start) & (key_pos <= row_pos)
            at = i * tokens + row
            bias[at : at + TILE] = jnp.where(allowed, 0.0, NEG)
    most = jnp.zeros((tokens, 1), F32)
    for at in range(0, q_cols, HD):
        part = q_ref[:, at : at + HD].astype(F32)
        most = jnp.maximum(most, jnp.sum(part * part, axis=1, keepdims=True))
    most_ref[...] = jnp.broadcast_to(jnp.max(most, axis=0, keepdims=True), most_ref.shape)


def largest(ref, most, cols):
    for at in range(0, ref.shape[0], HD):
        part = ref[at : at + HD, cols].astype(F32)
        most = jnp.maximum(most, jnp.sum(part * part, axis=1, keepdims=True))
    return most


def turn_kernel(kv_heads, sent_ref, own_ref, far_ref, turned, most_ref):
    tokens = own_ref.shape[0]
    most = jnp.zeros((HD, 1), F32)
    for n in range(2 * kv_heads):
        cols = slice(n * HD, (n + 1) * HD)
        at = 0
        for ref, size in ((sent_ref, sent_ref.shape[0] - tokens), (far_ref, tokens), (own_ref, tokens)):
            turned[n, :, at : at + size] = ref[:size, cols].T
            at += size
            if n % 2 == 0:
                most = largest(ref, most, cols)
    most_ref[...] = jnp.broadcast_to(jnp.max(most, axis=0, keepdims=True), most_ref.shape)


def attention_kernel(
    halves, q_ref, do_ref, sent_ref, got_ref, own_ref, far_ref,
    bias, turned, q_most, k_most,
    o_ref, dq_ref, kept_ref, back_ref,
    keys, values, keys_t, values_t, s_buf, p_bufs, d_bufs, inv_bufs,
    q_ts, cot_ts, q_ns, cot_ns, dk, dv,
):
    kv_heads, total_keys = keys.shape[0], keys.shape[1]
    tokens, q_cols = q_ref.shape
    rows = tokens // halves
    prompt_len = total_keys - 5 * tokens
    half = prompt_len // 2
    steps = q_cols // HD * halves // 2
    steps_per_kv = steps // kv_heads
    score_scale = 1.0 / math.sqrt(HD)
    exp_scale = score_scale * math.log2(math.e)
    resp_at = [prompt_len + i * tokens for i in range(6)]
    chunks = [slice(at, at + CHUNK) for at in range(0, total_keys, CHUNK)]
    longer = [slice(at, at + LONGER) for at in range(0, total_keys, LONGER)]
    cuts = [slice(at, at + total_keys // 2) for at in (0, total_keys // 2)]

    def columns(head):
        if isinstance(head, int):
            return slice(head * HD, (head + 1) * HD)
        return pl.ds(pl.multiple_of(head * HD, HD), HD)

    def place_of(which, step):
        head = step * 2 + which if halves == 1 else step
        row = 0 if halves == 1 else which * rows
        return slice(row, row + rows), columns(head)

    def kv_of(step):
        return step // steps_per_kv

    def bias_at(which, at, size):
        row = which * rows * (halves - 1)
        return bias[at - prompt_len : at - prompt_len + size, row : row + rows]

    def folded(x):
        return x.reshape(x.shape[0] // 8, 8, rows)

    def within(at):
        return [slice(start, start + TILE) for start in range(at.start, at.stop, TILE)]

    def weigh(which, step, fast):
        kv = kv_of(step)
        where = place_of(which, step)
        state = {"sum": jnp.zeros((8, rows), F32)}

        def lift():
            q_ts[which] = q_ref[where].T
            cot_ts[which] = do_ref[where].T

        def masked(s, at, tile):
            s = s[tile.start - at.start : tile.stop - at.start]
            return s if tile.start < prompt_len else s + bias_at(which, tile.start, TILE)

        def put(tile, p):
            state["sum"] = state["sum"] + jnp.sum(folded(p), axis=0)
            p_bufs[which, tile] = p.astype(BF16)

        def direct(at):
            s = dot(keys[kv, at], q_ts[which])
            for tile in within(at):
                put(tile, jnp.exp2(masked(s, at, tile) * exp_scale))

        def highest(at):
            s = dot(keys[kv, at], q_ts[which])
            for tile in within(at):
                part = masked(s, at, tile)
                s_buf[tile] = part
                top = jnp.max(folded(part), axis=0)
                state["top"] = jnp.maximum(state["top"], top) if "top" in state else top

        def settle():
            state["top"] = jnp.max(state["top"], axis=0, keepdims=True) * exp_scale

        def reduced(at):
            for tile in within(at):
                put(tile, jnp.exp2(s_buf[tile] * exp_scale - state["top"]))

        def finish():
            inverse = 1.0 / jnp.sum(state["sum"], axis=0, keepdims=True)
            inv_bufs[which] = jnp.broadcast_to(inverse, (8, rows))
            q_ns[which] = (q_ts[which].astype(F32) * inverse).astype(BF16).T
            cot_ns[which] = (cot_ts[which].astype(F32) * inverse).astype(BF16).T

        if fast:
            return [lift] + [functools.partial(direct, at) for at in chunks], finish
        work = [lift] + [functools.partial(highest, at) for at in chunks] + [settle]
        return work + [functools.partial(reduced, at) for at in chunks], finish

    def settled(which, step, state):
        kv = kv_of(step)
        where = place_of(which, step)

        def output(at):
            more = dot(values_t[kv, :, at], p_bufs[which, at])
            state["out"] = state["out"] + more if "out" in state else more

        def put():
            out = (state["out"] * inv_bufs[which, :1]).astype(BF16)
            o_ref[where] = out.T
            wide = cot_ts[which].astype(F32)
            state["delta"] = jnp.sum(wide * out.astype(F32), axis=0, keepdims=True)

        return [functools.partial(output, at) for at in cuts] + [put]

    def slopes(which, step, state):
        kv = kv_of(step)

        def slope(at):
            grads = dot(values[kv, at], cot_ts[which])
            for tile in within(at):
                part = grads[tile.start - at.start : tile.stop - at.start] - state["delta"]
                d_bufs[which, tile] = p_bufs[which, tile] * part.astype(BF16)

        return [functools.partial(slope, at) for at in chunks]

    def value_grads(which, step):
        kv = kv_of(step)

        def value_grad(at):
            dv[kv, at] += dot(p_bufs[which, at], cot_ns[which])

        return [functools.partial(value_grad, at) for at in longer]

    def key_grads(which, step):
        kv = kv_of(step)

        def key_grad(at):
            dk[kv, at] += dot(d_bufs[which, at], q_ns[which])

        return [functools.partial(key_grad, at) for at in longer]

    def query_grads(which, step):
        kv = kv_of(step)
        where = place_of(which, step)
        state = {}

        def query(at):
            more = dot(keys_t[kv, :, at], d_bufs[which, at])
            state["dq"] = state["dq"] + more if "dq" in state else more

        def put():
            dq = state["dq"] * (inv_bufs[which, :1] * score_scale)
            dq_ref[where] = dq.astype(BF16).T

        return [functools.partial(query, at) for at in cuts] + [put]

    def slot(which, step, fast):
        before, before_step = 1 - which, step - 1 + which
        state = {}
        work, finish = weigh(which, step, fast)
        started = not isinstance(step, int)
        first = key_grads(which, step - 1) if started else []
        second = query_grads(which, step - 1) if started else []
        if started or which == 1:
            first = settled(before, before_step, state) + first
            second = second + value_grads(before, before_step)
        together(work, first)
        if started or which == 1:
            together(slopes(before, before_step, state), second)
        finish()

    def together(vector, matrix):
        done = 0
        for i, work in enumerate(vector):
            work()
            while done * len(vector) < (i + 1) * len(matrix):
                matrix[done]()
                done += 1

    most = jnp.zeros((HD, 1), F32)
    for n in range(kv_heads):
        k_cols = slice(2 * n * HD, (2 * n + 1) * HD)
        v_cols = slice((2 * n + 1) * HD, (2 * n + 2) * HD)
        for ref, start, size, at, turned_at in (
            (sent_ref, 0, half, 0, 0),
            (got_ref, 0, half, half, None),
            (own_ref, 0, tokens, resp_at[0], half + 2 * tokens),
            (sent_ref, half, tokens, resp_at[1], half),
            (far_ref, 0, tokens, resp_at[2], half + tokens),
            (got_ref, half, tokens, resp_at[3], None),
            (got_ref, half + tokens, tokens, resp_at[4], None),
        ):
            k_rows = ref[start : start + size, k_cols]
            v_rows = ref[start : start + size, v_cols]
            keys[n, at : at + size] = k_rows
            values[n, at : at + size] = v_rows
            if turned_at is None:
                keys_t[n, :, at : at + size] = k_rows.T
                values_t[n, :, at : at + size] = v_rows.T
            else:
                there = slice(turned_at, turned_at + size)
                keys_t[n, :, at : at + size] = turned[2 * n, :, there]
                values_t[n, :, at : at + size] = turned[2 * n + 1, :, there]
        most = largest(got_ref, most, k_cols)
    dk[...] = jnp.zeros_like(dk)
    dv[...] = jnp.zeros_like(dv)
    keys_most = jnp.maximum(jnp.max(most), jnp.max(k_most[...]))
    most = jnp.max(q_most[...]) * keys_most * (score_scale * score_scale)
    small = most <= SAFE_SCORE * SAFE_SCORE
    def run(fast):
        def pair(step, carry):
            slot(0, step, fast)
            slot(1, step, fast)
            return carry

        slot(0, 0, fast)
        slot(1, 0, fast)
        lax.fori_loop(1, steps, pair, 0)

    pl.when(small)(functools.partial(run, True))
    pl.when(jnp.logical_not(small))(functools.partial(run, False))
    state = {}
    for work in settled(1, steps - 1, state) + key_grads(0, steps - 1):
        work()
    together(
        slopes(1, steps - 1, state), query_grads(0, steps - 1) + value_grads(1, steps - 1)
    )
    for work in key_grads(1, steps - 1) + query_grads(1, steps - 1):
        work()
    for n in range(kv_heads):
        k_cols = slice(2 * n * HD, (2 * n + 1) * HD)
        v_cols = slice((2 * n + 1) * HD, (2 * n + 2) * HD)
        for ref, start, size, at in (
            (kept_ref, 0, half, 0),
            (back_ref, 0, half, half),
            (kept_ref, half + 2 * tokens, tokens, resp_at[0]),
            (kept_ref, half, tokens, resp_at[1]),
            (kept_ref, half + tokens, tokens, resp_at[2]),
            (back_ref, half, tokens, resp_at[3]),
            (back_ref, half + tokens, tokens, resp_at[4]),
        ):
            grad_k = dk[n, at : at + size] * score_scale
            ref[start : start + size, k_cols] = grad_k.astype(ref.dtype)
            ref[start : start + size, v_cols] = dv[n, at : at + size].astype(ref.dtype)


def attention(lengths, resp_q, grad_out, sent, got, own, far):
    tokens = resp_q.shape[0]
    half = sent.shape[0] - 2 * tokens
    total_keys = 2 * half + 5 * tokens
    kv_heads = sent.shape[1] // (2 * HD)
    q_heads = resp_q.shape[1] // HD
    halves = 1 if tokens * total_keys <= MOST_SCORES else 2
    rows = tokens // halves
    pairs = tokens * q_heads * total_keys
    most = ((8, HD), F32)
    bias, q_most = local_call(
        mask_kernel, "mask", [lengths, resp_q], [((5 * tokens, tokens), F32), most], scalars=1
    )
    turned, k_most = local_call(
        functools.partial(turn_kernel, kv_heads),
        "turn",
        [sent, own, far],
        [((2 * kv_heads, HD, half + 3 * tokens), BF16), most],
    )
    return pl.pallas_call(
        functools.partial(attention_kernel, halves),
        in_specs=whole(10),
        out_specs=whole(4),
        out_shape=[
            jax.ShapeDtypeStruct(resp_q.shape, BF16),
            jax.ShapeDtypeStruct(resp_q.shape, BF16),
            jax.ShapeDtypeStruct((half + 3 * tokens, sent.shape[1]), F32),
            jax.ShapeDtypeStruct((half + 2 * tokens, sent.shape[1]), BF16),
        ],
        scratch_shapes=[
            pltpu.VMEM((kv_heads, total_keys, HD), BF16),
            pltpu.VMEM((kv_heads, total_keys, HD), BF16),
            pltpu.VMEM((kv_heads, HD, total_keys), BF16),
            pltpu.VMEM((kv_heads, HD, total_keys), BF16),
            pltpu.VMEM((total_keys, rows), F32),
            pltpu.VMEM((2, total_keys, rows), BF16),
            pltpu.VMEM((2, total_keys, rows), BF16),
            pltpu.VMEM((2, 8, rows), F32),
            pltpu.VMEM((2, HD, rows), BF16),
            pltpu.VMEM((2, HD, rows), BF16),
            pltpu.VMEM((2, rows, HD), BF16),
            pltpu.VMEM((2, rows, HD), BF16),
            pltpu.VMEM((kv_heads, total_keys, HD), F32),
            pltpu.VMEM((kv_heads, total_keys, HD), F32),
        ],
        compiler_params=pltpu.CompilerParams(vmem_limit_bytes=(36 if halves == 1 else 48) << 20),
        cost_estimate=pl.CostEstimate(
            flops=12 * HD * pairs, bytes_accessed=8 * resp_q.size, transcendentals=pairs
        ),
        name="attention",
    )(resp_q, grad_out, sent, got, own, far, bias, turned, q_most, k_most)


def swap_heads(array, by):
    devices = lax.axis_size("head")
    return lax.ppermute(array, "head", [(i, i ^ by) for i in range(devices)])


def swap_chips(array, by):
    devices = lax.axis_size("seq")
    return lax.ppermute(array, "seq", [(i, i ^ (by * CORES)) for i in range(devices)])


def swap_cores(array):
    devices = lax.axis_size("seq")
    return lax.ppermute(array, "seq", [(i, i ^ 1) for i in range(devices)])


def shift_chips(array, by):
    devices = lax.axis_size("seq")
    by = by * CORES
    return lax.ppermute(array, "seq", [(i, i + by) for i in range(devices) if 0 <= i + by < devices])


def shards(prompt_k, prompt_v, resp_q, resp_k, resp_v, grad_out, resp_lengths):
    tokens, kv_cols = resp_k.shape
    wide = 2 * kv_cols
    groups = lax.axis_size("head")
    chips = lax.axis_size("seq") // CORES
    block = prompt_k.shape[0]
    core = lax.rem(lax.axis_index("seq"), CORES)

    *pieces, own = pack([prompt_k, prompt_v, resp_k, resp_v], groups)
    pieces = [pieces[0]] + [swap_heads(pieces[k], k) for k in range(1, groups)]
    near = shift_chips(own, 1)
    far = shift_chips(own, 2)
    pieces[1:], near, far = lax.optimization_barrier((pieces[1:], near, far))
    mine = jnp.concatenate(pieces, axis=0)
    parts = [mine] + [swap_chips(mine, k) for k in range(1, chips)]
    chosen = jnp.where(core == 1, far, own)
    sent = jnp.concatenate(parts + [near, chosen], axis=0)
    got = swap_cores(sent)

    resp_out, grad_q, kept, back = attention(
        resp_lengths, resp_q, grad_out, sent, got, own, far
    )

    back = swap_cores(back)
    share = groups * block
    *parts, own = local_call(
        functools.partial(merge_kernel, chips, tokens),
        "merge",
        [kept, back],
        [((share, wide), BF16)] * chips
        + [((tokens // 2, wide), BF16)] * 4
        + [((tokens, wide), F32)],
    )
    near, far, parts = parts[chips : chips + 2], parts[chips + 2 :], parts[:chips]
    parts = [parts[0]] + [swap_chips(parts[k], k) for k in range(1, chips)]
    near = [shift_chips(part, -1) for part in near]
    far = [shift_chips(part, -2) for part in far]
    pieces = local_call(
        functools.partial(sum_kernel, chips),
        "sum_chips",
        parts,
        [((block, wide), BF16)] * groups,
        [pltpu.VMEM((share, wide), F32)],
    )
    pieces = [pieces[0]] + [swap_heads(pieces[k], k) for k in range(1, groups)]
    grad_k_prompt, grad_v_prompt, grad_k_resp, grad_v_resp = local_call(
        finish_kernel,
        "finish",
        [own] + near + far + pieces,
        [(prompt_k.shape, BF16)] * 2 + [((tokens, kv_cols), BF16)] * 2,
    )
    return (resp_out, grad_q, grad_k_resp, grad_v_resp, grad_k_prompt, grad_v_prompt)


def solution(mesh):
    placed = (
        P(("seq", "head"), None),
        P(("seq", "head"), None),
        P("seq", "head"),
        P("seq", "head"),
        P("seq", "head"),
        P("seq", "head"),
        P(),
    )
    return jax.shard_map(
        shards,
        mesh=mesh,
        in_specs=placed,
        out_specs=(
            P("seq", "head"),
            P("seq", "head"),
            P("seq", "head"),
            P("seq", "head"),
            P(("seq", "head"), None),
            P(("seq", "head"), None),
        ),
        check_vma=False,
    )
```
